32 devices in a mesh: fsdp: 2 (over x), ctx: 4 (over z), tp: 4 (over y, core).
Axes of the slice: x: 2, y: 2, z: 4, core: 2. Of those that a mesh axis runs over, the one named last changes fastest.
Arguments:
- activations: bfloat16 [2048, 2560], P(('fsdp', 'ctx'), 'tp'), may hold values from -6 to 6
- attn_gain: bfloat16 [2560], P('tp'), may hold values from 0.099609375 to 1.8984375
- query_down: bfloat16 [2560, 768], P('tp', ('fsdp', 'ctx')), may hold values from -0.125 to 0.125
- latent_down: bfloat16 [2560, 288], P('tp', ('fsdp', 'ctx')), may hold values from -0.125 to 0.125
- query_gain: bfloat16 [768], P(('fsdp', 'ctx')), may hold values from 0.099609375 to 1.8984375
- latent_gain: bfloat16 [256], P(('fsdp', 'ctx')), may hold values from 0.099609375 to 1.8984375
- query_up: bfloat16 [768, 3840], P(('fsdp', 'ctx'), 'tp'), may hold values from -0.21875 to 0.21875
- latent_up: bfloat16 [256, 5120], P(('fsdp', 'ctx'), 'tp'), may hold values from -0.375 to 0.375
- attn_output: bfloat16 [2560, 2560], P('tp', ('fsdp', 'ctx')), may hold values from -12 to 12
- ffn_gain: bfloat16 [2560], P('tp'), may hold values from 0.099609375 to 1.8984375
- ffn_gate: bfloat16 [2560, 6400], P(('fsdp', 'ctx'), 'tp'), may hold values from -0.125 to 0.125
- ffn_up: bfloat16 [2560, 6400], P(('fsdp', 'ctx'), 'tp'), may hold values from -0.125 to 0.125
- ffn_down: bfloat16 [6400, 2560], P('tp', ('fsdp', 'ctx')), may hold values from -0.8984375 to 0.8984375
- out_grad: bfloat16 [2048, 2560], P(('fsdp', 'ctx'), 'tp'), may hold values from -6 to 6
Outputs:
- result: bfloat16 [2048, 2560], P(('fsdp', 'ctx'), 'tp')
- input_grad: float32 [2048, 2560], P(('fsdp', 'ctx'), 'tp')
- attn_gain_grad: float32 [2560], P('tp')
- query_down_grad: float32 [2560, 768], P('tp', ('fsdp', 'ctx'))
- latent_down_grad: float32 [2560, 288], P('tp', ('fsdp', 'ctx'))
- query_gain_grad: float32 [768], P(('fsdp', 'ctx'))
- latent_gain_grad: float32 [256], P(('fsdp', 'ctx'))
- query_up_grad: float32 [768, 3840], P(('fsdp', 'ctx'), 'tp')
- latent_up_grad: float32 [256, 5120], P(('fsdp', 'ctx'), 'tp')
- attn_output_grad: float32 [2560, 2560], P('tp', ('fsdp', 'ctx'))
- ffn_gain_grad: float32 [2560], P('tp')
- ffn_gate_grad: float32 [2560, 6400], P(('fsdp', 'ctx'), 'tp')
- ffn_up_grad: float32 [2560, 6400], P(('fsdp', 'ctx'), 'tp')
- ffn_down_grad: float32 [6400, 2560], P('tp', ('fsdp', 'ctx'))
The draws below stay inside these ranges and needn't reach their ends.
All inputs are finite; a program needn't handle non-finite values.
Results may differ from the reference program's by a relative error of at most 0.02.
Values may be sent and summed in bfloat16 or wider, within the bound.
No kernel may reach another device: no remote copies, remote signals or barrier semaphores. Data moves between devices by JAX's collectives and lax.ppermute only.
A program may use at most 192 MiB of HBM per device.

```python
import math
import jax
import jax.numpy as jnp
from jax import lax

D = 2560
HEADS = 40
NOPE = 64
ROPE = 32
VDIM = 64
QRANK = 768
KVRANK = 256
FF = 6400
TOK_DEV = 256
TOKENS = 2048
N_FSDP = 2
N_CTX = 4


def block_scale(stream_key, shape, split, smallest, top_value):
    loudness = 1.0
    for position, blocks in split:
        heights = jax.random.uniform(jax.random.fold_in(jax.random.fold_in(stream_key, 6), position), (blocks,), jnp.float32, smallest / len(split), top_value / len(split))
        loudness = loudness * jnp.repeat(jnp.exp(heights), shape[position] // blocks).reshape((-1,) + (1,) * (len(shape) - 1 - position))
    return loudness


def bell_draw(rng, dims, width, limit, split=(), held_as=jnp.bfloat16):
    factor_of = block_scale(rng, dims, split, -0.22, 0.18) if split else 1.0
    entries = jax.random.normal(rng, dims, jnp.float32) * width * factor_of
    return jnp.minimum(jnp.maximum(entries, -limit), limit).astype(held_as)


def setup_inputs(seed: int = 0) -> dict:
    arg_keys = jax.random.split(jax.random.key(seed), 15)
    return {
        "activations": bell_draw(arg_keys[0], (TOKENS, D), 1.0, 6.0, ((0, 8), (1, 4))),
        "attn_gain": jnp.clip(1.0 + 0.18 * jax.random.normal(arg_keys[1], (D,), jnp.float32), 0.099609375, 1.8984375).astype(jnp.bfloat16),
        "query_down": bell_draw(arg_keys[2], (D, QRANK), D ** -0.5, 0.125, ((0, 4), (1, 8))),
        "latent_down": bell_draw(arg_keys[3], (D, KVRANK + ROPE), D ** -0.5, 0.125, ((0, 4), (1, 8))),
        "query_gain": jnp.clip(1.0 + 0.18 * jax.random.normal(arg_keys[4], (QRANK,), jnp.float32), 0.099609375, 1.8984375).astype(jnp.bfloat16),
        "latent_gain": jnp.clip(1.0 + 0.18 * jax.random.normal(arg_keys[5], (KVRANK,), jnp.float32), 0.099609375, 1.8984375).astype(jnp.bfloat16),
        "query_up": bell_draw(arg_keys[6], (QRANK, HEADS * (NOPE + ROPE)), QRANK ** -0.5, 0.21875, ((0, 8), (1, 4))),
        "latent_up": bell_draw(arg_keys[7], (KVRANK, HEADS * (NOPE + VDIM)), KVRANK ** -0.5, 0.375, ((0, 8), (1, 4))),
        "attn_output": bell_draw(arg_keys[8], (HEADS * VDIM, D), 2.0, 12.0, ((0, 4), (1, 8))),
        "ffn_gain": jnp.clip(1.0 + 0.18 * jax.random.normal(arg_keys[9], (D,), jnp.float32), 0.099609375, 1.8984375).astype(jnp.bfloat16),
        "ffn_gate": bell_draw(arg_keys[10], (D, FF), D ** -0.5, 0.125, ((0, 8), (1, 4))),
        "ffn_up": bell_draw(arg_keys[11], (D, FF), D ** -0.5, 0.125, ((0, 8), (1, 4))),
        "ffn_down": bell_draw(arg_keys[12], (FF, D), 0.15, 0.8984375, ((0, 4), (1, 8))),
        "out_grad": bell_draw(arg_keys[13], (TOKENS, D), 1.0, 6.0, ((0, 8), (1, 4))),
    }


RESID = 1.4 / math.sqrt(62.0)
EPSILON = 1e-05
NEGATIVE = -1e+30
HIGHEST = lax.Precision.HIGHEST

@jax.custom_vjp
def low(v):
    return lax.optimization_barrier(v.astype(jnp.bfloat16)).astype(jnp.float32)

@jax.custom_vjp
def low_back(v):
    return v

def low_keep(v):
    return (low(v), None)

def low_pass(kept, grad):
    return (grad,)

def back_keep(v):
    return (v, None)

def back_low(kept, grad):
    return (low(grad),)
low.defvjp(low_keep, low_pass)
low_back.defvjp(back_keep, back_low)

def matmul(left, right):
    return jnp.dot(left, right, precision=HIGHEST)

def rms_scaled(values):
    return values * lax.rsqrt(lax.optimization_barrier(jnp.mean(values * values, axis=-1, keepdims=True)) + EPSILON)

def turned(values):
    middle = values.shape[-1] // 2
    return jnp.concatenate([-values[..., middle:], values[..., :middle]], axis=-1)

def rotate(values, cos_table, sin_table):
    return values * cos_table + turned(values) * sin_table

def rotary_tables(positions):
    exponent = jnp.arange(0, ROPE, 2, dtype=jnp.float32) / ROPE
    inverse = 1.0 / 10000.0 ** exponent
    angles = positions[:, None] * inverse[None, :]
    angles = jnp.concatenate([angles, angles], axis=1)
    return (jnp.cos(angles), jnp.sin(angles))

def softmax_rows(scores):
    shifted = scores - lax.optimization_barrier(jnp.max(scores, axis=-1, keepdims=True))
    exponentials = jnp.exp(shifted)
    return exponentials / lax.optimization_barrier(jnp.sum(exponentials, axis=-1, keepdims=True))

def reference(activations, attn_gain, query_down, latent_down, query_gain, latent_gain, query_up, latent_up, attn_output, ffn_gain, ffn_gate, ffn_up, ffn_down, out_grad):
    seq_len = TOK_DEV * N_CTX
    score_scale = 1.0 / math.sqrt(NOPE + ROPE)
    params = tuple((member.astype(jnp.float32) for member in (attn_gain, query_down, latent_down, query_gain, latent_gain, query_up, latent_up, attn_output, ffn_gain, ffn_gate, ffn_up, ffn_down)))
    cos_table, sin_table = rotary_tables(jnp.arange(seq_len, dtype=jnp.float32))
    places = jnp.arange(seq_len, dtype=jnp.int32)
    allowed = places[None, :] <= places[:, None]

    def layer(weights, inputs):
        g_one, w_qdown, w_kvdown, g_query, g_latent, w_qup, w_kvup, w_out, g_two, w_gate, w_up, w_down = weights
        length = inputs.shape[0]
        normed = low(rms_scaled(inputs) * g_one)
        latent = low_back(matmul(normed, jnp.concatenate([w_qdown, w_kvdown], axis=1)))
        query_latent = latent[:, :QRANK]
        kv_latent = latent[:, QRANK:QRANK + KVRANK]
        rope_latent = latent[:, QRANK + KVRANK:]
        query_normed = low(rms_scaled(query_latent) * g_query)
        kv_normed = low(rms_scaled(kv_latent) * g_latent)
        queries = low_back(matmul(query_normed, w_qup)).reshape(length, HEADS, NOPE + ROPE)
        pairs = low_back(matmul(kv_normed, w_kvup)).reshape(length, HEADS, NOPE + VDIM)
        queries = low(jnp.concatenate([queries[..., :NOPE], rotate(queries[..., NOPE:], cos_table[:, None, :], sin_table[:, None, :])], axis=-1))
        rope_keys = low(rotate(rope_latent, cos_table, sin_table))
        pairs = low(pairs)

        def one_head(pieces):
            query_head, pair_head = pieces
            keys_head = jnp.concatenate([pair_head[:, :NOPE], rope_keys], axis=1)
            scores = low_back(matmul(query_head, keys_head.T) * score_scale)
            scores = jnp.where(allowed, scores, NEGATIVE)
            return matmul(low(softmax_rows(scores)), pair_head[:, NOPE:])
        outputs = lax.map(jax.checkpoint(one_head), (queries.transpose(1, 0, 2), pairs.transpose(1, 0, 2)))
        attended = low(low_back(outputs.transpose(1, 0, 2).reshape(length, HEADS * VDIM)))
        middle = inputs + RESID * low_back(matmul(attended, w_out))
        normed_two = low(rms_scaled(middle) * g_two)
        gate = low_back(matmul(normed_two, w_gate))
        upper = low_back(matmul(normed_two, w_up))
        hidden = low(gate * jax.nn.sigmoid(gate) * upper)
        return middle + RESID * low_back(matmul(hidden, w_down))

    def one_sequence(totals, pair):
        inputs, cotangent = pair
        outputs, pullback = jax.vjp(layer, params, inputs)
        weight_grads, input_grads = pullback(cotangent)
        return (jax.tree.map(jnp.add, totals, weight_grads), (outputs, input_grads))
    starts = jax.tree.map(jnp.zeros_like, params)
    inputs_all = activations.astype(jnp.float32).reshape(N_FSDP, seq_len, D)
    cotangents = out_grad.astype(jnp.float32).reshape(N_FSDP, seq_len, D)
    totals, (outputs, input_grads) = lax.scan(one_sequence, starts, (inputs_all, cotangents))
    return (outputs.reshape(TOKENS, D).astype(jnp.bfloat16), input_grads.reshape(TOKENS, D), totals[0], totals[1], totals[2], totals[3], totals[4], totals[5], totals[6], totals[7], totals[8], totals[9], totals[10], totals[11])
```

```python
import functools
import math

import jax
import jax.numpy as jnp
from jax import lax
from jax.experimental import pallas as pl
from jax.experimental.pallas import tpu as pltpu
from jax.sharding import PartitionSpec as P

NOPE = 64
ROPE = 32
VDIM = 64
QRANK = 768
KVRANK = 256
LANES = 128

RESID = 1.4 / math.sqrt(62.0)
EPSILON = 1e-05
NEGATIVE = -1e30
SCORE = 1.0 / math.sqrt(NOPE + ROPE)

F32 = jnp.float32
BF16 = jnp.bfloat16


def product(left, right):
    return jnp.dot(left, right, preferred_element_type=F32)


def times_transposed(left, right):
    return lax.dot_general(left, right, (((1,), (1,)), ((), ())), preferred_element_type=F32)


def transposed_times(left, right):
    return lax.dot_general(left, right, (((0,), (0,)), ((), ())), preferred_element_type=F32)


def turned(values):
    middle = values.shape[-1] // 2
    return jnp.concatenate([-values[..., middle:], values[..., :middle]], axis=-1)


def turned_back(values):
    middle = values.shape[-1] // 2
    return jnp.concatenate([values[..., middle:], -values[..., :middle]], axis=-1)


def rotate(values, cos_table, sin_table):
    return values * cos_table + turned(values) * sin_table


def rotate_back(grads, cos_table, sin_table):
    return grads * cos_table + turned_back(grads * sin_table)


def rotary_tables(positions):
    exponent = jnp.arange(0, ROPE, 2, dtype=F32) / ROPE
    inverse = 1.0 / 10000.0**exponent
    angles = positions[:, None] * inverse[None, :]
    angles = jnp.concatenate([angles, angles], axis=1)
    return (jnp.cos(angles), jnp.sin(angles))


def swap(value, axis, distance):
    size = lax.axis_size(axis)
    return lax.ppermute(value, axis, [(i, i ^ distance) for i in range(size)])


def from_next(value, axis, step):
    size = lax.axis_size(axis)
    return lax.ppermute(value, axis, [(i, (i - step) % size) for i in range(size)])


def aligned(pieces, index):
    size = len(pieces)
    if size == 1:
        return pieces[0][None]
    doubled = jnp.stack(pieces + pieces[:-1])
    return lax.dynamic_slice_in_dim(doubled, (size - index) % size, size, 0)


def gather_ctx(value):
    size = lax.axis_size("ctx")
    pieces = [value] + [from_next(value, "ctx", step) for step in range(1, size)]
    return aligned(pieces, lax.axis_index("ctx"))


def gather_fsdp(value):
    size = lax.axis_size("fsdp")
    if size == 2:
        return aligned([value, swap(value, "fsdp", 1)], lax.axis_index("fsdp"))
    return lax.all_gather(value, "fsdp", axis=0, tiled=False)


def gather_shards(value):
    both = gather_fsdp(gather_ctx(value))
    return both.reshape((both.shape[0] * both.shape[1],) + value.shape)


def chunks_to_ctx(chunks):
    size = lax.axis_size("ctx")
    index = lax.axis_index("ctx")
    pieces = []
    for step in range(size):
        mine = lax.dynamic_index_in_dim(chunks, (index - step) % size, 0, keepdims=False)
        pieces.append(mine if step == 0 else from_next(mine, "ctx", step))
    return aligned(pieces, index)


def chunk_sum_ctx(chunks):
    size = lax.axis_size("ctx")
    index = lax.axis_index("ctx")
    total = lax.dynamic_index_in_dim(chunks, index, 0, keepdims=False).astype(F32)
    for step in range(1, size):
        mine = lax.dynamic_index_in_dim(chunks, (index - step) % size, 0, keepdims=False)
        total = total + from_next(mine, "ctx", step).astype(F32)
    return total


def fold_fsdp(blocks):
    size = lax.axis_size("fsdp")
    if size == 2:
        index = lax.axis_index("fsdp")
        mine = lax.dynamic_index_in_dim(blocks, index, 0, keepdims=False)
        theirs = lax.dynamic_index_in_dim(blocks, 1 - index, 0, keepdims=False)
        return mine.astype(F32) + swap(theirs.astype(BF16), "fsdp", 1).astype(F32)
    return lax.psum_scatter(blocks.astype(BF16), "fsdp", scatter_dimension=0, tiled=False).astype(F32)


def shard_sum(stack):
    parts = stack.reshape((lax.axis_size("fsdp"), lax.axis_size("ctx")) + stack.shape[1:])
    return chunk_sum_ctx(fold_fsdp(parts).astype(BF16))


def shard_exchange(stack):
    parts = stack.reshape((lax.axis_size("fsdp"), lax.axis_size("ctx")) + stack.shape[1:])
    return chunks_to_ctx(fold_fsdp(parts).astype(BF16))


def tp_spread(value):
    far = swap(value, "tp", 2)
    near = swap(jnp.stack([value, far]), "tp", 1)
    return [value, near[0], far, near[1]]


def tp_total(value):
    half = value.shape[0] // 2
    core = lax.axis_index("tp") % 2
    halves = value.reshape(2, half, value.shape[1])
    mine = lax.dynamic_index_in_dim(halves, core, 0, keepdims=False)
    theirs = lax.dynamic_index_in_dim(halves, 1 - core, 0, keepdims=False)
    pair = (mine + swap(theirs, "tp", 1)).astype(BF16)
    total = pair.astype(F32) + swap(pair, "tp", 2).astype(F32)
    return aligned([total, swap(total, "tp", 1)], core).reshape(value.shape)


def spread_rows(block):
    return jnp.concatenate(tp_spread(block), axis=1)


def fold_tp(parts):
    sent = jnp.stack([parts[1].astype(BF16), parts[3].astype(BF16)])
    got = swap(sent, "tp", 1)
    near = parts[0].astype(F32) + got[0].astype(F32)
    far = parts[2].astype(F32) + got[1].astype(F32)
    return near + swap(far.astype(BF16), "tp", 2).astype(F32)


def relative_blocks(stack, index):
    return jnp.stack(
        [lax.dynamic_index_in_dim(stack, index ^ place, 0, keepdims=False) for place in range(4)]
    )


def turn_lanes(values, cos_table, lower_table, upper_table, sign):
    return (
        values * cos_table
        + sign * (pltpu.roll(values, LANES - ROPE // 2, 1) * lower_table)
        + sign * (pltpu.roll(values, ROPE // 2, 1) * upper_table)
    )


def masked_blocks(scores, place, rows, blocks, fill):
    key_row = lax.broadcasted_iota(jnp.int32, (rows, rows), 0)
    query_column = lax.broadcasted_iota(jnp.int32, (rows, rows), 1)
    out = [jnp.where(key_row <= query_column, scores[:rows], fill)]
    for block in range(1, blocks):
        seen = place + block >= blocks
        out.append(jnp.where(seen, scores[block * rows : (block + 1) * rows], fill))
    return out


def forward_kernel(
    blocks, place_ref, low_q, wq, low_kv, wkv, rope_key, cos_t, lower_t, upper_t, out, q_out, kv_out, lse_out
):
    place = place_ref[0]
    rows = low_q.shape[0]
    key_lane = lax.broadcasted_iota(jnp.int32, (low_kv.shape[0], LANES), 1)
    outs = []
    for head in range(2):
        lanes = slice(head * LANES, (head + 1) * LANES)
        raw = product(low_q[...], wq[:, lanes])
        query = turn_lanes(raw, cos_t[...], lower_t[...], upper_t[...], 1.0).astype(BF16)
        pair = product(low_kv[...], wkv[:, lanes]).astype(BF16)
        key = jnp.where(key_lane < NOPE, pair, rope_key[...])
        q_out[:, lanes] = query
        kv_out[:, lanes] = pair
        scores = times_transposed(key, query) * SCORE
        masked = masked_blocks(scores, place, rows, blocks, NEGATIVE)
        top = functools.reduce(
            jnp.maximum, [jnp.max(part, axis=0, keepdims=True) for part in masked]
        )
        powers = [jnp.exp(part - top) for part in masked]
        total = sum(jnp.sum(part, axis=0, keepdims=True) for part in powers)
        prob = jnp.concatenate([part.astype(BF16) for part in powers], axis=0)
        mixed = transposed_times(pair, prob) / total
        outs.append(jnp.transpose(mixed))
        lse_out[0, head : head + 1, :] = top + jnp.log(total)
    lane = lax.broadcasted_iota(jnp.int32, (rows, LANES), 1)
    out[...] = jnp.where(lane < VDIM, pltpu.roll(outs[0], VDIM, 1), outs[1]).astype(BF16)


def backward_kernel(
    blocks, place_ref, q_in, kv_in, rope_key, lse_in, dout, cos_t, lower_t, upper_t, dq_out, dkv_out, dkr_out
):
    place = place_ref[0]
    rows = q_in.shape[0]
    key_lane = lax.broadcasted_iota(jnp.int32, (kv_in.shape[0], LANES), 1)
    lane = lax.broadcasted_iota(jnp.int32, (rows, LANES), 1)

    @pl.when(pl.program_id(0) == 0)
    def _():
        dkr_out[...] = jnp.zeros_like(dkr_out)

    both = dout[...].astype(F32)
    dkr = jnp.zeros(dkr_out.shape, F32)
    for head in range(2):
        lanes = slice(head * LANES, (head + 1) * LANES)
        query = q_in[:, lanes]
        pair = kv_in[:, lanes]
        key = jnp.where(key_lane < NOPE, pair, rope_key[...])
        upper = pltpu.roll(both, VDIM, 1) if head == 0 else both
        out_grad = jnp.where(lane >= NOPE, upper, 0.0).astype(BF16)
        scores = times_transposed(key, query) * SCORE
        lse = lse_in[0, head : head + 1, :]
        masked = masked_blocks(scores, place, rows, blocks, NEGATIVE)
        prob = jnp.concatenate([jnp.exp(part - lse) for part in masked], axis=0)
        prob_grad = times_transposed(pair, out_grad)
        weighted = prob * prob_grad
        delta = jnp.sum(weighted, axis=0, keepdims=True)
        score_grad = (weighted - prob * delta).astype(BF16)
        key_grad = product(score_grad, query) * SCORE
        value_grad = product(prob.astype(BF16), out_grad)
        dkv_out[:, lanes] = jnp.where(key_lane < NOPE, key_grad, value_grad).astype(BF16)
        dkr = dkr + key_grad
        query_grad = jnp.transpose(transposed_times(key, score_grad)) * SCORE
        dq_out[:, lanes] = turn_lanes(
            query_grad, cos_t[...], lower_t[...], upper_t[...], -1.0
        ).astype(BF16)
    dkr_out[...] += dkr


def kernel_params():
    return pltpu.CompilerParams(vmem_limit_bytes=48 << 20, dimension_semantics=("arbitrary",))


def attention_forward(place, low_q, wq, low_kv, wkv, rope_key, tables, blocks):
    rows = low_q.shape[0]
    keys = low_kv.shape[0]
    pairs = wq.shape[1] // (2 * LANES)
    whole = lambda shape: pl.BlockSpec(shape, lambda i: (0, 0))
    column = lambda shape: pl.BlockSpec(shape, lambda i: (0, i))
    scalar = pl.BlockSpec(memory_space=pltpu.SMEM)
    heads = 2 * pairs
    return pl.pallas_call(
        functools.partial(forward_kernel, blocks),
        grid=(pairs,),
        in_specs=[
            scalar,
            whole(low_q.shape),
            column((wq.shape[0], 2 * LANES)),
            whole(low_kv.shape),
            column((wkv.shape[0], 2 * LANES)),
            whole(rope_key.shape),
        ]
        + [whole(table.shape) for table in tables],
        out_specs=[
            column((rows, LANES)),
            column((rows, 2 * LANES)),
            column((keys, 2 * LANES)),
            pl.BlockSpec((1, 8, rows), lambda i: (i, 0, 0)),
        ],
        out_shape=[
            jax.ShapeDtypeStruct((rows, pairs * LANES), BF16),
            jax.ShapeDtypeStruct((rows, heads * LANES), BF16),
            jax.ShapeDtypeStruct((keys, heads * LANES), BF16),
            jax.ShapeDtypeStruct((pairs, 8, rows), F32),
        ],
        compiler_params=kernel_params(),
        cost_estimate=pl.CostEstimate(
            flops=2 * heads * rows * (QRANK + 2 * keys) * LANES + 2 * heads * keys * KVRANK * LANES,
            bytes_accessed=8 << 20,
            transcendentals=heads * rows * keys,
        ),
        name="attention_forward",
    )(place, low_q, wq, low_kv, wkv, rope_key, *tables)


def attention_backward(place, queries, pairs_low, rope_key, lse, dout, tables, blocks):
    rows = queries.shape[0]
    keys = pairs_low.shape[0]
    pairs = queries.shape[1] // (2 * LANES)
    heads = 2 * pairs
    whole = lambda shape: pl.BlockSpec(shape, lambda i: (0, 0))
    column = lambda shape: pl.BlockSpec(shape, lambda i: (0, i))
    scalar = pl.BlockSpec(memory_space=pltpu.SMEM)
    return pl.pallas_call(
        functools.partial(backward_kernel, blocks),
        grid=(pairs,),
        in_specs=[
            scalar,
            column((rows, 2 * LANES)),
            column((keys, 2 * LANES)),
            whole(rope_key.shape),
            pl.BlockSpec((1, 8, rows), lambda i: (i, 0, 0)),
            column((rows, LANES)),
        ]
        + [whole(table.shape) for table in tables],
        out_specs=[
            column((rows, 2 * LANES)),
            column((keys, 2 * LANES)),
            whole((keys, LANES)),
        ],
        out_shape=[
            jax.ShapeDtypeStruct((rows, heads * LANES), BF16),
            jax.ShapeDtypeStruct((keys, heads * LANES), BF16),
            jax.ShapeDtypeStruct((keys, LANES), F32),
        ],
        compiler_params=kernel_params(),
        cost_estimate=pl.CostEstimate(
            flops=10 * heads * rows * keys * LANES,
            bytes_accessed=12 << 20,
            transcendentals=heads * rows * keys,
        ),
        name="attention_backward",
    )(place, queries, pairs_low, rope_key, lse, dout, *tables)


def lane_tables(cos_table, sin_table):
    rows = cos_table.shape[0]
    half = ROPE // 2
    ones = jnp.ones((rows, NOPE), F32)
    before = jnp.zeros((rows, NOPE), F32)
    after = jnp.zeros((rows, LANES - NOPE - ROPE), F32)
    gap = jnp.zeros((rows, half), F32)
    return (
        jnp.concatenate([ones, cos_table, after], axis=1),
        jnp.concatenate([before, -sin_table[:, :half], gap, after], axis=1),
        jnp.concatenate([before, gap, sin_table[:, half:], after], axis=1),
    )


def norm_source_grad(scaled, source, inverse, inner):
    return inverse[:, None] * scaled - source * (inverse * inverse * inverse * inner)[:, None]


def per_device(
    activations,
    attn_gain,
    query_down,
    latent_down,
    query_gain,
    latent_gain,
    query_up,
    latent_up,
    attn_output,
    ffn_gain,
    ffn_gate,
    ffn_up,
    ffn_down,
    out_grad,
):
    n_fsdp = lax.axis_size("fsdp")
    n_ctx = lax.axis_size("ctx")
    n_tp = lax.axis_size("tp")
    shards = n_fsdp * n_ctx
    rows, width = activations.shape
    full_width = width * n_tp
    ctx_index = lax.axis_index("ctx")
    tp_index = lax.axis_index("tp")
    local_heads = query_up.shape[1] // (NOPE + ROPE)
    hidden = ffn_gate.shape[1] // n_ctx
    shard_width = ffn_gate.shape[0]
    per_tp = shards // n_tp

    downs = gather_shards(jnp.concatenate([query_down, latent_down], axis=1))
    gains = gather_shards(jnp.concatenate([query_gain, latent_gain])[None, :].astype(F32))
    q_shard = query_down.shape[1]
    down_query = downs[:, :, :q_shard].transpose(1, 0, 2).reshape(width, QRANK)
    down_latent = downs[:, :, q_shard:].transpose(1, 0, 2).reshape(width, KVRANK + ROPE)
    down_both = jnp.concatenate([down_query, down_latent], axis=1)
    gain_query = gains[:, 0, : query_gain.shape[0]].reshape(QRANK)
    gain_latent = gains[:, 0, query_gain.shape[0] :].reshape(KVRANK)
    full_qup = gather_shards(query_up).reshape(QRANK, local_heads, NOPE + ROPE)
    full_qup = jnp.pad(full_qup, ((0, 0), (0, 0), (0, LANES - NOPE - ROPE)))
    full_qup = full_qup.reshape(QRANK, local_heads * LANES)
    full_kvup = gather_shards(latent_up).reshape(KVRANK, local_heads * LANES)
    full_out = gather_shards(attn_output)
    full_out = full_out.transpose(1, 0, 2).reshape(attn_output.shape[0], full_width)

    def column_chunk(weight):
        cut = weight.reshape(shard_width, n_ctx, hidden).transpose(1, 0, 2)
        stack = gather_fsdp(chunks_to_ctx(cut)).reshape(n_tp, per_tp * shard_width, hidden)
        return relative_blocks(stack, tp_index).reshape(full_width, hidden)

    def row_chunk(weight):
        cut = weight.reshape(n_ctx, hidden, shard_width)
        stack = gather_fsdp(chunks_to_ctx(cut)).reshape(n_tp, per_tp, hidden, shard_width)
        stack = relative_blocks(stack, tp_index).reshape(shards, hidden, shard_width)
        return stack.transpose(1, 0, 2).reshape(hidden, full_width)

    gate_weight = column_chunk(ffn_gate)
    up_weight = column_chunk(ffn_up)
    down_weight = row_chunk(ffn_down)

    def spread_sequence(block):
        pieces = [block] + [from_next(block, "ctx", step) for step in range(1, n_ctx)]
        return spread_rows(jnp.concatenate(pieces, axis=0))

    def fold_sequence(partial_value):
        parts = [partial_value[:, p * width : (p + 1) * width] for p in range(n_tp)]
        mine = fold_tp(parts)
        total = mine[:rows]
        for step in range(1, n_ctx):
            sent = mine[step * rows : (step + 1) * rows].astype(BF16)
            total = total + from_next(sent, "ctx", n_ctx - step).astype(F32)
        return total

    inputs = activations.astype(F32)
    gain_one = attn_gain.astype(F32)
    inverse_one = lax.rsqrt(
        lax.psum(jnp.sum(inputs * inputs, axis=1), "tp") / full_width + EPSILON
    )
    normed_low = (inputs * inverse_one[:, None] * gain_one).astype(BF16)
    latent = tp_total(product(normed_low, down_both))
    query_latent = latent[:, :QRANK]
    kv_latent = latent[:, QRANK : QRANK + KVRANK]
    rope_latent = latent[:, QRANK + KVRANK :]
    inverse_query = lax.rsqrt(jnp.mean(query_latent * query_latent, axis=1) + EPSILON)
    inverse_latent = lax.rsqrt(jnp.mean(kv_latent * kv_latent, axis=1) + EPSILON)
    query_low = (query_latent * inverse_query[:, None] * gain_query).astype(BF16)
    latent_low = (kv_latent * inverse_latent[:, None] * gain_latent).astype(BF16)

    query_pos = ctx_index * rows + jnp.arange(rows, dtype=jnp.int32)
    cos_table, sin_table = rotary_tables(query_pos.astype(F32))
    tables = lane_tables(cos_table, sin_table)
    rope_low = rotate(rope_latent, cos_table, sin_table).astype(BF16)
    rope_low = jnp.pad(rope_low, ((0, 0), (NOPE, LANES - NOPE - ROPE)))
    sent = jnp.concatenate([latent_low, rope_low], axis=1)
    whole = jnp.concatenate(
        [sent] + [from_next(sent, "ctx", step) for step in range(1, n_ctx)], axis=0
    )
    whole_latent = whole[:, :KVRANK]
    rope_key = whole[:, KVRANK:]

    place = ctx_index.astype(jnp.int32).reshape(1)
    attn_low, queries_low, pairs_low, lse = attention_forward(
        place, query_low, full_qup, whole_latent, full_kvup, rope_key, tables, n_ctx
    )
    out_parts = product(attn_low, full_out)
    out_parts = out_parts.reshape(rows, n_tp, width).transpose(1, 0, 2)
    out_parts = relative_blocks(out_parts, tp_index)
    middle = inputs + RESID * fold_tp([out_parts[p] for p in range(n_tp)])

    gain_two = ffn_gain.astype(F32)
    inverse_two = lax.rsqrt(
        lax.psum(jnp.sum(middle * middle, axis=1), "tp") / full_width + EPSILON
    )
    second_low = spread_sequence((middle * inverse_two[:, None] * gain_two).astype(BF16))
    upstream = out_grad.astype(F32)
    branch_low = spread_sequence((RESID * upstream).astype(BF16))
    hidden_grad = times_transposed(branch_low, down_weight)
    gate = product(second_low, gate_weight)
    upper = product(second_low, up_weight)
    sigmoid_gate = jax.nn.sigmoid(gate)
    activated = gate * sigmoid_gate
    hidden_low = (activated * upper).astype(BF16)
    gate_low = (hidden_grad * upper * sigmoid_gate * (1.0 + gate * (1.0 - sigmoid_gate))).astype(BF16)
    upper_low = (hidden_grad * activated).astype(BF16)
    second_grad = fold_sequence(
        times_transposed(gate_low, gate_weight) + times_transposed(upper_low, up_weight)
    )
    result = middle + RESID * fold_sequence(product(hidden_low, down_weight))
    scaled_two = second_grad * gain_two
    grad_gain_two = jnp.sum(second_grad * middle * inverse_two[:, None], axis=0)
    middle_grad = upstream + norm_source_grad(
        scaled_two,
        middle,
        inverse_two,
        lax.psum(jnp.sum(scaled_two * middle, axis=1), "tp") / full_width,
    )

    def column_owner(grad):
        stack = relative_blocks(grad.reshape(n_tp, per_tp * shard_width, hidden), tp_index)
        got = shard_exchange(stack.reshape(shards, shard_width, hidden))
        return got.transpose(1, 0, 2).reshape(shard_width, n_ctx * hidden).astype(F32)

    def row_owner(grad):
        stack = grad.reshape(hidden, n_tp, width).transpose(1, 0, 2)
        stack = relative_blocks(stack, tp_index).reshape(n_tp, hidden, per_tp, shard_width)
        stack = stack.transpose(0, 2, 1, 3).reshape(shards, hidden, shard_width)
        return shard_exchange(stack).reshape(n_ctx * hidden, shard_width).astype(F32)

    grad_gate = column_owner(transposed_times(second_low, gate_low))
    grad_up = column_owner(transposed_times(second_low, upper_low))
    grad_down = row_owner(transposed_times(hidden_low, branch_low))

    attn_branch = jnp.stack(tp_spread((RESID * middle_grad).astype(BF16)))
    attn_branch = relative_blocks(attn_branch, tp_index)
    attn_branch_low = attn_branch.transpose(1, 0, 2).reshape(rows, full_width)
    attended_grad_low = times_transposed(attn_branch_low, full_out).astype(BF16)
    grad_out_proj = transposed_times(attn_low, attn_branch_low)
    grad_out = shard_sum(
        grad_out_proj.reshape(attn_output.shape[0], shards, shard_width).transpose(1, 0, 2)
    )
    query_grad_low, pair_grad_low, rope_grads = attention_backward(
        place, queries_low, pairs_low, rope_key, lse, attended_grad_low, tables, n_ctx
    )
    grad_query_up = transposed_times(query_low, query_grad_low)
    grad_query_up = grad_query_up.reshape(QRANK, local_heads, LANES)[:, :, : NOPE + ROPE]
    grad_query_up = shard_sum(grad_query_up.reshape(shards, QRANK // shards, query_up.shape[1]))
    grad_latent_up = transposed_times(whole_latent, pair_grad_low)
    grad_latent_up = shard_sum(
        grad_latent_up.reshape(shards, KVRANK // shards, local_heads * LANES)
    )
    kv_parts = jnp.concatenate(
        [
            times_transposed(pair_grad_low, full_kvup),
            rope_grads[:, NOPE : NOPE + ROPE],
        ],
        axis=1,
    )
    kv_total = kv_parts[:rows]
    for step in range(1, n_ctx):
        part = kv_parts[step * rows : (step + 1) * rows].astype(BF16)
        kv_total = kv_total + from_next(part, "ctx", n_ctx - step).astype(F32)
    latent_sums = tp_total(
        jnp.concatenate([times_transposed(query_grad_low, full_qup), kv_total], axis=1)
    )
    query_norm_grad = latent_sums[:, :QRANK]
    latent_norm_grad = latent_sums[:, QRANK : QRANK + KVRANK]
    rope_grad = rotate_back(latent_sums[:, QRANK + KVRANK :], cos_table, sin_table)
    scaled_query = query_norm_grad * gain_query
    grad_gain_query = jnp.sum(query_norm_grad * query_latent * inverse_query[:, None], axis=0)
    query_raw_grad = norm_source_grad(
        scaled_query, query_latent, inverse_query, jnp.mean(scaled_query * query_latent, axis=1)
    )
    scaled_latent = latent_norm_grad * gain_latent
    grad_gain_latent = jnp.sum(latent_norm_grad * kv_latent * inverse_latent[:, None], axis=0)
    latent_raw_grad = norm_source_grad(
        scaled_latent, kv_latent, inverse_latent, jnp.mean(scaled_latent * kv_latent, axis=1)
    )
    latent_grad = jnp.concatenate([query_raw_grad, latent_raw_grad, rope_grad], axis=1)
    latent_grad_low = latent_grad.astype(BF16)

    grad_down_both = transposed_times(normed_low, latent_grad_low)
    query_part = grad_down_both[:, :QRANK].reshape(width, shards, q_shard)
    latent_part = grad_down_both[:, QRANK:].reshape(width, shards, latent_down.shape[1])
    grad_downs = shard_sum(
        jnp.concatenate([query_part, latent_part], axis=2).transpose(1, 0, 2)
    )
    normed_grad = times_transposed(latent_grad_low, down_both)
    grad_gain_one = jnp.sum(normed_grad * inputs * inverse_one[:, None], axis=0)
    row_inner = jnp.sum(latent_grad * latent, axis=1) / inverse_one / full_width
    input_grad = middle_grad + norm_source_grad(
        normed_grad * gain_one, inputs, inverse_one, row_inner
    )
    gain_sums = lax.psum(
        jnp.concatenate([grad_gain_one, grad_gain_two, grad_gain_query, grad_gain_latent]),
        ("fsdp", "ctx"),
    )
    gain_attn_sum = gain_sums[:width]
    gain_ffn_sum = gain_sums[width : 2 * width]
    shard_index = lax.axis_index("fsdp") * n_ctx + ctx_index
    gain_query_sum = lax.dynamic_slice_in_dim(
        gain_sums[2 * width : 2 * width + QRANK], shard_index * query_gain.shape[0], query_gain.shape[0]
    )
    gain_latent_sum = lax.dynamic_slice_in_dim(
        gain_sums[2 * width + QRANK :], shard_index * latent_gain.shape[0], latent_gain.shape[0]
    )
    return (
        result.astype(BF16),
        input_grad,
        gain_attn_sum,
        grad_downs[:, :q_shard],
        grad_downs[:, q_shard:],
        gain_query_sum,
        gain_latent_sum,
        grad_query_up,
        grad_latent_up,
        grad_out,
        gain_ffn_sum,
        grad_gate,
        grad_up,
        grad_down,
    )


def solution(mesh):
    return jax.shard_map(
        per_device,
        mesh=mesh,
        in_specs=(
            P(("fsdp", "ctx"), "tp"),
            P("tp"),
            P("tp", ("fsdp", "ctx")),
            P("tp", ("fsdp", "ctx")),
            P(("fsdp", "ctx")),
            P(("fsdp", "ctx")),
            P(("fsdp", "ctx"), "tp"),
            P(("fsdp", "ctx"), "tp"),
            P("tp", ("fsdp", "ctx")),
            P("tp"),
            P(("fsdp", "ctx"), "tp"),
            P(("fsdp", "ctx"), "tp"),
            P("tp", ("fsdp", "ctx")),
            P(("fsdp", "ctx"), "tp"),
        ),
        out_specs=(
            P(("fsdp", "ctx"), "tp"),
            P(("fsdp", "ctx"), "tp"),
            P("tp"),
            P("tp", ("fsdp", "ctx")),
            P("tp", ("fsdp", "ctx")),
            P(("fsdp", "ctx")),
            P(("fsdp", "ctx")),
            P(("fsdp", "ctx"), "tp"),
            P(("fsdp", "ctx"), "tp"),
            P("tp", ("fsdp", "ctx")),
            P("tp"),
            P(("fsdp", "ctx"), "tp"),
            P(("fsdp", "ctx"), "tp"),
            P("tp", ("fsdp", "ctx")),
        ),
        check_vma=False,
    )
```

```python
import functools
import math

import jax
import jax.numpy as jnp
import numpy as np
from jax import lax
from jax.experimental import pallas as pl
from jax.experimental.pallas import tpu as pltpu
from jax.sharding import PartitionSpec as P

NOPE = 64
ROPE = 32
VDIM = 64
QRANK = 768
KVRANK = 256
LANES = 128
SUBLANES = 16

RESID = 1.4 / math.sqrt(62.0)
EPSILON = 1e-05
NEGATIVE = -1e30
SCORE = 1.0 / math.sqrt(NOPE + ROPE)

F32 = jnp.float32
BF16 = jnp.bfloat16

LATENT = QRANK + KVRANK
LAT_COLS = LATENT + LANES
LOW_ROWS = LAT_COLS - QRANK


def round_up(size, unit):
    return -(-size // unit) * unit


def product(left, right):
    return jnp.dot(left, right, preferred_element_type=F32)


def times_transposed(left, right):
    return lax.dot_general(left, right, (((1,), (1,)), ((), ())), preferred_element_type=F32)


def transposed_times(left, right):
    return lax.dot_general(left, right, (((0,), (0,)), ((), ())), preferred_element_type=F32)


def rotary_tables(positions):
    exponent = jnp.arange(0, ROPE, 2, dtype=F32) / ROPE
    inverse = 1.0 / 10000.0**exponent
    angles = positions[:, None] * inverse[None, :]
    angles = jnp.concatenate([angles, angles], axis=1)
    return (jnp.cos(angles), jnp.sin(angles))


def lane_tables(cos_table, sin_table):
    rows = cos_table.shape[0]
    half = ROPE // 2
    ones = jnp.ones((rows, NOPE), F32)
    before = jnp.zeros((rows, NOPE), F32)
    after = jnp.zeros((rows, LANES - NOPE - ROPE), F32)
    gap = jnp.zeros((rows, half), F32)
    return (
        jnp.concatenate([ones, cos_table, after], axis=1),
        jnp.concatenate([before, -sin_table[:, :half], gap, after], axis=1),
        jnp.concatenate([before, gap, sin_table[:, half:], after], axis=1),
    )


def turn_lanes(values, cos_table, lower_table, upper_table, sign):
    return (
        values * cos_table
        + sign * (pltpu.roll(values, LANES - ROPE // 2, 1) * lower_table)
        + sign * (pltpu.roll(values, ROPE // 2, 1) * upper_table)
    )


def swap(value, axis, distance):
    size = lax.axis_size(axis)
    return lax.ppermute(value, axis, [(i, i ^ distance) for i in range(size)])


def after(value, *others):
    return lax.optimization_barrier((value,) + others)[0]


def spread_ctx(own):
    first = swap(own, "ctx", 1)
    second = swap(own, "ctx", 2)
    return [own, first, second, swap(second, "ctx", 1)]


def exchange_ctx(chunks):
    return [chunks[0]] + [swap(chunks[k], "ctx", k) for k in range(1, len(chunks))]


def sum_ctx(parts):
    third = swap(parts[3].astype(BF16), "ctx", 1)
    far = (parts[2].astype(F32) + third.astype(F32)).astype(BF16)
    near = swap(parts[1].astype(BF16), "ctx", 1)
    return parts[0].astype(F32) + near.astype(F32) + swap(far, "ctx", 2).astype(F32)


def spread_tp(own):
    far = swap(own, "tp", 2)
    return [own, swap(own, "tp", 1), far, swap(far, "tp", 1)]


def fold_halves(keep, send):
    pair = (keep + swap(send, "tp", 1)).astype(BF16)
    mine = pair.astype(F32) + swap(pair, "tp", 2).astype(F32)
    return mine, swap(mine, "tp", 1)


def at_once(copies):
    for copy in copies:
        copy.start()
    for copy in copies:
        copy.wait()


def shard_place(where, index, n_ctx):
    return (where[0] ^ (index // n_ctx)) * n_ctx + (where[1] ^ (index % n_ctx))


def row_copies(where, pieces, first_row, rows, target, sems, first_sem, n_ctx):
    if len(pieces) == 1:
        return [pltpu.make_async_copy(pieces[0], target, sems.at[first_sem])]
    out = []
    for index, piece in enumerate(pieces):
        start = pl.multiple_of(shard_place(where, index, n_ctx) * rows, SUBLANES)
        out.append(
            pltpu.make_async_copy(
                piece.at[pl.ds(first_row, rows), :],
                target.at[pl.ds(start, rows), :],
                sems.at[first_sem + index],
            )
        )
    return out


def feature_start(where, place, width):
    return pl.multiple_of((where[2] ^ place) * width, LANES)


def feature_copies(where, pieces, target, row, rows, width, sems, first_sem):
    return [
        pltpu.make_async_copy(
            piece,
            target.at[pl.ds(row, rows), pl.ds(feature_start(where, place, width), width)],
            sems.at[first_sem + place],
        )
        for place, piece in enumerate(pieces)
    ]


def run_kernel(body, inputs, outputs, scratch, flops, moved, name, grid=None, exps=0):
    return pl.pallas_call(
        body,
        grid=grid if grid is not None else (),
        in_specs=[spec for _, spec in inputs],
        out_specs=[spec for _, spec in outputs],
        out_shape=[shape for shape, _ in outputs],
        scratch_shapes=scratch,
        compiler_params=pltpu.CompilerParams(vmem_limit_bytes=56 << 20),
        cost_estimate=pl.CostEstimate(flops=flops, bytes_accessed=moved, transcendentals=exps),
        name=name,
    )(*[array for array, _ in inputs])


VMEM = pl.BlockSpec(memory_space=pltpu.VMEM)
SMEM = pl.BlockSpec(memory_space=pltpu.SMEM)
ANY = pl.BlockSpec(memory_space=pl.ANY)


def shape(dims, dtype=BF16):
    return jax.ShapeDtypeStruct(dims, dtype)


def cut_hidden(where, gate, up, down):
    rows, total = gate.shape
    hidden = total // 4
    columns = round_up(3 * hidden, LANES)

    def body(where_ref, gate_ref, up_ref, down_ref, *rest):
        outs, stage = rest[:4], rest[4]
        blank = jnp.zeros((rows, columns - 3 * hidden), BF16)
        for place in range(4):
            units = slice(place * hidden, (place + 1) * hidden)
            turned = jnp.transpose(down_ref[units, :])
            stage[place] = jnp.concatenate(
                [gate_ref[:, units], up_ref[:, units], turned, blank], axis=1
            )
        for step, out in enumerate(outs):
            out[...] = stage[where_ref[1] ^ step]

    return run_kernel(
        body,
        [(where, SMEM), (gate, VMEM), (up, VMEM), (down, VMEM)],
        [(shape((rows, columns)), VMEM)] * 4,
        [pltpu.VMEM((4, rows, columns), BF16)],
        0,
        12 * rows * total,
        "cut_hidden",
    )


def join_hidden(where, pieces, hidden):
    rows = pieces[0].shape[0]

    def body(where_ref, p0, p1, p2, p3, gate_ref, up_ref, down_ref, stage):
        for step, piece in enumerate((p0, p1, p2, p3)):
            stage[where_ref[1] ^ step] = piece[...]
        for first, out in ((0, gate_ref), (hidden, up_ref)):
            out[...] = jnp.concatenate(
                [stage[place][:, first : first + hidden].astype(F32) for place in range(4)], axis=1
            )
        for place in range(4):
            part = stage[place][:, 2 * hidden : 3 * hidden].astype(F32)
            down_ref[place * hidden : (place + 1) * hidden, :] = jnp.transpose(part)

    return run_kernel(
        body,
        [(where, SMEM)] + [(piece, VMEM) for piece in pieces],
        [
            (shape((rows, 4 * hidden), F32), VMEM),
            (shape((rows, 4 * hidden), F32), VMEM),
            (shape((4 * hidden, rows), F32), VMEM),
        ],
        [pltpu.VMEM((4,) + pieces[0].shape, BF16)],
        0,
        80 * rows * hidden,
        "join_hidden",
    )


def latent_products(where, normed, pick, query_pieces, low_pieces, query_rows, low_rows, first_low, n_ctx):
    rows, width = normed.shape
    half = rows // 2
    shared = query_pieces is low_pieces
    arrays = list(query_pieces) if shared else list(query_pieces) + list(low_pieces)

    def body(where_ref, normed_ref, pick_ref, *rest):
        refs = rest[: len(arrays)]
        keep, send, joined, low_in, total, sems = rest[len(arrays) :]
        query_refs = refs[: len(query_pieces)]
        low_refs = query_refs if shared else refs[len(query_pieces) :]
        copies = row_copies(
            where_ref, query_refs, 0, query_rows, joined.at[pl.ds(0, QRANK), :], sems, 0, n_ctx
        )
        copies += row_copies(
            where_ref, low_refs, first_low, low_rows, low_in, sems, len(query_refs), n_ctx
        )
        at_once(copies)
        joined[QRANK:, :] = product(pick_ref[...], low_in[...]).astype(BF16)
        total[...] = times_transposed(normed_ref[...], joined[...])
        core = where_ref[3]
        keep[...] = total[pl.ds(pl.multiple_of(core * half, 8), half), :]
        send[...] = total[pl.ds(pl.multiple_of((1 - core) * half, 8), half), :]

    return run_kernel(
        body,
        [(where, SMEM), (normed, VMEM), (pick, VMEM)] + [(a, ANY) for a in arrays],
        [
            (shape((half, LAT_COLS), F32), VMEM),
            (shape((half, LAT_COLS), F32), VMEM),
            (shape((LAT_COLS, width)), VMEM),
        ],
        [
            pltpu.VMEM((pick.shape[1], width), BF16),
            pltpu.VMEM((rows, LAT_COLS), F32),
            pltpu.SemaphoreType.DMA((len(query_pieces) + len(low_pieces),)),
        ],
        2 * rows * width * LAT_COLS,
        8 << 20,
        "latent_products",
    )


def latent_norms(where, mine, other, gain_query, gain_latent, tables):
    half = mine.shape[0]
    rows = 2 * half

    def body(where_ref, mine_ref, other_ref, gq, gl, cos_t, lower_t, upper_t, latent, query_low, payload):
        core = where_ref[3]
        latent[pl.ds(pl.multiple_of(core * half, 8), half), :] = mine_ref[...]
        latent[pl.ds(pl.multiple_of((1 - core) * half, 8), half), :] = other_ref[...]
        query = latent[:, :QRANK]
        inverse = lax.rsqrt(jnp.mean(query * query, axis=1, keepdims=True) + EPSILON)
        query_low[...] = (query * inverse * gq[...]).astype(BF16)
        low = latent[:, QRANK:LATENT]
        inverse = lax.rsqrt(jnp.mean(low * low, axis=1, keepdims=True) + EPSILON)
        payload[:, :KVRANK] = (low * inverse * gl[...]).astype(BF16)
        rope = pltpu.roll(latent[:, LATENT:], NOPE, 1)
        payload[:, KVRANK:] = turn_lanes(rope, cos_t[...], lower_t[...], upper_t[...], 1.0).astype(BF16)

    return run_kernel(
        body,
        [(where, SMEM)]
        + [(a, VMEM) for a in (mine, other, gain_query, gain_latent) + tables],
        [
            (shape((rows, LAT_COLS), F32), VMEM),
            (shape((rows, QRANK)), VMEM),
            (shape((rows, KVRANK + LANES)), VMEM),
        ],
        [],
        20 * rows * LAT_COLS,
        4 << 20,
        "latent_norms",
    )


def masked_blocks(scores, place, rows, blocks):
    key_row = lax.broadcasted_iota(jnp.int32, (rows, rows), 0)
    query_column = lax.broadcasted_iota(jnp.int32, (rows, rows), 1)
    out = [jnp.where(key_row <= query_column, scores[:rows], NEGATIVE)]
    for block in range(1, blocks):
        seen = (place ^ block) < place
        out.append(jnp.where(seen, scores[block * rows : (block + 1) * rows], NEGATIVE))
    return out


def head_lanes(index):
    return pl.ds(pl.multiple_of(index * 2 * LANES, 2 * LANES), 2 * LANES)


def up_copies(where_ref, refs, wq, wkv, sems, n_ctx):
    if len(refs) == 2:
        return [
            pltpu.make_async_copy(refs[0], wq, sems.at[0]),
            pltpu.make_async_copy(refs[1], wkv, sems.at[1]),
        ]
    query_rows = QRANK // len(refs)
    low_rows = KVRANK // len(refs)
    return row_copies(where_ref, refs, 0, query_rows, wq, sems, 0, n_ctx) + row_copies(
        where_ref, refs, query_rows, low_rows, wkv, sems, len(refs), n_ctx
    )


def attention_forward(where, query_low, payloads, ups, tables, heads, n_ctx):
    rows = query_low.shape[0]
    blocks = len(payloads)
    keys = blocks * rows
    pairs = heads // 2
    whole = lambda dims: pl.BlockSpec(dims, lambda i: (0, 0))
    column = lambda dims: pl.BlockSpec(dims, lambda i: (0, i))

    def body(where_ref, low_q, cos_t, lower_t, upper_t, *rest):
        sources = rest[:blocks]
        up_refs = rest[blocks : blocks + len(ups)]
        out, q_out, kv_out, lse_out, wq, wkv, tokens, sems = rest[blocks + len(ups) :]
        step = pl.program_id(0)

        @pl.when(step == 0)
        def _():
            copies = up_copies(where_ref, up_refs, wq, wkv, sems, n_ctx)
            first = len(copies)
            for block, source in enumerate(sources):
                copies.append(
                    pltpu.make_async_copy(
                        source, tokens.at[pl.ds(block * rows, rows), :], sems.at[first + block]
                    )
                )
            at_once(copies)

        key_lane = lax.broadcasted_iota(jnp.int32, (keys, LANES), 1)
        raw_pair = product(low_q[...], wq[:, head_lanes(step)])
        kv_pair = product(tokens[:, :KVRANK], wkv[:, head_lanes(step)]).astype(BF16)
        rope_key = tokens[:, KVRANK:]
        kv_out[...] = kv_pair
        outs = []
        for head in range(2):
            lanes = slice(head * LANES, (head + 1) * LANES)
            query = turn_lanes(
                raw_pair[:, lanes], cos_t[...], lower_t[...], upper_t[...], 1.0
            ).astype(BF16)
            pair = kv_pair[:, lanes]
            key = jnp.where(key_lane < NOPE, pair, rope_key)
            q_out[:, lanes] = query
            scores = times_transposed(key, query) * SCORE
            masked = masked_blocks(scores, where_ref[1], rows, blocks)
            top = functools.reduce(
                jnp.maximum, [jnp.max(part, axis=0, keepdims=True) for part in masked]
            )
            powers = [jnp.exp(part - top) for part in masked]
            total = sum(jnp.sum(part, axis=0, keepdims=True) for part in powers)
            prob = jnp.concatenate([part.astype(BF16) for part in powers], axis=0)
            mixed = transposed_times(pair, prob) / total
            outs.append(jnp.transpose(mixed))
            lse_out[0, head : head + 1, :] = top + jnp.log(total)
        lane = lax.broadcasted_iota(jnp.int32, (rows, LANES), 1)
        out[...] = jnp.where(lane < VDIM, pltpu.roll(outs[0], VDIM, 1), outs[1]).astype(BF16)

    return run_kernel(
        body,
        [(where, SMEM), (query_low, whole(query_low.shape))]
        + [(table, whole(table.shape)) for table in tables]
        + [(a, ANY) for a in list(payloads) + list(ups)],
        [
            (shape((rows, pairs * LANES)), column((rows, LANES))),
            (shape((rows, heads * LANES)), column((rows, 2 * LANES))),
            (shape((keys, heads * LANES)), column((keys, 2 * LANES))),
            (shape((pairs, 8, rows), F32), pl.BlockSpec((1, 8, rows), lambda i: (i, 0, 0))),
        ],
        [
            pltpu.VMEM((QRANK, heads * LANES), BF16),
            pltpu.VMEM((KVRANK, heads * LANES), BF16),
            pltpu.VMEM((keys, KVRANK + LANES), BF16),
            pltpu.SemaphoreType.DMA((2 * len(ups) + blocks,)),
        ],
        2 * heads * rows * (QRANK + 2 * keys) * LANES + 2 * heads * keys * KVRANK * LANES,
        12 << 20,
        "attention_forward",
        grid=(pairs,),
        exps=heads * rows * keys,
    )


def attention_backward(where, queries, pairs_low, lse, payloads, ups, branch, outs_w, tables, n_ctx):
    rows, q_lanes = queries.shape
    heads = q_lanes // LANES
    pairs = heads // 2
    blocks = len(payloads)
    keys = blocks * rows
    width = branch[0].shape[1]
    full_width = 4 * width
    inner = outs_w[0].shape[1]
    whole = lambda dims: pl.BlockSpec(dims, lambda i: (0, 0))
    column = lambda dims: pl.BlockSpec(dims, lambda i: (0, i))
    moved = list(payloads) + list(ups) + list(branch) + list(outs_w)

    def body(where_ref, q_in, kv_in, lse_in, cos_t, lower_t, upper_t, *rest):
        refs = rest[: len(moved)]
        (dq_out, dkv_out, query_sum, kv_keep, kv_1, kv_2, kv_3) = rest[len(moved) : len(moved) + 7]
        wq, wkv, rope_key, wo, grad_in, dout, kv_sum, sems = rest[len(moved) + 7 :]
        step = pl.program_id(0)
        place = where_ref[1]

        @pl.when(step == 0)
        def _():
            at = 0
            sources, at = refs[at : at + blocks], at + blocks
            up_refs, at = refs[at : at + len(ups)], at + len(ups)
            branch_refs, at = refs[at : at + 4], at + 4
            out_refs = refs[at:]
            copies = up_copies(where_ref, up_refs, wq, wkv, sems, n_ctx)
            for block, source in enumerate(sources):
                copies.append(
                    pltpu.make_async_copy(
                        source.at[:, pl.ds(KVRANK, LANES)],
                        rope_key.at[pl.ds(block * rows, rows), :],
                        sems.at[len(copies)],
                    )
                )
            copies += feature_copies(
                where_ref, branch_refs, grad_in, 0, rows, width, sems, len(copies)
            )
            copies += row_copies(
                where_ref, out_refs, 0, full_width // len(out_refs), wo, sems, len(copies), n_ctx
            )
            at_once(copies)
            dout[...] = product(grad_in[...], wo[...]).astype(BF16).astype(F32)
            query_sum[...] = jnp.zeros_like(query_sum)
            kv_sum[...] = jnp.zeros_like(kv_sum)

        key_lane = lax.broadcasted_iota(jnp.int32, (keys, LANES), 1)
        lane = lax.broadcasted_iota(jnp.int32, (rows, LANES), 1)
        both = dout[:, pl.ds(pl.multiple_of(step * LANES, LANES), LANES)]
        dkr = jnp.zeros((keys, LANES), F32)
        dq_parts = []
        dkv_parts = []
        for head in range(2):
            lanes = slice(head * LANES, (head + 1) * LANES)
            query = q_in[:, lanes]
            pair = kv_in[:, lanes]
            key = jnp.where(key_lane < NOPE, pair, rope_key[...])
            upper = pltpu.roll(both, VDIM, 1) if head == 0 else both
            out_grad = jnp.where(lane >= NOPE, upper, 0.0).astype(BF16)
            scores = times_transposed(key, query) * SCORE
            top = lse_in[0, head : head + 1, :]
            masked = masked_blocks(scores, place, rows, blocks)
            prob = jnp.concatenate([jnp.exp(part - top) for part in masked], axis=0)
            prob_grad = times_transposed(pair, out_grad)
            weighted = prob * prob_grad
            delta = jnp.sum(weighted, axis=0, keepdims=True)
            score_grad = (weighted - prob * delta).astype(BF16)
            key_grad = product(score_grad, query) * SCORE
            value_grad = product(prob.astype(BF16), out_grad)
            dkv_parts.append(jnp.where(key_lane < NOPE, key_grad, value_grad).astype(BF16))
            dkr = dkr + key_grad
            query_grad = jnp.transpose(transposed_times(key, score_grad)) * SCORE
            dq_parts.append(
                turn_lanes(query_grad, cos_t[...], lower_t[...], upper_t[...], -1.0).astype(BF16)
            )
        dq_pair = jnp.concatenate(dq_parts, axis=1)
        dkv_pair = jnp.concatenate(dkv_parts, axis=1)
        dq_out[...] = dq_pair
        dkv_out[...] = dkv_pair
        query_sum[...] += times_transposed(dq_pair, wq[:, head_lanes(step)])
        kv_sum[:, :KVRANK] += times_transposed(dkv_pair, wkv[:, head_lanes(step)])
        kv_sum[:, KVRANK:] += jnp.where(key_lane >= NOPE, dkr, 0.0)

        @pl.when(step == pairs - 1)
        def _():
            kv_keep[...] = kv_sum[:rows]
            for block, out in ((1, kv_1), (2, kv_2), (3, kv_3)):
                out[...] = kv_sum[block * rows : (block + 1) * rows].astype(BF16)

    return run_kernel(
        body,
        [
            (where, SMEM),
            (queries, column((rows, 2 * LANES))),
            (pairs_low, column((keys, 2 * LANES))),
            (lse, pl.BlockSpec((1, 8, rows), lambda i: (i, 0, 0))),
        ]
        + [(table, whole(table.shape)) for table in tables]
        + [(a, ANY) for a in moved],
        [
            (shape((rows, heads * LANES)), column((rows, 2 * LANES))),
            (shape((keys, heads * LANES)), column((keys, 2 * LANES))),
            (shape((rows, QRANK), F32), whole((rows, QRANK))),
            (shape((rows, KVRANK + LANES), F32), whole((rows, KVRANK + LANES))),
        ]
        + [(shape((rows, KVRANK + LANES)), whole((rows, KVRANK + LANES)))] * 3,
        [
            pltpu.VMEM((QRANK, heads * LANES), BF16),
            pltpu.VMEM((KVRANK, heads * LANES), BF16),
            pltpu.VMEM((keys, LANES), BF16),
            pltpu.VMEM((full_width, inner), BF16),
            pltpu.VMEM((rows, full_width), BF16),
            pltpu.VMEM((rows, inner), F32),
            pltpu.VMEM((keys, KVRANK + LANES), F32),
            pltpu.SemaphoreType.DMA((2 * len(ups) + blocks + 4 + len(outs_w),)),
        ],
        10 * heads * rows * keys * LANES,
        24 << 20,
        "attention_backward",
        grid=(pairs,),
        exps=heads * rows * keys,
    )


def output_products(where, attended, outs_w, n_ctx):
    rows, inner = attended.shape
    count = len(outs_w)
    full_width = sum(a.shape[0] for a in outs_w)
    width = full_width // 4

    def body(where_ref, attended_ref, *rest):
        refs = rest[:count]
        keep, send, weight, sems = rest[count:]
        at_once(row_copies(where_ref, refs, 0, full_width // count, weight, sems, 0, n_ctx))
        for place in range(4):
            block = weight[pl.ds(feature_start(where_ref, place, width), width), :]
            part = times_transposed(attended_ref[...], block)
            if place % 2 == 0:
                keep[place // 2] = part
            else:
                send[place // 2] = part.astype(BF16)

    return run_kernel(
        body,
        [(where, SMEM), (attended, VMEM)] + [(a, ANY) for a in outs_w],
        [(shape((2, rows, width), F32), VMEM), (shape((2, rows, width)), VMEM)],
        [pltpu.VMEM((full_width, inner), BF16), pltpu.SemaphoreType.DMA((count,))],
        2 * rows * inner * full_width,
        6 << 20,
        "output_products",
    )


def feed_forward(where, tokens, branches, weights, hidden, n_ctx):
    blocks = len(tokens)
    rows, width = tokens[0][0].shape
    full_width = 4 * width
    columns = weights[0].shape[1]
    upper_end = round_up(2 * hidden, LANES)
    lower_start = 2 * hidden // LANES * LANES
    shift = 2 * hidden - lower_start
    lower_cols = columns - lower_start
    flat = [piece for group in tokens for piece in group]
    flat += [piece for group in branches for piece in group]
    total = blocks * rows
    moved = flat + list(weights)

    def body(where_ref, *rest):
        refs = rest[: len(moved)]
        pairs_out, active_out, keep, send, normed, branch, weight, sems = rest[len(moved) :]
        copies = row_copies(
            where_ref, refs[len(flat) :], 0, full_width // len(weights), weight, sems, len(flat), n_ctx
        )
        for block in range(blocks):
            for first, target in ((0, normed), (4 * blocks, branch)):
                at = first + 4 * block
                copies += feature_copies(
                    where_ref, refs[at : at + 4], target, block * rows, rows, width, sems, at
                )
        at_once(copies)

        def hidden_block(block, carry):
            here = pl.ds(pl.multiple_of(block * rows, rows), rows)
            both = product(normed[here, :], weight[:, :upper_end])
            lower = product(branch[here, :], weight[:, lower_start:])
            gate = both[:, :hidden]
            upper = both[:, hidden : 2 * hidden]
            grad = lower[:, shift : shift + hidden]
            sigmoid = 1.0 / (1.0 + jnp.exp(-gate))
            active = gate * sigmoid
            pairs_out[here, :] = jnp.concatenate(
                [
                    grad * upper * sigmoid * (1.0 + gate * (1.0 - sigmoid)),
                    grad * active,
                    jnp.zeros((rows, upper_end - 2 * hidden), F32),
                ],
                axis=1,
            ).astype(BF16)
            active_out[here, :] = jnp.concatenate(
                [
                    jnp.zeros((rows, shift), F32),
                    active * upper,
                    jnp.zeros((rows, lower_cols - shift - hidden), F32),
                ],
                axis=1,
            ).astype(BF16)
            return carry

        lax.fori_loop(0, blocks, hidden_block, 0)
        for place in range(4):
            block = weight[pl.ds(feature_start(where_ref, place, width), width), :upper_end]
            part = times_transposed(pairs_out[...], block).astype(BF16)
            (send if place % 2 else keep)[place // 2] = part

    return run_kernel(
        body,
        [(where, SMEM)] + [(a, ANY) for a in moved],
        [
            (shape((total, upper_end)), VMEM),
            (shape((total, lower_cols)), VMEM),
            (shape((2, total, width)), VMEM),
            (shape((2, total, width)), VMEM),
        ],
        [
            pltpu.VMEM((total, full_width), BF16),
            pltpu.VMEM((total, full_width), BF16),
            pltpu.VMEM((full_width, columns), BF16),
            pltpu.SemaphoreType.DMA((len(moved),)),
        ],
        10 * total * full_width * hidden,
        28 << 20,
        "feed_forward",
        exps=total * hidden,
    )


def feed_forward_result(where, active, weights, hidden, n_ctx):
    total, lower_cols = active.shape
    columns = weights[0].shape[1]
    full_width = sum(a.shape[0] for a in weights)
    width = full_width // 4
    count = len(weights)

    def body(where_ref, active_ref, *rest):
        refs = rest[:count]
        keep, send, weight, sems = rest[count:]
        cut = [ref.at[:, pl.ds(columns - lower_cols, lower_cols)] for ref in refs]
        at_once(row_copies(where_ref, cut, 0, full_width // count, weight, sems, 0, n_ctx))
        for place in range(4):
            block = weight[pl.ds(feature_start(where_ref, place, width), width), :]
            part = times_transposed(active_ref[...], block).astype(BF16)
            (send if place % 2 else keep)[place // 2] = part

    return run_kernel(
        body,
        [(where, SMEM), (active, VMEM)] + [(a, ANY) for a in weights],
        [(shape((2, total, width)), VMEM), (shape((2, total, width)), VMEM)],
        [pltpu.VMEM((full_width, lower_cols), BF16), pltpu.SemaphoreType.DMA((count,))],
        2 * total * full_width * hidden,
        10 << 20,
        "feed_forward_result",
    )


def owner_blocks(where_ref, part, n_ctx):
    per_row = n_ctx // 2
    return (where_ref[0] ^ (part // per_row)) * per_row + ((where_ref[1] // 2) ^ (part % per_row))


def feed_forward_grads(where, tokens, branches, pairs_grad, active, hidden, columns, shards, n_ctx, distance):
    blocks = len(tokens)
    rows, width = tokens[0][0].shape
    total = blocks * rows
    upper_end = pairs_grad.shape[1]
    lower_cols = active.shape[1]
    lower_start = columns - lower_cols
    shard_rows = 4 * width // shards
    flat = [piece for group in tokens for piece in group]
    flat += [piece for group in branches for piece in group]

    def gradient(normed, branch, pairs_ref, active_ref):
        first = transposed_times(normed, pairs_ref[...])
        second = transposed_times(branch, active_ref[...])
        middle = first[:, lower_start:] + second[:, : upper_end - lower_start]
        return jnp.concatenate(
            [first[:, :lower_start], middle, second[:, upper_end - lower_start :]], axis=1
        ).astype(BF16)

    def body(where_ref, pairs_ref, active_ref, *rest):
        refs = rest[: len(flat)]
        rest = rest[len(flat) :]
        outs = rest[: -4]
        normed, branch, stage, sems = rest[-4:]
        copies = []
        for block in range(blocks):
            for first, target in ((0, normed), (4 * blocks, branch)):
                at = first + 4 * block
                copies += feature_copies(
                    where_ref, refs[at : at + 4], target, block * rows, rows, width, sems, at
                )
        at_once(copies)
        if distance is None:
            for place in range(4):
                here = slice(place * width, (place + 1) * width)
                outs[0][here, :] = gradient(normed[:, here], branch[:, here], pairs_ref, active_ref)
            return
        for pair in range(n_ctx // 2):
            place = owner_blocks(where_ref, distance * (n_ctx // 2) + pair, n_ctx)
            here = pl.ds(pl.multiple_of(place * width, LANES), width)
            stage[...] = gradient(normed[:, here], branch[:, here], pairs_ref, active_ref)
            for low in range(2):
                start = pl.multiple_of((low ^ (where_ref[1] % 2)) * shard_rows, SUBLANES)
                outs[2 * pair + low][...] = stage[pl.ds(start, shard_rows), :]

    if distance is None:
        outputs = [(shape((4 * width, columns)), VMEM)]
    else:
        outputs = [(shape((shard_rows, columns)), VMEM)] * n_ctx
    return run_kernel(
        body,
        [(where, SMEM), (pairs_grad, VMEM), (active, VMEM)] + [(a, ANY) for a in flat],
        outputs,
        [
            pltpu.VMEM((total, 4 * width), BF16),
            pltpu.VMEM((total, 4 * width), BF16),
            pltpu.VMEM((width, columns), BF16),
            pltpu.SemaphoreType.DMA((len(flat),)),
        ],
        6 * total * 4 * width * hidden // (1 if distance is None else 2),
        18 << 20,
        "feed_forward_grads",
    )


def output_grads(where, attended, branch, shards, n_ctx, paired):
    rows, inner = attended.shape
    width = branch[0].shape[1]
    shard_rows = 4 * width // shards

    def body(where_ref, attended_ref, b0, b1, b2, b3, *rest):
        outs = rest[:-3]
        grad_in, stage, sems = rest[-3:]
        at_once(feature_copies(where_ref, (b0, b1, b2, b3), grad_in, 0, rows, width, sems, 0))
        for part in range(4):
            place = owner_blocks(where_ref, part, n_ctx) if paired else part
            here = pl.ds(pl.multiple_of(place * width, LANES), width)
            stage[...] = transposed_times(grad_in[:, here], attended_ref[...]).astype(BF16)
            if not paired:
                outs[0][part * width : (part + 1) * width, :] = stage[...]
                continue
            for low in range(2):
                start = pl.multiple_of((low ^ (where_ref[1] % 2)) * shard_rows, SUBLANES)
                outs[2 * part + low][...] = stage[pl.ds(start, shard_rows), :]

    if paired:
        outputs = [(shape((shard_rows, inner)), VMEM)] * shards
    else:
        outputs = [(shape((4 * width, inner)), VMEM)]
    return run_kernel(
        body,
        [(where, SMEM), (attended, VMEM)] + [(a, ANY) for a in branch],
        outputs,
        [
            pltpu.VMEM((rows, 4 * width), BF16),
            pltpu.VMEM((width, inner), BF16),
            pltpu.SemaphoreType.DMA((4,)),
        ],
        2 * rows * inner * 4 * width,
        6 << 20,
        "output_grads",
    )


def up_grads(where, query_low, query_grad, payloads, pair_grad, shards, n_ctx, paired):
    rows = query_low.shape[0]
    blocks = len(payloads)
    lanes = query_grad.shape[1]
    query_rows = QRANK // shards
    low_rows = KVRANK // shards

    def body(where_ref, low_q, dq, dkv, *rest):
        sources = rest[:blocks]
        rest = rest[blocks:]
        outs = rest[:-4]
        tokens, stage_q, stage_kv, sems = rest[-4:]
        at_once(
            [
                pltpu.make_async_copy(
                    source.at[:, pl.ds(0, KVRANK)],
                    tokens.at[pl.ds(block * rows, rows), :],
                    sems.at[block],
                )
                for block, source in enumerate(sources)
            ]
        )
        grad_q = transposed_times(low_q[...], dq[...]).astype(BF16)
        grad_kv = transposed_times(tokens[...], dkv[...]).astype(BF16)
        if not paired:
            outs[0][...] = grad_q
            outs[1][...] = grad_kv
            return
        stage_q[...] = grad_q
        stage_kv[...] = grad_kv
        for index, out in enumerate(outs):
            place = shard_place(where_ref, index, n_ctx)
            out[:query_rows, :] = stage_q[
                pl.ds(pl.multiple_of(place * query_rows, SUBLANES), query_rows), :
            ]
            out[query_rows:, :] = stage_kv[
                pl.ds(pl.multiple_of(place * low_rows, SUBLANES), low_rows), :
            ]

    if paired:
        outputs = [(shape((query_rows + low_rows, lanes)), VMEM)] * shards
    else:
        outputs = [(shape((QRANK, lanes)), VMEM), (shape((KVRANK, lanes)), VMEM)]
    return run_kernel(
        body,
        [(where, SMEM), (query_low, VMEM), (query_grad, VMEM), (pair_grad, VMEM)]
        + [(a, ANY) for a in payloads],
        outputs,
        [
            pltpu.VMEM((blocks * rows, KVRANK), BF16),
            pltpu.VMEM((QRANK, lanes), BF16),
            pltpu.VMEM((KVRANK, lanes), BF16),
            pltpu.SemaphoreType.DMA((blocks,)),
        ],
        2 * lanes * (rows * QRANK + blocks * rows * KVRANK),
        10 << 20,
        "up_grads",
    )


def input_backward(
    where,
    mine,
    other,
    latent,
    gain_query,
    gain_latent,
    tables,
    normed,
    joined,
    activations,
    inverse_one,
    gain_one,
    middle_grad,
    pick,
    query_rows,
    low_rows,
    shards,
    n_ctx,
    paired,
):
    half = mine.shape[0]
    rows, width = normed.shape
    full_width = 4 * width
    low_in = pick.shape[1]

    def body(
        where_ref, mine_ref, other_ref, latent_ref, gq, gl, cos_t, lower_t, upper_t, normed_ref,
        joined_ref, act_ref, inverse_ref, gain_ref, middle_ref, pick_ref, input_out, query_gain_out,
        latent_gain_out, gain_out, *rest
    ):
        outs = rest[:-3]
        sums, stage_q, stage_low = rest[-3:]
        core = where_ref[3]
        sums[pl.ds(pl.multiple_of(core * half, 8), half), :] = mine_ref[...]
        sums[pl.ds(pl.multiple_of((1 - core) * half, 8), half), :] = other_ref[...]
        parts = []
        for first, last, gain, out in (
            (0, QRANK, gq, query_gain_out),
            (QRANK, LATENT, gl, latent_gain_out),
        ):
            source = latent_ref[:, first:last]
            grad = sums[:, first:last]
            inverse = lax.rsqrt(jnp.mean(source * source, axis=1, keepdims=True) + EPSILON)
            out[...] = jnp.sum(grad * source * inverse, axis=0, keepdims=True)
            scaled = grad * gain[...]
            inner = jnp.mean(scaled * source, axis=1, keepdims=True)
            parts.append(inverse * scaled - source * (inverse * inverse * inverse * inner))
        rope = turn_lanes(sums[:, LATENT:], cos_t[...], lower_t[...], upper_t[...], -1.0)
        parts.append(pltpu.roll(rope, LANES - NOPE, 1))
        latent_grad = jnp.concatenate(parts, axis=1)
        low = latent_grad.astype(BF16)
        down_grad = transposed_times(low, normed_ref[...]).astype(BF16)
        if paired:
            stage_q[...] = down_grad[:QRANK]
            stage_low[...] = transposed_times(pick_ref[...], down_grad[QRANK:]).astype(BF16)
            for index, out in enumerate(outs):
                place = shard_place(where_ref, index, n_ctx)
                out[:query_rows, :] = stage_q[
                    pl.ds(pl.multiple_of(place * query_rows, SUBLANES), query_rows), :
                ]
                out[query_rows:, :] = stage_low[
                    pl.ds(pl.multiple_of(place * low_rows, SUBLANES), low_rows), :
                ]
        else:
            outs[0][...] = down_grad
        row_inner = jnp.sum(latent_grad * latent_ref[...], axis=1, keepdims=True)
        normed_grad = product(low, joined_ref[...])
        source = act_ref[...].astype(F32)
        inverse = inverse_ref[...]
        gain_out[...] = jnp.sum(normed_grad * source * inverse, axis=0, keepdims=True)
        input_out[...] = (
            middle_ref[...]
            + inverse * (normed_grad * gain_ref[...])
            - source * (inverse * inverse * row_inner / full_width)
        )

    if paired:
        outputs = [(shape((query_rows + low_rows, width)), VMEM)] * shards
    else:
        outputs = [(shape((LAT_COLS, width)), VMEM)]
    arrays = (mine, other, latent, gain_query, gain_latent) + tables
    arrays += (normed, joined, activations, inverse_one, gain_one, middle_grad, pick)
    return run_kernel(
        body,
        [(where, SMEM)] + [(a, VMEM) for a in arrays],
        [
            (shape((rows, width), F32), VMEM),
            (shape((1, QRANK), F32), VMEM),
            (shape((1, KVRANK), F32), VMEM),
            (shape((1, width), F32), VMEM),
        ]
        + outputs,
        [
            pltpu.VMEM((rows, LAT_COLS), F32),
            pltpu.VMEM((QRANK, width), BF16),
            pltpu.VMEM((low_in, width), BF16),
        ],
        4 * rows * width * LAT_COLS,
        12 << 20,
        "input_backward",
    )


def pick_matrix(columns, rows_each, valid):
    matrix = np.zeros((LOW_ROWS, columns), np.float32)
    for row in range(KVRANK + ROPE):
        matrix[row, row // valid * rows_each + row % valid] = 1.0
    return jnp.asarray(matrix, BF16)


def per_device(
    activations,
    attn_gain,
    query_down,
    latent_down,
    query_gain,
    latent_gain,
    query_up,
    latent_up,
    attn_output,
    ffn_gain,
    ffn_gate,
    ffn_up,
    ffn_down,
    out_grad,
):
    n_fsdp = lax.axis_size("fsdp")
    n_ctx = lax.axis_size("ctx")
    n_tp = lax.axis_size("tp")
    shards = n_fsdp * n_ctx
    paired = n_fsdp == 2 and shards == 2 * n_tp
    rows, width = activations.shape
    full_width = width * n_tp
    fsdp_index = lax.axis_index("fsdp").astype(jnp.int32)
    ctx_index = lax.axis_index("ctx").astype(jnp.int32)
    tp_index = lax.axis_index("tp").astype(jnp.int32)
    shard_index = fsdp_index * n_ctx + ctx_index
    where = jnp.stack([fsdp_index, ctx_index, tp_index, tp_index % 2])
    local_heads = query_up.shape[1] // (NOPE + ROPE)
    hidden = ffn_gate.shape[1] // n_ctx
    columns = round_up(3 * hidden, LANES)
    q_shard = query_down.shape[1]
    low_shard = latent_down.shape[1]
    both_axes = ("fsdp", "ctx")

    def spread_shards(own):
        pieces = spread_ctx(own)
        return pieces + [swap(piece, "fsdp", 1) for piece in pieces]

    def gather_rows(value):
        return lax.all_gather(value, both_axes, axis=0, tiled=True)

    def sum_shards(parts):
        summed = [
            parts[k].astype(F32) + swap(parts[n_ctx + k], "fsdp", 1).astype(F32)
            for k in range(n_ctx)
        ]
        return sum_ctx(summed)

    def scatter_rows(value):
        return lax.psum_scatter(value, both_axes, scatter_dimension=0, tiled=True).astype(F32)

    inputs = activations.astype(F32)
    gain_one = attn_gain.astype(F32)
    inverse_one = lax.rsqrt(
        lax.psum(jnp.sum(inputs * inputs, axis=1), "tp") / full_width + EPSILON
    )
    normed_low = (inputs * inverse_one[:, None] * gain_one).astype(BF16)
    gains = jnp.zeros((QRANK + KVRANK,), F32)
    gains = lax.dynamic_update_slice(
        gains, query_gain.astype(F32), (shard_index * query_gain.shape[0],)
    )
    gains = lax.dynamic_update_slice(
        gains, latent_gain.astype(F32), (QRANK + shard_index * latent_gain.shape[0],)
    )
    gains = lax.psum(gains, both_axes)
    gain_query = gains[None, :QRANK]
    gain_latent = gains[None, QRANK:]

    query_pad = jnp.pad(
        query_up.reshape(query_up.shape[0], local_heads, NOPE + ROPE),
        ((0, 0), (0, 0), (0, LANES - NOPE - ROPE)),
    ).reshape(query_up.shape[0], local_heads * LANES)
    if paired:
        low_rows = round_up(low_shard, SUBLANES)
        pick = pick_matrix(shards * low_rows, low_rows, low_shard)
        down_own = jnp.concatenate(
            [query_down.T, latent_down.T, jnp.zeros((low_rows - low_shard, width), BF16)]
        )
        downs = spread_shards(down_own)
        query_pieces = low_pieces = downs
        first_low = q_shard
        up_own = after(jnp.concatenate([query_pad, latent_up]), downs[1])
        ups = spread_shards(up_own)
        out_own = after(attn_output.T, ups[1])
        outs_w = spread_shards(out_own)
        chunk_after = outs_w[1]
    else:
        low_rows = low_shard
        pick = pick_matrix(LOW_ROWS, KVRANK + ROPE, KVRANK + ROPE)
        query_pieces = [gather_rows(query_down.T)]
        low_pieces = [
            jnp.pad(gather_rows(latent_down.T), ((0, LOW_ROWS - KVRANK - ROPE), (0, 0)))
        ]
        first_low = 0
        ups = [gather_rows(query_pad), gather_rows(latent_up)]
        outs_w = [gather_rows(attn_output.T)]
        chunk_after = outs_w[0]

    chunks = list(cut_hidden(where, ffn_gate, ffn_up, ffn_down))
    chunks[1], chunks[2], chunks[3], _ = lax.optimization_barrier(
        (chunks[1], chunks[2], chunks[3], chunk_after)
    )
    hidden_pieces = exchange_ctx(chunks)
    if paired:
        weights = hidden_pieces + [swap(piece, "fsdp", 1) for piece in hidden_pieces]
    else:
        stack = jnp.stack(hidden_pieces)
        stack = jnp.stack(
            [
                lax.dynamic_index_in_dim(stack, ctx_index ^ k, 0, keepdims=False)
                for k in range(n_ctx)
            ]
        )
        weights = [lax.all_gather(stack, "fsdp", axis=0).reshape(full_width, columns)]

    keep, send, joined = latent_products(
        where, normed_low, pick, query_pieces, low_pieces, q_shard, low_rows, first_low, n_ctx
    )
    mine, other = fold_halves(keep, send)
    query_pos = ctx_index * rows + jnp.arange(rows, dtype=jnp.int32)
    tables = lane_tables(*rotary_tables(query_pos.astype(F32)))
    latent, query_low, payload = latent_norms(where, mine, other, gain_query, gain_latent, tables)
    payloads = spread_ctx(payload)

    attended, queries_low, pairs_low, lse = attention_forward(
        where, query_low, payloads, ups, tables, local_heads, n_ctx
    )

    def fold_tp(keep, send):
        got = swap(send, "tp", 1)
        far = (keep[1].astype(F32) + got[1].astype(F32)).astype(BF16)
        near = keep[0].astype(F32) + got[0].astype(F32)
        return near + swap(far, "tp", 2).astype(F32)

    keep, send = output_products(where, attended, outs_w, n_ctx)
    middle = inputs + RESID * fold_tp(keep, send)

    gain_two = ffn_gain.astype(F32)
    inverse_two = lax.rsqrt(
        lax.psum(jnp.sum(middle * middle, axis=1), "tp") / full_width + EPSILON
    )
    second_low = (middle * inverse_two[:, None] * gain_two).astype(BF16)
    upstream = out_grad.astype(F32)
    branch_own = (RESID * upstream).astype(BF16)
    branches = [spread_tp(block) for block in spread_ctx(after(branch_own, hidden_pieces[1]))]
    tokens = [spread_tp(block) for block in spread_ctx(second_low)]
    pairs_grad, active, keep, send = feed_forward(where, tokens, branches, weights, hidden, n_ctx)

    def fold_sequence(keep, send):
        got = swap(send, "tp", 1)
        totals = []
        for block in reversed(range(n_ctx)):
            here = slice(block * rows, (block + 1) * rows)
            far = (keep[1, here].astype(F32) + got[1, here].astype(F32)).astype(BF16)
            near = keep[0, here].astype(F32) + got[0, here].astype(F32)
            totals.append(near + swap(far, "tp", 2).astype(F32))
        return sum_ctx(totals[::-1])

    second_grad = fold_sequence(keep, send)
    scaled_two = second_grad * gain_two
    grad_gain_two = jnp.sum(second_grad * middle * inverse_two[:, None], axis=0)
    inner_two = lax.psum(jnp.sum(scaled_two * middle, axis=1), "tp") / full_width
    middle_grad = upstream + (
        inverse_two[:, None] * scaled_two
        - middle * (inverse_two * inverse_two * inverse_two * inner_two)[:, None]
    )
    branch = spread_tp((RESID * middle_grad).astype(BF16))

    grads = functools.partial(
        feed_forward_grads, where, tokens, branches, pairs_grad, active, hidden, columns, shards, n_ctx
    )
    if paired:
        sent = grads(1)
        kept = grads(0)
        sums = [
            (kept[k].astype(F32) + swap(sent[k], "fsdp", 1).astype(F32)).astype(BF16)
            for k in range(n_ctx)
        ]
    else:
        total = grads(None)[0].reshape(n_fsdp, n_ctx, full_width // shards, columns)
        total = lax.psum_scatter(total, "fsdp", scatter_dimension=0, tiled=False)
        sums = [
            lax.dynamic_index_in_dim(total, ctx_index ^ k, 0, keepdims=False) for k in range(n_ctx)
        ]
    grad_gate, grad_up, grad_down = join_hidden(where, exchange_ctx(sums), hidden)

    query_grad, pair_grad, query_sum, kv_keep, kv_1, kv_2, kv_3 = attention_backward(
        where, queries_low, pairs_low, lse, payloads, ups, branch, outs_w, tables, n_ctx
    )
    kv_total = sum_ctx([kv_keep, kv_1, kv_2, kv_3])
    both = jnp.concatenate([query_sum, kv_total], axis=1).reshape(2, rows // 2, LAT_COLS)
    mine, other = fold_halves(
        lax.dynamic_index_in_dim(both, tp_index % 2, 0, keepdims=False),
        lax.dynamic_index_in_dim(both, 1 - tp_index % 2, 0, keepdims=False),
    )
    input_grad, grad_query_gain, grad_latent_gain, grad_gain_one, *down_parts = input_backward(
        where,
        mine,
        other,
        latent,
        gain_query,
        gain_latent,
        tables,
        normed_low,
        joined,
        activations,
        inverse_one[:, None],
        gain_one[None, :],
        middle_grad,
        pick,
        q_shard,
        low_rows,
        shards,
        n_ctx,
        paired,
    )
    out_parts = output_grads(where, attended, branch, shards, n_ctx, paired)
    up_parts = up_grads(where, query_low, query_grad, payloads, pair_grad, shards, n_ctx, paired)
    if paired:
        grad_out = sum_shards(out_parts)
        grad_ups = sum_shards(up_parts)
        grad_query_up, grad_latent_up = grad_ups[: query_up.shape[0]], grad_ups[query_up.shape[0] :]
        grad_downs = sum_shards(down_parts)
        grad_query_down = grad_downs[:q_shard]
        grad_latent_down = grad_downs[q_shard : q_shard + low_shard]
    else:
        grad_out = scatter_rows(out_parts[0])
        grad_query_up, grad_latent_up = scatter_rows(up_parts[0]), scatter_rows(up_parts[1])
        grad_query_down = scatter_rows(down_parts[0][:QRANK])
        grad_latent_down = scatter_rows(down_parts[0][QRANK : LATENT + ROPE])
    grad_query_up = grad_query_up.reshape(query_up.shape[0], local_heads, LANES)
    grad_query_up = grad_query_up[:, :, : NOPE + ROPE].reshape(query_up.shape)

    result = middle + RESID * fold_sequence(
        *feed_forward_result(where, active, weights, hidden, n_ctx)
    )
    gain_sums = lax.psum(
        jnp.concatenate(
            [grad_gain_one[0], grad_gain_two, grad_query_gain[0], grad_latent_gain[0]]
        ),
        both_axes,
    )
    gain_query_sum = lax.dynamic_slice_in_dim(
        gain_sums, 2 * width + shard_index * query_gain.shape[0], query_gain.shape[0]
    )
    gain_latent_sum = lax.dynamic_slice_in_dim(
        gain_sums, 2 * width + QRANK + shard_index * latent_gain.shape[0], latent_gain.shape[0]
    )
    return (
        result.astype(BF16),
        input_grad,
        gain_sums[:width],
        grad_query_down.T,
        grad_latent_down.T,
        gain_query_sum,
        gain_latent_sum,
        grad_query_up,
        grad_latent_up,
        grad_out.T,
        gain_sums[width : 2 * width],
        grad_gate,
        grad_up,
        grad_down,
    )


def solution(mesh):
    tokens = P(("fsdp", "ctx"), "tp")
    by_columns = P("tp", ("fsdp", "ctx"))
    by_rows = P(("fsdp", "ctx"), "tp")
    latent_vector = P(("fsdp", "ctx"))
    feature_vector = P("tp")
    weights = (
        feature_vector,
        by_columns,
        by_columns,
        latent_vector,
        latent_vector,
        by_rows,
        by_rows,
        by_columns,
        feature_vector,
        by_rows,
        by_rows,
        by_columns,
    )
    return jax.shard_map(
        per_device,
        mesh=mesh,
        in_specs=(tokens,) + weights + (tokens,),
        out_specs=(tokens, tokens) + weights,
        check_vma=False,
    )
```

```python
import functools
import math

import jax
import jax.numpy as jnp
import numpy as np
from jax import lax
from jax.experimental import pallas as pl
from jax.experimental.pallas import tpu as pltpu
from jax.sharding import PartitionSpec as P

NOPE = 64
ROPE = 32
VDIM = 64
QRANK = 768
KVRANK = 256
LANES = 128
SUBLANES = 16

RESID = 1.4 / math.sqrt(62.0)
EPSILON = 1e-05
NEGATIVE = -1e30
SCORE = 1.0 / math.sqrt(NOPE + ROPE)

F32 = jnp.float32
BF16 = jnp.bfloat16

LATENT = QRANK + KVRANK
LAT_COLS = LATENT + LANES
LOW_ROWS = LAT_COLS - QRANK


CFG = {'df': 'perm', 'tok': 'perm', 'Wx': 'perm', 'Wg': 'perm', 'yout': 'perm', 'psum_row': 1, 'psum_inner': 1, 'psum_gain': 1, 'Wparts': 2, 'zchain': [['a2', 'a1'], ['a3'], ['b2', 'b1'], ['b3']], 'xchain': [['a0'], ['b0'], ['a1'], ['a2'], ['a3'], ['b1'], ['b2'], ['b3']]}


def cfg(key, default=None):
    return CFG.get(key, default)


class Names(dict):
    def pick(self, key):
        return [self[n] for n in cfg(key, []) if n in self]


def round_up(size, unit):
    return -(-size // unit) * unit


def product(left, right):
    return jnp.dot(left, right, preferred_element_type=F32)


def times_transposed(left, right):
    return lax.dot_general(left, right, (((1,), (1,)), ((), ())), preferred_element_type=F32)


def transposed_times(left, right):
    return lax.dot_general(left, right, (((0,), (0,)), ((), ())), preferred_element_type=F32)


def rotary_tables(positions):
    exponent = jnp.arange(0, ROPE, 2, dtype=F32) / ROPE
    inverse = 1.0 / 10000.0**exponent
    angles = positions[:, None] * inverse[None, :]
    angles = jnp.concatenate([angles, angles], axis=1)
    return (jnp.cos(angles), jnp.sin(angles))


def lane_tables(cos_table, sin_table):
    rows = cos_table.shape[0]
    half = ROPE // 2
    ones = jnp.ones((rows, NOPE), F32)
    before = jnp.zeros((rows, NOPE), F32)
    after = jnp.zeros((rows, LANES - NOPE - ROPE), F32)
    gap = jnp.zeros((rows, half), F32)
    return (
        jnp.concatenate([ones, cos_table, after], axis=1),
        jnp.concatenate([before, -sin_table[:, :half], gap, after], axis=1),
        jnp.concatenate([before, gap, sin_table[:, half:], after], axis=1),
    )


def turn_lanes(values, cos_table, lower_table, upper_table, sign):
    return (
        values * cos_table
        + sign * (pltpu.roll(values, LANES - ROPE // 2, 1) * lower_table)
        + sign * (pltpu.roll(values, ROPE // 2, 1) * upper_table)
    )


def swap(value, axis, distance):
    size = lax.axis_size(axis)
    return lax.ppermute(value, axis, [(i, i ^ distance) for i in range(size)])


def together(*arrays):
    count = len(arrays)
    return pl.pallas_call(
        lambda *refs: None,
        in_specs=[pl.BlockSpec(memory_space=pl.ANY)] * count,
        out_specs=[pl.BlockSpec(memory_space=pl.ANY)] * count,
        out_shape=[jax.ShapeDtypeStruct(a.shape, a.dtype) for a in arrays],
        input_output_aliases={i: i for i in range(count)},
        name="together",
    )(*arrays)


def after_copies(value, waits):
    def body(value_ref, *rest):
        rest[-1][...] = value_ref[...]

    return pl.pallas_call(
        body,
        in_specs=[pl.BlockSpec(memory_space=pltpu.VMEM)]
        + [pl.BlockSpec(memory_space=pl.ANY)] * len(waits),
        out_specs=pl.BlockSpec(memory_space=pltpu.VMEM),
        out_shape=jax.ShapeDtypeStruct(value.shape, value.dtype),
        name="after_copies",
    )(value, *waits)


def gated(value, waits):
    return pl.pallas_call(
        lambda *refs: None,
        in_specs=[pl.BlockSpec(memory_space=pl.ANY)] * (1 + len(waits)),
        out_specs=pl.BlockSpec(memory_space=pl.ANY),
        out_shape=jax.ShapeDtypeStruct(value.shape, value.dtype),
        input_output_aliases={0: 0},
        name="gated",
    )(value, *waits)


def in_turn(groups, order, move):
    operands = dict(groups)
    arrived = {}
    before = []
    for group in order:
        group = [name for name in group if name in operands]
        if before:
            both = together(*[operands[name] for name in group], *[arrived[name] for name in before])
            for name, array in zip(group, both[: len(group)]):
                operands[name] = array
            for name, array in zip(before, both[len(group) :]):
                arrived[name] = array
        for name in group:
            arrived[name] = move(name, operands[name])
        before = group
    return operands, arrived


def total_tp(value, tag=""):
    if cfg("psum_" + tag):
        return lax.psum(value, "tp")
    value = value + swap(value, "tp", 1)
    return value + swap(value, "tp", 2)


def spread_ctx(own, direct=False):
    if direct:
        return [own] + [swap(own, "ctx", k) for k in range(1, 4)]
    first = swap(own, "ctx", 1)
    second = swap(own, "ctx", 2)
    return [own, first, second, swap(second, "ctx", 1)]


def exchange_ctx(chunks):
    return [chunks[0]] + [swap(chunks[k], "ctx", k) for k in range(1, len(chunks))]


def sum_ctx(parts, marks=None, meanwhile=(None, None)):
    third = parts[3].astype(BF16)
    if meanwhile[0] is not None:
        third = meanwhile[0](third)
    third = swap(third, "ctx", 1)
    far = (parts[2].astype(F32) + third.astype(F32)).astype(BF16)
    near = swap(parts[1].astype(BF16), "ctx", 1)
    if meanwhile[1] is not None:
        far = meanwhile[1](far, third)
    if marks is not None:
        marks += [third, near]
    return parts[0].astype(F32) + near.astype(F32) + swap(far, "ctx", 2).astype(F32)


def total_shards(value):
    if lax.axis_size("fsdp") != 2 or cfg("psum_gain"):
        return lax.psum(value, ("fsdp", "ctx"))
    for axis, distance in (("fsdp", 1), ("ctx", 1), ("ctx", 2)):
        value = value + swap(value, axis, distance)
    return value


def spread_tp(own):
    far = swap(own, "tp", 2)
    return [own, swap(own, "tp", 1), far, swap(far, "tp", 1)]


def fold_halves(keep, send):
    pair = (keep + swap(send, "tp", 1)).astype(BF16)
    mine = pair.astype(F32) + swap(pair, "tp", 2).astype(F32)
    return mine, swap(mine, "tp", 1)


def at_once(copies):
    for copy in copies:
        copy.start()
    for copy in copies:
        copy.wait()


def shard_place(where, index, n_ctx):
    return (where[0] ^ (index // n_ctx)) * n_ctx + (where[1] ^ (index % n_ctx))


def row_copies(where, pieces, first_row, rows, target, sems, first_sem, n_ctx):
    if len(pieces) == 1:
        return [pltpu.make_async_copy(pieces[0], target, sems.at[first_sem])]
    out = []
    for index, piece in enumerate(pieces):
        start = pl.multiple_of(shard_place(where, index, n_ctx) * rows, SUBLANES)
        out.append(
            pltpu.make_async_copy(
                piece.at[pl.ds(first_row, rows), :],
                target.at[pl.ds(start, rows), :],
                sems.at[first_sem + index],
            )
        )
    return out


def feature_start(where, place, width):
    return pl.multiple_of((where[2] ^ place) * width, LANES)


def feature_copies(where, pieces, target, row, rows, width, sems, first_sem):
    return [
        pltpu.make_async_copy(
            piece,
            target.at[pl.ds(row, rows), pl.ds(feature_start(where, place, width), width)],
            sems.at[first_sem + place],
        )
        for place, piece in enumerate(pieces)
    ]


def run_kernel(body, inputs, outputs, scratch, flops, moved, name, grid=None, exps=0, waits=()):
    count = len(inputs)
    inputs = list(inputs) + [(array, ANY) for array in waits]

    def used(*refs):
        body(*refs[:count], *refs[len(inputs) :])

    return pl.pallas_call(
        used,
        grid=grid if grid is not None else (),
        in_specs=[spec for _, spec in inputs],
        out_specs=[spec for _, spec in outputs],
        out_shape=[shape for shape, _ in outputs],
        scratch_shapes=scratch,
        compiler_params=pltpu.CompilerParams(vmem_limit_bytes=56 << 20),
        cost_estimate=pl.CostEstimate(flops=flops, bytes_accessed=moved, transcendentals=exps),
        name=name,
    )(*[array for array, _ in inputs])


VMEM = pl.BlockSpec(memory_space=pltpu.VMEM)
SMEM = pl.BlockSpec(memory_space=pltpu.SMEM)
ANY = pl.BlockSpec(memory_space=pl.ANY)


def shape(dims, dtype=BF16):
    return jax.ShapeDtypeStruct(dims, dtype)


def cut_hidden(where, gate, up, down, parts=1, waits=()):
    rows, total = gate.shape
    hidden = total // 4
    columns = round_up(3 * hidden, LANES)

    def body(where_ref, gate_ref, up_ref, down_ref, *rest):
        outs, stage = rest[:-1], rest[-1]
        blank = jnp.zeros((rows, columns - 3 * hidden), BF16)
        for place in range(4):
            units = slice(place * hidden, (place + 1) * hidden)
            turned = jnp.transpose(down_ref[units, :])
            stage[place] = jnp.concatenate(
                [gate_ref[:, units], up_ref[:, units], turned, blank], axis=1
            )
        for number, out in enumerate(outs):
            first = number // 4 * (rows // parts)
            out[...] = stage[where_ref[1] ^ (number % 4), first : first + rows // parts]

    return run_kernel(
        body,
        [(where, SMEM), (gate, VMEM), (up, VMEM), (down, VMEM)],
        [(shape((rows // parts, columns)), VMEM)] * (4 * parts),
        [pltpu.VMEM((4, rows, columns), BF16)],
        0,
        12 * rows * total,
        "cut_hidden",
        waits=waits,
    )


def join_hidden(where, pieces, hidden, waits=()):
    rows = pieces[0].shape[0]

    def body(where_ref, p0, p1, p2, p3, gate_ref, up_ref, down_ref, stage):
        for step, piece in enumerate((p0, p1, p2, p3)):
            stage[where_ref[1] ^ step] = piece[...]
        for first, out in ((0, gate_ref), (hidden, up_ref)):
            out[...] = jnp.concatenate(
                [stage[place][:, first : first + hidden].astype(F32) for place in range(4)], axis=1
            )
        for place in range(4):
            part = stage[place][:, 2 * hidden : 3 * hidden].astype(F32)
            down_ref[place * hidden : (place + 1) * hidden, :] = jnp.transpose(part)

    return run_kernel(
        body,
        [(where, SMEM)] + [(piece, VMEM) for piece in pieces],
        [
            (shape((rows, 4 * hidden), F32), VMEM),
            (shape((rows, 4 * hidden), F32), VMEM),
            (shape((4 * hidden, rows), F32), VMEM),
        ],
        [pltpu.VMEM((4,) + pieces[0].shape, BF16)],
        0,
        80 * rows * hidden,
        "join_hidden",
        waits=waits,
    )


def latent_products(
    where, normed, pick, query_pieces, low_pieces, query_rows, low_rows, first_low, n_ctx, paired, waits=()
):
    rows, width = normed.shape
    half = rows // 2
    shared = query_pieces is low_pieces
    shards = len(query_pieces)
    arrays = list(query_pieces) if shared else list(query_pieces) + list(low_pieces)

    def body(where_ref, normed_ref, pick_ref, *rest):
        refs = rest[: len(arrays)]
        keep, send, joined, query_gain, latent_gain, low_in, total, sems = rest[len(arrays) :]
        query_refs = refs[: len(query_pieces)]
        low_refs = query_refs if shared else refs[len(query_pieces) :]
        copies = row_copies(
            where_ref, query_refs, 0, query_rows, joined.at[pl.ds(0, QRANK), :], sems, 0, n_ctx
        )
        copies += row_copies(
            where_ref, low_refs, first_low, low_rows, low_in, sems, len(query_refs), n_ctx
        )
        at_once(copies)
        joined[QRANK:, :] = product(pick_ref[...], low_in[...]).astype(BF16)
        if paired:
            first = LATENT + ROPE
            pieces = joined[first : first + SUBLANES, :LANES].astype(F32)
            query_gain[...] = jnp.concatenate(
                [pieces[i : i + 1, :query_rows] for i in range(shards)], axis=1
            )
            latent_gain[...] = jnp.concatenate(
                [pieces[i : i + 1, query_rows:] for i in range(shards)], axis=1
            )
            joined[first : first + SUBLANES, :] = jnp.zeros((SUBLANES, width), BF16)
        total[...] = times_transposed(normed_ref[...], joined[...])
        core = where_ref[3]
        keep[...] = total[pl.ds(pl.multiple_of(core * half, 8), half), :]
        send[...] = total[pl.ds(pl.multiple_of((1 - core) * half, 8), half), :]

    return run_kernel(
        body,
        [(where, SMEM), (normed, VMEM), (pick, VMEM)] + [(a, ANY) for a in arrays],
        [
            (shape((half, LAT_COLS), F32), VMEM),
            (shape((half, LAT_COLS), F32), VMEM),
            (shape((LAT_COLS, width)), VMEM),
            (shape((1, QRANK), F32), VMEM),
            (shape((1, KVRANK), F32), VMEM),
        ],
        [
            pltpu.VMEM((pick.shape[1], width), BF16),
            pltpu.VMEM((rows, LAT_COLS), F32),
            pltpu.SemaphoreType.DMA((len(query_pieces) + len(low_pieces),)),
        ],
        2 * rows * width * LAT_COLS,
        8 << 20,
        "latent_products",
        waits=waits,
    )


def latent_norms(where, mine, other, gain_query, gain_latent, tables, waits=()):
    half = mine.shape[0]
    rows = 2 * half

    def body(where_ref, mine_ref, other_ref, gq, gl, cos_t, lower_t, upper_t, latent, query_low, payload):
        core = where_ref[3]
        latent[pl.ds(pl.multiple_of(core * half, 8), half), :] = mine_ref[...]
        latent[pl.ds(pl.multiple_of((1 - core) * half, 8), half), :] = other_ref[...]
        query = latent[:, :QRANK]
        inverse = lax.rsqrt(jnp.mean(query * query, axis=1, keepdims=True) + EPSILON)
        query_low[...] = (query * inverse * gq[...]).astype(BF16)
        low = latent[:, QRANK:LATENT]
        inverse = lax.rsqrt(jnp.mean(low * low, axis=1, keepdims=True) + EPSILON)
        payload[:, :KVRANK] = (low * inverse * gl[...]).astype(BF16)
        rope = pltpu.roll(latent[:, LATENT:], NOPE, 1)
        payload[:, KVRANK:] = turn_lanes(rope, cos_t[...], lower_t[...], upper_t[...], 1.0).astype(BF16)

    return run_kernel(
        body,
        [(where, SMEM)]
        + [(a, VMEM) for a in (mine, other, gain_query, gain_latent) + tables],
        [
            (shape((rows, LAT_COLS), F32), VMEM),
            (shape((rows, QRANK)), VMEM),
            (shape((rows, KVRANK + LANES)), VMEM),
        ],
        [],
        20 * rows * LAT_COLS,
        4 << 20,
        "latent_norms",
        waits=waits,
    )


def masked_blocks(scores, place, rows, blocks):
    key_row = lax.broadcasted_iota(jnp.int32, (rows, rows), 0)
    query_column = lax.broadcasted_iota(jnp.int32, (rows, rows), 1)
    out = [jnp.where(key_row <= query_column, scores[:rows], NEGATIVE)]
    for block in range(1, blocks):
        seen = (place ^ block) < place
        out.append(jnp.where(seen, scores[block * rows : (block + 1) * rows], NEGATIVE))
    return out


def head_lanes(index):
    return pl.ds(pl.multiple_of(index * 2 * LANES, 2 * LANES), 2 * LANES)


def up_copies(where_ref, refs, wq, wkv, sems, n_ctx):
    if len(refs) == 1:
        shards = refs[0].shape[0]
        out = []
        for shard in range(shards):
            first = 0
            for total, target in ((QRANK, wq), (KVRANK, wkv)):
                rows = total // shards
                out.append(
                    pltpu.make_async_copy(
                        refs[0].at[shard, pl.ds(first, rows), :],
                        target.at[pl.ds(shard * rows, rows), :],
                        sems.at[len(out)],
                    )
                )
                first += rows
        return out
    if len(refs) == 3:
        return [
            pltpu.make_async_copy(refs[0], wq, sems.at[0]),
            pltpu.make_async_copy(refs[1], wkv, sems.at[1]),
        ]
    shards = len(refs) // 2
    query_rows = QRANK // shards
    low_rows = KVRANK // shards
    refs = refs[:shards]
    return row_copies(where_ref, refs, 0, query_rows, wq, sems, 0, n_ctx) + row_copies(
        where_ref, refs, query_rows, low_rows, wkv, sems, shards, n_ctx
    )


def out_copies(where_ref, refs, target, sems, first_sem, n_ctx):
    if len(refs) == 1:
        shards = refs[0].shape[0]
        first = (QRANK + KVRANK) // shards
        half = target.shape[0] // shards // 2
        inner = target.shape[1]
        return [
            pltpu.make_async_copy(
                refs[0].at[index // 2, pl.ds(first, half), pl.ds(index % 2 * inner, inner)],
                target.at[pl.ds(index * half, half), :],
                sems.at[first_sem + index],
            )
            for index in range(2 * shards)
        ]
    if len(refs) == 3:
        return [pltpu.make_async_copy(refs[2], target, sems.at[first_sem])]
    refs = refs[len(refs) // 2 :]
    return row_copies(where_ref, refs, 0, refs[0].shape[0], target, sems, first_sem, n_ctx)


def sequence_refs(source):
    return [piece for group in source for piece in group] if isinstance(source, list) else [source]


def sequence_shape(source):
    if isinstance(source, list):
        return (4 * len(source),) + source[0][0].shape
    return source.shape


def sequence_copies(where, refs, target, rows, width, sems, first_sem):
    if len(refs) == 1:
        return block_copies(where, refs[0], target, sems, first_sem)
    return [
        feature_copies(
            where, refs[at : at + 4], target, at // 4 * rows, rows, width, sems, first_sem + at
        )
        for at in range(0, len(refs), 4)
    ]


def block_copies(where, source, target, sems, first_sem):
    count, rows, width = source.shape
    lists = []
    for step in range(count // 4):
        lists.append(
            [
                pltpu.make_async_copy(
                    source.at[(where[1] ^ step) * 4 + tp],
                    target.at[pl.ds(step * rows, rows), pl.ds(tp * width, width)],
                    sems.at[first_sem + 4 * step + tp],
                )
                for tp in range(4)
            ]
        )
    return lists


def hidden_copies(where, arrays, target, sems, first_sem, n_ctx, columns=None):
    cut = (lambda ref: ref) if columns is None else (lambda ref: ref.at[:, columns])
    if len(arrays) == 1:
        return [pltpu.make_async_copy(cut(arrays[0]), target, sems.at[first_sem])]
    if len(arrays[0].shape) == 2:
        rows = arrays[0].shape[0]
        parts = target.shape[0] // (rows * 2 * n_ctx)
        out = []
        for number, ref in enumerate(arrays):
            part, index = number // (2 * n_ctx), number % (2 * n_ctx)
            start = shard_place(where, index, n_ctx) * parts + part
            start = pl.multiple_of(start * rows, SUBLANES)
            out.append(
                pltpu.make_async_copy(
                    cut(ref), target.at[pl.ds(start, rows), :], sems.at[first_sem + number]
                )
            )
        return out
    out = []
    step = 0
    for array in arrays:
        places = array.shape[1] if len(array.shape) == 4 else 1
        for number in range(places):
            for fsdp in range(array.shape[0]):
                block = array.at[fsdp, number] if len(array.shape) == 4 else array.at[fsdp]
                rows = block.shape[0]
                start = pl.multiple_of((fsdp * n_ctx + (where[1] ^ step)) * rows, SUBLANES)
                out.append(
                    pltpu.make_async_copy(
                        cut(block), target.at[pl.ds(start, rows), :], sems.at[first_sem + len(out)]
                    )
                )
            step += 1
    return out


def attention_forward(where, query_low, payloads, ups, tables, heads, n_ctx, waits=()):
    rows = query_low.shape[0]
    blocks = len(payloads)
    keys = blocks * rows
    pairs = heads // 2
    whole = lambda dims: pl.BlockSpec(dims, lambda i: (0, 0))
    column = lambda dims: pl.BlockSpec(dims, lambda i: (0, i))

    def body(where_ref, low_q, cos_t, lower_t, upper_t, *rest):
        sources = rest[:blocks]
        up_refs = rest[blocks : blocks + len(ups)]
        out, q_out, kv_out, lse_out, wq, wkv, tokens, sems = rest[blocks + len(ups) :]
        step = pl.program_id(0)

        @pl.when(step == 0)
        def _():
            copies = up_copies(where_ref, up_refs, wq, wkv, sems, n_ctx)
            first = len(copies)
            for block, source in enumerate(sources):
                copies.append(
                    pltpu.make_async_copy(
                        source, tokens.at[pl.ds(block * rows, rows), :], sems.at[first + block]
                    )
                )
            at_once(copies)

        key_lane = lax.broadcasted_iota(jnp.int32, (keys, LANES), 1)
        raw_pair = product(low_q[...], wq[:, head_lanes(step)])
        kv_pair = product(tokens[:, :KVRANK], wkv[:, head_lanes(step)]).astype(BF16)
        rope_key = tokens[:, KVRANK:]
        kv_out[...] = kv_pair
        outs = []
        for head in range(2):
            lanes = slice(head * LANES, (head + 1) * LANES)
            query = turn_lanes(
                raw_pair[:, lanes], cos_t[...], lower_t[...], upper_t[...], 1.0
            ).astype(BF16)
            pair = kv_pair[:, lanes]
            key = jnp.where(key_lane < NOPE, pair, rope_key)
            q_out[:, lanes] = query
            scores = times_transposed(key, query) * SCORE
            masked = masked_blocks(scores, where_ref[1], rows, blocks)
            top = functools.reduce(
                jnp.maximum, [jnp.max(part, axis=0, keepdims=True) for part in masked]
            )
            powers = [jnp.exp(part - top) for part in masked]
            total = sum(jnp.sum(part, axis=0, keepdims=True) for part in powers)
            prob = jnp.concatenate([part.astype(BF16) for part in powers], axis=0)
            mixed = transposed_times(pair, prob) / total
            outs.append(jnp.transpose(mixed))
            lse_out[0, head : head + 1, :] = top + jnp.log(total)
        lane = lax.broadcasted_iota(jnp.int32, (rows, LANES), 1)
        out[...] = jnp.where(lane < VDIM, pltpu.roll(outs[0], VDIM, 1), outs[1]).astype(BF16)

    return run_kernel(
        body,
        [(where, SMEM), (query_low, whole(query_low.shape))]
        + [(table, whole(table.shape)) for table in tables]
        + [(a, ANY) for a in list(payloads) + list(ups)],
        [
            (shape((rows, pairs * LANES)), column((rows, LANES))),
            (shape((rows, heads * LANES)), column((rows, 2 * LANES))),
            (shape((keys, heads * LANES)), column((keys, 2 * LANES))),
            (shape((pairs, 8, rows), F32), pl.BlockSpec((1, 8, rows), lambda i: (i, 0, 0))),
        ],
        [
            pltpu.VMEM((QRANK, heads * LANES), BF16),
            pltpu.VMEM((KVRANK, heads * LANES), BF16),
            pltpu.VMEM((keys, KVRANK + LANES), BF16),
            pltpu.SemaphoreType.DMA((64 + blocks,)),
        ],
        2 * heads * rows * (QRANK + 2 * keys) * LANES + 2 * heads * keys * KVRANK * LANES,
        12 << 20,
        "attention_forward",
        grid=(pairs,),
        exps=heads * rows * keys,
        waits=waits,
    )


def attention_backward(where, queries, pairs_low, lse, payloads, ups, branch, tables, n_ctx, waits=()):
    rows, q_lanes = queries.shape
    heads = q_lanes // LANES
    pairs = heads // 2
    blocks = len(payloads)
    keys = blocks * rows
    width = branch[0].shape[1]
    full_width = 4 * width
    inner = heads * VDIM
    whole = lambda dims: pl.BlockSpec(dims, lambda i: (0, 0))
    column = lambda dims: pl.BlockSpec(dims, lambda i: (0, i))
    moved = list(payloads) + list(ups) + list(branch)

    def body(where_ref, q_in, kv_in, lse_in, cos_t, lower_t, upper_t, *rest):
        refs = rest[: len(moved)]
        (dq_out, dkv_out, query_sum, kv_keep, kv_1, kv_2, kv_3) = rest[len(moved) : len(moved) + 7]
        wq, wkv, rope_key, wo, grad_in, dout, kv_sum, sems = rest[len(moved) + 7 :]
        step = pl.program_id(0)
        place = where_ref[1]

        @pl.when(step == 0)
        def _():
            at = 0
            sources, at = refs[at : at + blocks], at + blocks
            up_refs, at = refs[at : at + len(ups)], at + len(ups)
            branch_refs = refs[at : at + 4]
            copies = up_copies(where_ref, up_refs, wq, wkv, sems, n_ctx)
            for block, source in enumerate(sources):
                copies.append(
                    pltpu.make_async_copy(
                        source.at[:, pl.ds(KVRANK, LANES)],
                        rope_key.at[pl.ds(block * rows, rows), :],
                        sems.at[len(copies)],
                    )
                )
            copies += feature_copies(
                where_ref, branch_refs, grad_in, 0, rows, width, sems, len(copies)
            )
            copies += out_copies(where_ref, up_refs, wo, sems, len(copies), n_ctx)
            at_once(copies)
            dout[...] = product(grad_in[...], wo[...]).astype(BF16).astype(F32)
            query_sum[...] = jnp.zeros_like(query_sum)
            kv_sum[...] = jnp.zeros_like(kv_sum)

        key_lane = lax.broadcasted_iota(jnp.int32, (keys, LANES), 1)
        lane = lax.broadcasted_iota(jnp.int32, (rows, LANES), 1)
        both = dout[:, pl.ds(pl.multiple_of(step * LANES, LANES), LANES)]
        dkr = jnp.zeros((keys, LANES), F32)
        dq_parts = []
        dkv_parts = []
        for head in range(2):
            lanes = slice(head * LANES, (head + 1) * LANES)
            query = q_in[:, lanes]
            pair = kv_in[:, lanes]
            key = jnp.where(key_lane < NOPE, pair, rope_key[...])
            upper = pltpu.roll(both, VDIM, 1) if head == 0 else both
            out_grad = jnp.where(lane >= NOPE, upper, 0.0).astype(BF16)
            scores = times_transposed(key, query) * SCORE
            top = lse_in[0, head : head + 1, :]
            masked = masked_blocks(scores, place, rows, blocks)
            prob = jnp.concatenate([jnp.exp(part - top) for part in masked], axis=0)
            prob_grad = times_transposed(pair, out_grad)
            weighted = prob * prob_grad
            delta = jnp.sum(weighted, axis=0, keepdims=True)
            score_grad = (weighted - prob * delta).astype(BF16)
            key_grad = product(score_grad, query) * SCORE
            value_grad = product(prob.astype(BF16), out_grad)
            dkv_parts.append(jnp.where(key_lane < NOPE, key_grad, value_grad).astype(BF16))
            dkr = dkr + key_grad
            query_grad = jnp.transpose(transposed_times(key, score_grad)) * SCORE
            dq_parts.append(
                turn_lanes(query_grad, cos_t[...], lower_t[...], upper_t[...], -1.0).astype(BF16)
            )
        dq_pair = jnp.concatenate(dq_parts, axis=1)
        dkv_pair = jnp.concatenate(dkv_parts, axis=1)
        dq_out[...] = dq_pair
        dkv_out[...] = dkv_pair
        query_sum[...] += times_transposed(dq_pair, wq[:, head_lanes(step)])
        kv_sum[:, :KVRANK] += times_transposed(dkv_pair, wkv[:, head_lanes(step)])
        kv_sum[:, KVRANK:] += jnp.where(key_lane >= NOPE, dkr, 0.0)

        @pl.when(step == pairs - 1)
        def _():
            kv_keep[...] = kv_sum[:rows]
            for block, out in ((1, kv_1), (2, kv_2), (3, kv_3)):
                out[...] = kv_sum[block * rows : (block + 1) * rows].astype(BF16)

    return run_kernel(
        body,
        [
            (where, SMEM),
            (queries, column((rows, 2 * LANES))),
            (pairs_low, column((keys, 2 * LANES))),
            (lse, pl.BlockSpec((1, 8, rows), lambda i: (i, 0, 0))),
        ]
        + [(table, whole(table.shape)) for table in tables]
        + [(a, ANY) for a in moved],
        [
            (shape((rows, heads * LANES)), column((rows, 2 * LANES))),
            (shape((keys, heads * LANES)), column((keys, 2 * LANES))),
            (shape((rows, QRANK), F32), whole((rows, QRANK))),
            (shape((rows, KVRANK + LANES), F32), whole((rows, KVRANK + LANES))),
        ]
        + [(shape((rows, KVRANK + LANES)), whole((rows, KVRANK + LANES)))] * 3,
        [
            pltpu.VMEM((QRANK, heads * LANES), BF16),
            pltpu.VMEM((KVRANK, heads * LANES), BF16),
            pltpu.VMEM((keys, LANES), BF16),
            pltpu.VMEM((full_width, inner), BF16),
            pltpu.VMEM((rows, full_width), BF16),
            pltpu.VMEM((rows, inner), F32),
            pltpu.VMEM((keys, KVRANK + LANES), F32),
            pltpu.SemaphoreType.DMA((128 + blocks,)),
        ],
        10 * heads * rows * keys * LANES,
        24 << 20,
        "attention_backward",
        grid=(pairs,),
        exps=heads * rows * keys,
        waits=waits,
    )


def output_products(where, attended, ups, full_width, n_ctx, waits=()):
    rows, inner = attended.shape
    count = len(ups)
    width = full_width // 4

    def body(where_ref, attended_ref, *rest):
        refs = rest[:count]
        keep, send, weight, sems = rest[count:]
        at_once(out_copies(where_ref, refs, weight, sems, 0, n_ctx))
        for place in range(4):
            block = weight[pl.ds(feature_start(where_ref, place, width), width), :]
            part = times_transposed(attended_ref[...], block)
            if place % 2 == 0:
                keep[place // 2] = part
            else:
                send[place // 2] = part.astype(BF16)

    return run_kernel(
        body,
        [(where, SMEM), (attended, VMEM)] + [(a, ANY) for a in ups],
        [(shape((2, rows, width), F32), VMEM), (shape((2, rows, width)), VMEM)],
        [pltpu.VMEM((full_width, inner), BF16), pltpu.SemaphoreType.DMA((64,))],
        2 * rows * inner * full_width,
        6 << 20,
        "output_products",
        waits=waits,
    )


def feed_forward(where, tokens, branches, weights, gains, hidden, n_ctx):
    count, rows, width = sequence_shape(tokens)
    blocks = count // 4
    full_width = 4 * width
    columns = weights[0].shape[-1]
    upper_end = round_up(2 * hidden, LANES)
    lower_start = 2 * hidden // LANES * LANES
    shift = 2 * hidden - lower_start
    lower_cols = columns - lower_start
    total = blocks * rows
    token_list, branch_list = sequence_refs(tokens), sequence_refs(branches)
    flat = len(token_list) + len(branch_list)
    moved = token_list + branch_list + list(gains) + list(weights)

    def body(where_ref, *rest):
        refs = rest[: len(moved)]
        pairs_out, active_out, keep, send, inverse_out = rest[len(moved) : len(moved) + 5]
        normed, branch, weight, gain, sems = rest[len(moved) + 5 :]
        first = 2 * count
        weight_copies = feature_copies(
            where_ref, refs[flat : flat + 4], gain, 0, gain.shape[0], width, sems, first
        ) + hidden_copies(where_ref, refs[flat + 4 :], weight, sems, first + 4, n_ctx)
        token_copies = [
            first_list + second_list
            for first_list, second_list in zip(
                sequence_copies(
                    where_ref, refs[: len(token_list)], normed, rows, width, sems, 0
                ),
                sequence_copies(
                    where_ref, refs[len(token_list) : flat], branch, rows, width, sems, count
                ),
            )
        ]
        for copy in weight_copies + sum(token_copies, []):
            copy.start()
        for copy in weight_copies:
            copy.wait()

        def hidden_block(block, carry):
            for number, copies in enumerate(token_copies):

                @pl.when(block == number)
                def _():
                    for copy in copies:
                        copy.wait()

            here = pl.ds(pl.multiple_of(block * rows, rows), rows)
            source = normed[here, :].astype(F32) / gain[:1, :]
            inverse = lax.rsqrt(jnp.mean(source * source, axis=1, keepdims=True) + EPSILON)

            @pl.when(block == 0)
            def _():
                inverse_out[...] = jnp.broadcast_to(inverse, inverse_out.shape)

            both = product(normed[here, :], weight[:, :upper_end]) * inverse
            lower = product(branch[here, :], weight[:, lower_start:])
            gate = both[:, :hidden]
            upper = both[:, hidden : 2 * hidden]
            grad = lower[:, shift : shift + hidden]
            scaled = grad * inverse
            sigmoid = 1.0 / (1.0 + jnp.exp(-gate))
            active = gate * sigmoid
            pairs_out[here, :] = jnp.concatenate(
                [
                    scaled * upper * sigmoid * (1.0 + gate * (1.0 - sigmoid)),
                    scaled * active,
                    jnp.zeros((rows, upper_end - 2 * hidden), F32),
                ],
                axis=1,
            ).astype(BF16)
            active_out[here, :] = jnp.concatenate(
                [
                    jnp.zeros((rows, shift), F32),
                    active * upper,
                    jnp.zeros((rows, lower_cols - shift - hidden), F32),
                ],
                axis=1,
            ).astype(BF16)
            return carry

        lax.fori_loop(0, blocks, hidden_block, 0)
        for place in range(4):
            block = weight[pl.ds(feature_start(where_ref, place, width), width), :upper_end]
            part = times_transposed(pairs_out[...], block).astype(BF16)
            (send if place % 2 else keep)[place // 2] = part

    return run_kernel(
        body,
        [(where, SMEM)] + [(a, ANY) for a in moved],
        [
            (shape((total, upper_end)), VMEM),
            (shape((total, lower_cols)), VMEM),
            (shape((2, total, width)), VMEM),
            (shape((2, total, width)), VMEM),
            (shape((rows, LANES), F32), VMEM),
        ],
        [
            pltpu.VMEM((total, full_width), BF16),
            pltpu.VMEM((total, full_width), BF16),
            pltpu.VMEM((full_width, columns), BF16),
            pltpu.VMEM(gains[0].shape[:1] + (full_width,), F32),
            pltpu.SemaphoreType.DMA((2 * count + 4 + full_width // SUBLANES,)),
        ],
        10 * total * full_width * hidden,
        28 << 20,
        "feed_forward",
        exps=total * hidden,
    )


def feed_forward_result(where, active, weights, rows, hidden, n_ctx, halves, waits=()):
    total, lower_cols = active.shape
    columns = weights[0].shape[-1]
    full_width = sum(a.size for a in weights) // columns
    width = full_width // 4
    count = len(weights)

    def body(where_ref, active_ref, *rest):
        refs = rest[:count]
        outs = rest[count:-2]
        weight, sems = rest[-2:]
        lower = pl.ds(columns - lower_cols, lower_cols)
        at_once(hidden_copies(where_ref, refs, weight, sems, 0, n_ctx, columns=lower))
        for tp in range(4):
            if halves:
                block = weight[pl.ds(feature_start(where_ref, tp, width), width), :]
                part = times_transposed(active_ref[...], block).astype(BF16)
                outs[tp % 2][tp // 2] = part
                continue
            block = weight[tp * width : (tp + 1) * width, :]
            part = times_transposed(active_ref[...], block).astype(BF16)
            for step in range(total // rows):
                outs[0][(where_ref[1] ^ step) * 4 + tp] = part[step * rows : (step + 1) * rows]

    return run_kernel(
        body,
        [(where, SMEM), (active, VMEM)] + [(a, ANY) for a in weights],
        [(shape((2, total, width)), VMEM)] * 2
        if halves
        else [(shape((4 * total // rows, rows, width)), VMEM)],
        [
            pltpu.VMEM((full_width, lower_cols), BF16),
            pltpu.SemaphoreType.DMA((full_width // SUBLANES,)),
        ],
        2 * total * full_width * hidden,
        10 << 20,
        "feed_forward_result",
        waits=waits,
    )


def feed_forward_grads(
    where, tokens, branches, pairs_grad, active, hidden, columns, shards, n_ctx, pair=None, distance=None,
    waits=()
):
    count, rows, width = sequence_shape(tokens)
    token_list, branch_list = sequence_refs(tokens), sequence_refs(branches)
    total = count // 4 * rows
    upper_end = pairs_grad.shape[1]
    lower_cols = active.shape[1]
    lower_start = columns - lower_cols
    shard_rows = 4 * width // shards

    def gradient(normed, branch, pairs_ref, active_ref):
        first = transposed_times(normed, pairs_ref[...])
        second = transposed_times(branch, active_ref[...])
        middle = first[:, lower_start:] + second[:, : upper_end - lower_start]
        return jnp.concatenate(
            [first[:, :lower_start], middle, second[:, upper_end - lower_start :]], axis=1
        ).astype(BF16)

    def body(where_ref, pairs_ref, active_ref, *rest):
        token_refs, rest = rest[: len(token_list)], rest[len(token_list) :]
        branch_refs, rest = rest[: len(branch_list)], rest[len(branch_list) :]
        outs = rest[:-4]
        out = outs[0]
        normed, branch, stage, sems = rest[-4:]
        copies = sequence_copies(where_ref, token_refs, normed, rows, width, sems, 0)
        copies += sequence_copies(where_ref, branch_refs, branch, rows, width, sems, count)
        at_once(sum(copies, []))
        if distance is not None:
            for number in range(n_ctx // 2):
                place = owner_blocks(where_ref, distance * (n_ctx // 2) + number, n_ctx)
                here = pl.ds(pl.multiple_of(place * width, LANES), width)
                stage[...] = gradient(normed[:, here], branch[:, here], pairs_ref, active_ref)
                for low in range(2):
                    start = pl.multiple_of((low ^ (where_ref[1] % 2)) * shard_rows, SUBLANES)
                    outs[2 * number + low][...] = stage[pl.ds(start, shard_rows), :]
            return
        if pair is None:
            for place in range(4):
                here = slice(place * width, (place + 1) * width)
                out[here, :] = gradient(normed[:, here], branch[:, here], pairs_ref, active_ref)
            return
        for fsdp in range(shards // n_ctx):
            place = fsdp * (n_ctx // 2) + ((where_ref[1] // 2) ^ pair)
            here = pl.ds(pl.multiple_of(place * width, LANES), width)
            stage[...] = gradient(normed[:, here], branch[:, here], pairs_ref, active_ref)
            for low in range(2):
                start = pl.multiple_of((low ^ (where_ref[1] % 2)) * shard_rows, SUBLANES)
                out[fsdp, low] = stage[pl.ds(start, shard_rows), :]

    if distance is not None:
        outputs = [(shape((shard_rows, columns)), VMEM)] * n_ctx
    elif pair is None:
        outputs = [(shape((4 * width, columns)), VMEM)]
    else:
        outputs = [(shape((shards // n_ctx, 2, shard_rows, columns)), VMEM)]
    return run_kernel(
        body,
        [(where, SMEM), (pairs_grad, VMEM), (active, VMEM)]
        + [(a, ANY) for a in token_list + branch_list],
        outputs,
        [
            pltpu.VMEM((total, 4 * width), BF16),
            pltpu.VMEM((total, 4 * width), BF16),
            pltpu.VMEM((width, columns), BF16),
            pltpu.SemaphoreType.DMA((2 * count,)),
        ],
        6 * total * 4 * width * hidden // 2,
        18 << 20,
        "feed_forward_grads",
        waits=waits,
    )


def owner_blocks(where_ref, part, n_ctx):
    per_row = n_ctx // 2
    return (where_ref[0] ^ (part // per_row)) * per_row + ((where_ref[1] // 2) ^ (part % per_row))


def output_grads(where, attended, branch, shards, n_ctx, paired, waits=()):
    rows, inner = attended.shape
    width = branch[0].shape[1]
    shard_rows = 4 * width // shards

    def body(where_ref, attended_ref, b0, b1, b2, b3, *rest):
        outs = rest[:-3]
        grad_in, stage, sems = rest[-3:]
        at_once(feature_copies(where_ref, (b0, b1, b2, b3), grad_in, 0, rows, width, sems, 0))
        for part in range(4):
            place = owner_blocks(where_ref, part, n_ctx) if paired else part
            here = pl.ds(pl.multiple_of(place * width, LANES), width)
            stage[...] = transposed_times(grad_in[:, here], attended_ref[...]).astype(BF16)
            if not paired:
                outs[0][part * width : (part + 1) * width, :] = stage[...]
                continue
            for low in range(2):
                start = pl.multiple_of((low ^ (where_ref[1] % 2)) * shard_rows, SUBLANES)
                outs[2 * part + low][...] = stage[pl.ds(start, shard_rows), :]

    if paired:
        outputs = [(shape((shard_rows, inner)), VMEM)] * shards
    else:
        outputs = [(shape((4 * width, inner)), VMEM)]
    return run_kernel(
        body,
        [(where, SMEM), (attended, VMEM)] + [(a, ANY) for a in branch],
        outputs,
        [
            pltpu.VMEM((rows, 4 * width), BF16),
            pltpu.VMEM((width, inner), BF16),
            pltpu.SemaphoreType.DMA((4,)),
        ],
        2 * rows * inner * 4 * width,
        6 << 20,
        "output_grads",
        waits=waits,
    )


def up_grads(where, query_low, query_grad, payloads, pair_grad, shards, n_ctx, paired, waits=()):
    rows = query_low.shape[0]
    blocks = len(payloads)
    lanes = query_grad.shape[1]
    query_rows = QRANK // shards
    low_rows = KVRANK // shards

    def body(where_ref, low_q, dq, dkv, *rest):
        sources = rest[:blocks]
        rest = rest[blocks:]
        outs = rest[:-4]
        tokens, stage_q, stage_kv, sems = rest[-4:]
        at_once(
            [
                pltpu.make_async_copy(
                    source.at[:, pl.ds(0, KVRANK)],
                    tokens.at[pl.ds(block * rows, rows), :],
                    sems.at[block],
                )
                for block, source in enumerate(sources)
            ]
        )
        grad_q = transposed_times(low_q[...], dq[...]).astype(BF16)
        grad_kv = transposed_times(tokens[...], dkv[...]).astype(BF16)
        if not paired:
            outs[0][...] = grad_q
            outs[1][...] = grad_kv
            return
        stage_q[...] = grad_q
        stage_kv[...] = grad_kv
        for index, out in enumerate(outs):
            place = shard_place(where_ref, index, n_ctx)
            out[:query_rows, :] = stage_q[
                pl.ds(pl.multiple_of(place * query_rows, SUBLANES), query_rows), :
            ]
            out[query_rows:, :] = stage_kv[
                pl.ds(pl.multiple_of(place * low_rows, SUBLANES), low_rows), :
            ]

    if paired:
        outputs = [(shape((query_rows + low_rows, lanes)), VMEM)] * shards
    else:
        outputs = [(shape((QRANK, lanes)), VMEM), (shape((KVRANK, lanes)), VMEM)]
    return run_kernel(
        body,
        [(where, SMEM), (query_low, VMEM), (query_grad, VMEM), (pair_grad, VMEM)]
        + [(a, ANY) for a in payloads],
        outputs,
        [
            pltpu.VMEM((blocks * rows, KVRANK), BF16),
            pltpu.VMEM((QRANK, lanes), BF16),
            pltpu.VMEM((KVRANK, lanes), BF16),
            pltpu.SemaphoreType.DMA((blocks,)),
        ],
        2 * lanes * (rows * QRANK + blocks * rows * KVRANK),
        10 << 20,
        "up_grads",
        waits=waits,
    )


def attention_grads(where, attended, branch, query_low, query_grad, payloads, pair_grad, shards, waits=()):
    rows, inner = attended.shape
    width = branch[0].shape[1]
    blocks = len(payloads)
    lanes = query_grad.shape[1]
    query_rows = QRANK // shards
    low_rows = KVRANK // shards
    half = 4 * width // shards // 2

    def body(where_ref, attended_ref, low_q, dq, dkv, *rest):
        sources = rest[:blocks]
        branch_refs = rest[blocks : blocks + 4]
        out, tokens, grad_in, sems = rest[blocks + 4 :]
        copies = [
            pltpu.make_async_copy(
                source.at[:, pl.ds(0, KVRANK)],
                tokens.at[pl.ds(block * rows, rows), :],
                sems.at[block],
            )
            for block, source in enumerate(sources)
        ]
        copies += feature_copies(where_ref, branch_refs, grad_in, 0, rows, width, sems, blocks)
        at_once(copies)
        grad_q = transposed_times(low_q[...], dq[...]).astype(BF16)
        grad_kv = transposed_times(tokens[...], dkv[...]).astype(BF16)
        for shard in range(shards):
            out[shard, :query_rows, :] = grad_q[shard * query_rows : (shard + 1) * query_rows]
            out[shard, query_rows : query_rows + low_rows, :] = grad_kv[
                shard * low_rows : (shard + 1) * low_rows
            ]
        grad_out = transposed_times(grad_in[...], attended_ref[...]).astype(BF16)
        for index in range(2 * shards):
            side = slice(index % 2 * inner, (index % 2 + 1) * inner)
            out[index // 2, query_rows + low_rows :, side] = grad_out[index * half : (index + 1) * half]

    return run_kernel(
        body,
        [(where, SMEM)]
        + [(a, VMEM) for a in (attended, query_low, query_grad, pair_grad)]
        + [(a, ANY) for a in list(payloads) + list(branch)],
        [(shape((shards, query_rows + low_rows + half, lanes)), VMEM)],
        [
            pltpu.VMEM((blocks * rows, KVRANK), BF16),
            pltpu.VMEM((rows, 4 * width), BF16),
            pltpu.SemaphoreType.DMA((blocks + 4,)),
        ],
        2 * lanes * (rows * QRANK + blocks * rows * KVRANK) + 2 * rows * inner * 4 * width,
        16 << 20,
        "attention_grads",
        waits=waits,
    )[0]


def input_backward(
    where,
    mine,
    other,
    latent,
    gain_query,
    gain_latent,
    tables,
    normed,
    joined,
    activations,
    inverse_one,
    gain_one,
    middle_grad,
    pick,
    query_rows,
    low_rows,
    shards,
    n_ctx,
    paired,
    waits=(),
):
    half = mine.shape[0]
    rows, width = normed.shape
    full_width = 4 * width
    low_in = pick.shape[1]

    def body(
        where_ref, mine_ref, other_ref, latent_ref, gq, gl, cos_t, lower_t, upper_t, normed_ref,
        joined_ref, act_ref, inverse_ref, gain_ref, middle_ref, pick_ref, input_out, query_gain_out,
        latent_gain_out, gain_out, *rest
    ):
        outs = rest[:-3]
        sums, stage_q, stage_low = rest[-3:]
        core = where_ref[3]
        sums[pl.ds(pl.multiple_of(core * half, 8), half), :] = mine_ref[...]
        sums[pl.ds(pl.multiple_of((1 - core) * half, 8), half), :] = other_ref[...]
        parts = []
        for first, last, gain, out in (
            (0, QRANK, gq, query_gain_out),
            (QRANK, LATENT, gl, latent_gain_out),
        ):
            source = latent_ref[:, first:last]
            grad = sums[:, first:last]
            inverse = lax.rsqrt(jnp.mean(source * source, axis=1, keepdims=True) + EPSILON)
            out[...] = jnp.sum(grad * source * inverse, axis=0, keepdims=True)
            scaled = grad * gain[...]
            inner = jnp.mean(scaled * source, axis=1, keepdims=True)
            parts.append(inverse * scaled - source * (inverse * inverse * inverse * inner))
        rope = turn_lanes(sums[:, LATENT:], cos_t[...], lower_t[...], upper_t[...], -1.0)
        parts.append(pltpu.roll(rope, LANES - NOPE, 1))
        latent_grad = jnp.concatenate(parts, axis=1)
        low = latent_grad.astype(BF16)
        down_grad = transposed_times(low, normed_ref[...]).astype(BF16)
        if paired:
            stage_q[...] = down_grad[:QRANK]
            gains = [
                jnp.concatenate(
                    [
                        query_gain_out[:, i * query_rows : (i + 1) * query_rows],
                        latent_gain_out[:, i * KVRANK // shards : (i + 1) * KVRANK // shards],
                        jnp.zeros((1, width - LANES), F32),
                    ],
                    axis=1,
                )
                for i in range(shards)
            ]
            first = LATENT + ROPE - QRANK
            low_part = jnp.concatenate(
                [
                    down_grad[QRANK : LATENT + ROPE].astype(F32),
                    jnp.concatenate(gains, axis=0),
                    jnp.zeros((LOW_ROWS - first - shards, width), F32),
                ],
                axis=0,
            ).astype(BF16)
            stage_low[...] = transposed_times(pick_ref[...], low_part).astype(BF16)
            for index, out in enumerate(outs):
                place = shard_place(where_ref, index, n_ctx)
                out[:query_rows, :] = stage_q[
                    pl.ds(pl.multiple_of(place * query_rows, SUBLANES), query_rows), :
                ]
                out[query_rows:, :] = stage_low[
                    pl.ds(pl.multiple_of(place * low_rows, SUBLANES), low_rows), :
                ]
        else:
            outs[0][...] = down_grad
        row_inner = jnp.sum(latent_grad * latent_ref[...], axis=1, keepdims=True)
        normed_grad = product(low, joined_ref[...])
        source = act_ref[...].astype(F32)
        inverse = inverse_ref[...]
        gain_out[...] = jnp.sum(normed_grad * source * inverse, axis=0, keepdims=True)
        input_out[...] = (
            middle_ref[...]
            + inverse * (normed_grad * gain_ref[...])
            - source * (inverse * inverse * row_inner / full_width)
        )

    if paired:
        outputs = [(shape((query_rows + low_rows, width)), VMEM)] * shards
    else:
        outputs = [(shape((LAT_COLS, width)), VMEM)]
    arrays = (mine, other, latent, gain_query, gain_latent) + tables
    arrays += (normed, joined, activations, inverse_one, gain_one, middle_grad, pick)
    return run_kernel(
        body,
        [(where, SMEM)] + [(a, VMEM) for a in arrays],
        [
            (shape((rows, width), F32), VMEM),
            (shape((1, QRANK), F32), VMEM),
            (shape((1, KVRANK), F32), VMEM),
            (shape((1, width), F32), VMEM),
        ]
        + outputs,
        [
            pltpu.VMEM((rows, LAT_COLS), F32),
            pltpu.VMEM((QRANK, width), BF16),
            pltpu.VMEM((low_in, width), BF16),
        ],
        4 * rows * width * LAT_COLS,
        12 << 20,
        "input_backward",
        waits=waits,
    )


def pick_matrix(columns, rows_each, valid):
    matrix = np.zeros((LOW_ROWS, columns), np.float32)
    for row in range(KVRANK + ROPE):
        matrix[row, row // valid * rows_each + row % valid] = 1.0
    for shard in range(columns // rows_each if rows_each > valid else 0):
        matrix[KVRANK + ROPE + shard, shard * rows_each + valid] = 1.0
    return jnp.asarray(matrix, BF16)


def per_device(
    activations,
    attn_gain,
    query_down,
    latent_down,
    query_gain,
    latent_gain,
    query_up,
    latent_up,
    attn_output,
    ffn_gain,
    ffn_gate,
    ffn_up,
    ffn_down,
    out_grad,
):
    n_fsdp = lax.axis_size("fsdp")
    n_ctx = lax.axis_size("ctx")
    n_tp = lax.axis_size("tp")
    shards = n_fsdp * n_ctx
    paired = n_fsdp == 2 and shards == 2 * n_tp
    rows, width = activations.shape
    full_width = width * n_tp
    fsdp_index = lax.axis_index("fsdp").astype(jnp.int32)
    ctx_index = lax.axis_index("ctx").astype(jnp.int32)
    tp_index = lax.axis_index("tp").astype(jnp.int32)
    shard_index = fsdp_index * n_ctx + ctx_index
    where = jnp.stack([fsdp_index, ctx_index, tp_index, tp_index % 2])
    local_heads = query_up.shape[1] // (NOPE + ROPE)
    hidden = ffn_gate.shape[1] // n_ctx
    columns = round_up(3 * hidden, LANES)
    q_shard = query_down.shape[1]
    low_shard = latent_down.shape[1]
    both_axes = ("fsdp", "ctx")

    names = Names()
    up_rows = query_up.shape[0] + latent_up.shape[0]

    def spread_shards(own, tag):
        waits = names.pick(tag + "_z")
        sent = after_copies(own, waits) if waits else own
        pieces = [own] + spread_ctx(sent, cfg(tag + "_direct", False))[1:]
        names.update({tag + str(i): piece for i, piece in enumerate(pieces)})
        waits = names.pick(tag + "_x")
        sent = after_copies(own, waits) if waits else own
        for k, piece in enumerate([sent] + pieces[1:]):
            waits = names.pick(tag + "_x" + str(k))
            if waits:
                piece = after_copies(piece, waits)
            pieces.append(swap(piece, "fsdp", 1))
            names[tag + str(4 + k)] = pieces[-1]
        return pieces

    def gather_rows(value):
        return lax.all_gather(value, both_axes, axis=0, tiled=True)

    def fold_shards(parts):
        return [
            (parts[k].astype(F32) + swap(parts[n_ctx + k], "fsdp", 1).astype(F32)).astype(BF16)
            for k in range(n_ctx)
        ]

    def scatter_rows(value):
        return lax.psum_scatter(value, both_axes, scatter_dimension=0, tiled=True).astype(F32)

    inputs = activations.astype(F32)
    gain_one = attn_gain.astype(F32)
    inverse_one = lax.rsqrt(total_tp(jnp.sum(inputs * inputs, axis=1), "row") / full_width + EPSILON)
    gain_two = ffn_gain.astype(F32)
    gains_two = spread_tp(jnp.broadcast_to(gain_two[None, :], (8, width)))
    normed_low = (inputs * inverse_one[:, None] * gain_one).astype(BF16)
    query_pad = jnp.pad(
        query_up.reshape(query_up.shape[0], local_heads, NOPE + ROPE),
        ((0, 0), (0, 0), (0, LANES - NOPE - ROPE)),
    ).reshape(query_up.shape[0], local_heads * LANES)
    if paired:
        low_rows = round_up(low_shard, SUBLANES)
        pick = pick_matrix(shards * low_rows, low_rows, low_shard)
        down_own = jnp.concatenate(
            [
                query_down.T,
                latent_down.T,
                jnp.pad(
                    jnp.concatenate([query_gain, latent_gain])[None, :],
                    ((0, low_rows - low_shard - 1), (0, width - LANES)),
                ),
            ]
        )
        downs = spread_shards(down_own, "d")
        query_pieces = low_pieces = downs
        first_low = q_shard
        out_own = attn_output.T
        if cfg("A") == "sc":
            half = out_own.shape[0] // 2
            out_own = jnp.concatenate([out_own[:half], out_own[half:]], axis=1)
            held = jnp.concatenate([query_pad, latent_up, out_own])
            waits = names.pick("A_after")
            if waits:
                held = after_copies(held, waits)
            ups = [lax.all_gather(held, both_axes, axis=0)]
            names["A"] = ups[0]
        else:
            ups = spread_shards(jnp.concatenate([query_pad, latent_up]), "u")
            ups = ups + spread_shards(out_own, "o")
    else:
        low_rows = low_shard
        pick = pick_matrix(LOW_ROWS, KVRANK + ROPE, KVRANK + ROPE)
        query_pieces = [gather_rows(query_down.T)]
        low_pieces = [
            jnp.pad(gather_rows(latent_down.T), ((0, LOW_ROWS - KVRANK - ROPE), (0, 0)))
        ]
        first_low = 0
        ups = [gather_rows(query_pad), gather_rows(latent_up), gather_rows(attn_output.T)]

    w_parts = cfg("Wparts", 1) if paired else 1
    chunks = cut_hidden(
        where, ffn_gate, ffn_up, ffn_down, parts=w_parts, waits=names.pick("cut")
    )
    hidden_pieces = exchange_ctx(chunks[:4])
    names["chunk"] = chunks[0]
    names.update({"h" + str(i): piece for i, piece in enumerate(hidden_pieces)})
    if paired and cfg("Wx", "perm") == "perm":
        weights = []
        if cfg("zchain"):
            tags = "abcd"[:w_parts]
            operands = {
                tags[part] + str(k): chunks[4 * part + k] for part in range(w_parts) for k in range(1, 4)
            }
            waits = names.pick("zchain_after")
            if waits:
                for name in cfg("zchain")[0]:
                    operands[name] = gated(operands[name], waits)
            _, got = in_turn(operands, cfg("zchain"), lambda n, v: swap(v, "ctx", int(n[1])))
            for part in range(w_parts):
                got[tags[part] + "0"] = chunks[4 * part]
            waits = names.pick("xchain_after")
            if waits:
                for name in cfg("xchain")[0]:
                    got[name] = gated(got[name], waits)
            if cfg("xchain"):
                got, crossed = in_turn(got, cfg("xchain"), lambda n, v: swap(v, "fsdp", 1))
            else:
                crossed = {n: swap(v, "fsdp", 1) for n, v in got.items()}
            for tag in tags:
                weights += [got[tag + str(k)] for k in range(4)]
                weights += [crossed[tag + str(k)] for k in range(4)]
            names.update({"h" + n: v for n, v in got.items()})
            names.update({"w" + n: v for n, v in crossed.items()})
        for part in range(w_parts if not cfg("zchain") else 0):
            own = exchange_ctx(chunks[4 * part : 4 * part + 4])
            other = [swap(piece, "fsdp", 1) for piece in own]
            weights += own + other
            tag = "abcd"[part] if w_parts > 1 else ""
            names.update({"h" + tag + str(i): piece for i, piece in enumerate(own)})
            names.update({"w" + tag + str(i): piece for i, piece in enumerate(other)})
    elif paired and cfg("Wx") == "sc4":
        weights = [lax.all_gather(piece, "fsdp", axis=0) for piece in hidden_pieces]
        names.update({"w" + str(i): piece for i, piece in enumerate(weights)})
    elif paired:
        weights = [lax.all_gather(piece, "fsdp", axis=0) for piece in hidden_pieces[:2]]
        weights.append(lax.all_gather(jnp.stack(hidden_pieces[2:]), "fsdp", axis=0))
        names.update({"w" + str(i): piece for i, piece in enumerate(weights)})

    def spread_sequence(own, tag):
        if cfg(tag, "perm") == "sc":
            out = lax.all_gather(own, ("ctx", "tp"), axis=0)
            names[tag] = out
            return out
        sent = own
        if cfg(tag + "_gate"):
            waits = names.pick(tag + "_gate")
            sent = together(own, *waits)[0] if False else after_copies(own, waits)
        out = [spread_tp(own)] + [
            spread_tp(block) for block in spread_ctx(sent, cfg(tag + "_direct", False))[1:]
        ]
        for k, group in enumerate(out):
            names.update({tag + str(k) + str(i): piece for i, piece in enumerate(group)})
        return out

    upstream = out_grad.astype(F32)
    branch_own = (RESID * upstream).astype(BF16)
    branches = spread_sequence(branch_own, "df")
    if not paired:
        stack = jnp.stack(hidden_pieces)
        stack = jnp.stack(
            [
                lax.dynamic_index_in_dim(stack, ctx_index ^ k, 0, keepdims=False)
                for k in range(n_ctx)
            ]
        )
        weights = [lax.all_gather(stack, "fsdp", axis=0).reshape(full_width, columns)]

    keep, send, joined, gain_query, gain_latent = latent_products(
        where,
        normed_low,
        pick,
        query_pieces,
        low_pieces,
        q_shard,
        low_rows,
        first_low,
        n_ctx,
        paired,
        waits=names.pick("latent_products"),
    )
    if not paired:
        gains = jnp.zeros((QRANK + KVRANK,), F32)
        gains = lax.dynamic_update_slice(
            gains, query_gain.astype(F32), (shard_index * query_gain.shape[0],)
        )
        gains = lax.dynamic_update_slice(
            gains, latent_gain.astype(F32), (QRANK + shard_index * latent_gain.shape[0],)
        )
        gains = lax.psum(gains, both_axes)
        gain_query = gains[None, :QRANK]
        gain_latent = gains[None, QRANK:]
    mine, other = fold_halves(keep, send)
    names["fold"] = mine
    query_pos = ctx_index * rows + jnp.arange(rows, dtype=jnp.int32)
    tables = lane_tables(*rotary_tables(query_pos.astype(F32)))
    if cfg("psum_lat"):
        names["plat"] = lax.psum(mine[:8, :128] * 0.0, "tp")
    latent, query_low, payload = latent_norms(
        where,
        mine,
        other,
        gain_query,
        gain_latent,
        tables,
        waits=names.pick("latent_norms"),
    )
    payloads = spread_ctx(payload, cfg("pay_direct", False))
    names.update({"p" + str(i): piece for i, piece in enumerate(payloads)})

    attended, queries_low, pairs_low, lse = attention_forward(
        where, query_low, payloads, ups, tables, local_heads, n_ctx, waits=names.pick("attention_forward")
    )

    def fold_tp(keep, send):
        got = swap(send, "tp", 1)
        far = (keep[1].astype(F32) + got[1].astype(F32)).astype(BF16)
        near = keep[0].astype(F32) + got[0].astype(F32)
        return near + swap(far, "tp", 2).astype(F32)

    keep, send = output_products(
        where,
        attended,
        ups,
        full_width,
        n_ctx,
        waits=names.pick("output_products"),
    )
    middle = inputs + RESID * fold_tp(keep, send)

    second_low = (middle * gain_two).astype(BF16)
    if cfg("psum_mid"):
        mark = lax.psum(middle[:8, :128] * 0.0, "tp")
        second_low = gated(second_low, [mark])
    tokens = spread_sequence(second_low, "tok")
    pairs_grad, active, keep, send, inverse_two = feed_forward(
        where, tokens, branches, weights, gains_two, hidden, n_ctx
    )
    inverse_two = inverse_two[:, :1]

    def fold_sequence(keep, send, marks=None, meanwhile=(None, None)):
        got = swap(send, "tp", 1)
        totals = []
        for block in reversed(range(n_ctx)):
            here = slice(block * rows, (block + 1) * rows)
            far = (keep[1, here].astype(F32) + got[1, here].astype(F32)).astype(BF16)
            near = keep[0, here].astype(F32) + got[0, here].astype(F32)
            other = swap(far, "tp", 2)
            if marks is not None:
                marks.append(other)
            totals.append(near + other.astype(F32))
        return sum_ctx(totals[::-1], marks, meanwhile)

    grads = functools.partial(
        feed_forward_grads, where, tokens, branches, pairs_grad, active, hidden, columns, shards, n_ctx
    )
    fold_marks = []
    made = []
    pairwise = cfg("Wg", "perm") == "sc"

    def make_grads(number):
        if pairwise:
            return grads(pair=number, waits=names.pick("grads%d" % number))
        return grads(distance=number, waits=names.pick("grads%d" % number))

    def far_grads(value):
        if not cfg("far_gate"):
            return value
        names["y3"] = fold_marks[0]
        first, *rest = make_grads(1)
        value, first = together(value, first)
        made.append([first] + rest)
        return value

    def near_grads(value, third):
        if not cfg("near_gate"):
            return value
        names["z1"] = third
        first, *rest = make_grads(0)
        value, first = together(value, first)
        made.append([first] + rest)
        return value

    second_grad = fold_sequence(
        keep, send, fold_marks, (far_grads, near_grads) if paired else (None, None)
    )
    names.update({"y3": fold_marks[0], "y0": fold_marks[3], "z1": fold_marks[4], "z1b": fold_marks[5]})
    scaled_two = second_grad * gain_two
    grad_gain_two = jnp.sum(second_grad * middle, axis=0)
    inner_two = total_tp(jnp.sum(scaled_two * middle, axis=1), "inner") / full_width
    middle_grad = upstream + scaled_two - middle * (inverse_two * inverse_two * inner_two[:, None])
    branch = spread_tp((RESID * middle_grad).astype(BF16))

    names.update({"b" + str(i): piece for i, piece in enumerate(branch)})
    halves = cfg("yout", "perm") == "perm"

    def make_result():
        marks = []
        parts = feed_forward_result(
            where, active, weights, rows, hidden, n_ctx, halves, waits=names.pick("ffr")
        )
        names["ffr"] = parts[0]
        if halves:
            total = fold_sequence(*parts, marks)
            names.update({"ry" + str(3 - i): mark for i, mark in enumerate(marks[:4])})
            names.update({"rz3": marks[4], "rz1": marks[5]})
        else:
            total = lax.psum_scatter(parts[0], ("ctx", "tp"), scatter_dimension=0, tiled=False)
            names["rs"] = total
        return middle + RESID * total.astype(F32)

    if not cfg("ffr_late"):
        result = make_result()
    if paired:
        while len(made) < 2:
            made.append(make_grads(1 - len(made)))
        if pairwise:
            far, near = [
                lax.psum_scatter(part[0], "fsdp", scatter_dimension=0, tiled=False) for part in made
            ]
            sums = [near[0], near[1], far[0], far[1]]
            names.update({"far": far, "near": near})
        else:
            sums = [None] * n_ctx
            order = cfg("gchain", [["3", "2", "1", "0"]])
            _, moved = in_turn(
                {str(k): made[0][k] for k in range(n_ctx)}, order, lambda n, v: swap(v, "fsdp", 1)
            )
            names.update({"g" + n: v for n, v in moved.items()})
            for k in range(n_ctx):
                sums[k] = (made[1][k].astype(F32) + moved[str(k)].astype(F32)).astype(BF16)
    else:
        total = grads()[0].reshape(n_fsdp, n_ctx, full_width // shards, columns)
        total = lax.psum_scatter(total, "fsdp", scatter_dimension=0, tiled=False)
        sums = [
            lax.dynamic_index_in_dim(total, ctx_index ^ k, 0, keepdims=False) for k in range(n_ctx)
        ]
    if cfg("hchain"):
        _, got = in_turn(
            {str(k): sums[k] for k in range(1, 4)},
            cfg("hchain"),
            lambda n, v: swap(v, "ctx", int(n)),
        )
        hidden_sums = [sums[0]] + [got[str(k)] for k in range(1, 4)]
    else:
        hidden_sums = exchange_ctx(sums)
    names.update({"hs" + str(i): piece for i, piece in enumerate(hidden_sums)})

    query_grad, pair_grad, query_sum, kv_keep, kv_1, kv_2, kv_3 = attention_backward(
        where,
        queries_low,
        pairs_low,
        lse,
        payloads,
        ups,
        branch,
        tables,
        n_ctx,
        waits=names.pick("attention_backward"),
    )
    names["dq"] = query_sum
    kv_marks = []
    kv_total = sum_ctx([kv_keep, kv_1, kv_2, kv_3], kv_marks)
    names.update({"k3": kv_marks[0], "k1": kv_marks[1]})
    both = jnp.concatenate([query_sum, kv_total], axis=1).reshape(2, rows // 2, LAT_COLS)
    mine, other = fold_halves(
        lax.dynamic_index_in_dim(both, tp_index % 2, 0, keepdims=False),
        lax.dynamic_index_in_dim(both, 1 - tp_index % 2, 0, keepdims=False),
    )
    joint = paired and cfg("A") == "sc"
    if joint:
        joint_parts = attention_grads(
            where,
            attended,
            branch,
            query_low,
            query_grad,
            payloads,
            pair_grad,
            shards,
            waits=names.pick("attention_grads"),
        )
        names["ap"] = joint_parts
    else:
        out_parts = output_grads(
            where, attended, branch, shards, n_ctx, paired, waits=names.pick("output_grads")
        )
        names["op"] = out_parts[0]
        up_parts = up_grads(
            where,
            query_low,
            query_grad,
            payloads,
            pair_grad,
            shards,
            n_ctx,
            paired,
            waits=names.pick("up_grads"),
        )
        names["up"] = up_parts[0]
    if cfg("ffr_late"):
        result = make_result()
    if paired and not joint:
        out_sums = fold_shards(out_parts)
        up_sums = fold_shards(up_parts)
        names.update({"os" + str(i): piece for i, piece in enumerate(out_sums)})
        names.update({"us" + str(i): piece for i, piece in enumerate(up_sums)})
    if cfg("join_early"):
        grad_gate, grad_up, grad_down = join_hidden(
            where, hidden_sums, hidden, waits=names.pick("join_hidden")
        )
        names["gg"] = grad_gate
    input_grad, grad_query_gain, grad_latent_gain, grad_gain_one, *down_parts = input_backward(
        where,
        mine,
        other,
        latent,
        gain_query,
        gain_latent,
        tables,
        normed_low,
        joined,
        activations,
        inverse_one[:, None],
        gain_one[None, :],
        middle_grad,
        pick,
        q_shard,
        low_rows,
        shards,
        n_ctx,
        paired,
        waits=names.pick("input_backward"),
    )
    names["ig"] = down_parts[0]
    if not cfg("join_early"):
        grad_gate, grad_up, grad_down = join_hidden(
            where, hidden_sums, hidden, waits=names.pick("join_hidden")
        )
    if paired:
        if joint:
            held_sum = lax.psum_scatter(joint_parts, both_axes, scatter_dimension=0, tiled=False)
            held_sum = held_sum.astype(F32)
            grad_ups, grad_out = held_sum[: up_rows], held_sum[up_rows:]
            half = grad_out.shape[1] // 2
            grad_out = jnp.concatenate([grad_out[:, :half], grad_out[:, half:]], axis=0)
        else:
            grad_out = sum_ctx(out_sums)
            grad_ups = sum_ctx(up_sums)
        grad_query_up = grad_ups[: query_up.shape[0]]
        grad_latent_up = grad_ups[query_up.shape[0] :]
        grad_downs = sum_ctx(fold_shards(down_parts))
        grad_query_down = grad_downs[:q_shard]
        grad_latent_down = grad_downs[q_shard : q_shard + low_shard]
    else:
        grad_out = scatter_rows(out_parts[0])
        grad_query_up, grad_latent_up = scatter_rows(up_parts[0]), scatter_rows(up_parts[1])
        grad_query_down = scatter_rows(down_parts[0][:QRANK])
        grad_latent_down = scatter_rows(down_parts[0][QRANK : LATENT + ROPE])
    grad_query_up = grad_query_up.reshape(query_up.shape[0], local_heads, LANES)
    grad_query_up = grad_query_up[:, :, : NOPE + ROPE].reshape(query_up.shape)

    gain_sums = total_shards(jnp.concatenate([grad_gain_one[0], grad_gain_two]))
    if paired:
        gain_row = grad_downs[q_shard + low_shard]
        gain_query_sum = gain_row[:q_shard]
        gain_latent_sum = gain_row[q_shard : q_shard + latent_gain.shape[0]]
    else:
        gain_query_sum = scatter_rows(grad_query_gain[0])
        gain_latent_sum = scatter_rows(grad_latent_gain[0])
    return (
        result.astype(BF16),
        input_grad,
        gain_sums[:width],
        grad_query_down.T,
        grad_latent_down.T,
        gain_query_sum,
        gain_latent_sum,
        grad_query_up,
        grad_latent_up,
        grad_out.T,
        gain_sums[width : 2 * width],
        grad_gate,
        grad_up,
        grad_down,
    )


def solution(mesh):
    tokens = P(("fsdp", "ctx"), "tp")
    by_columns = P("tp", ("fsdp", "ctx"))
    by_rows = P(("fsdp", "ctx"), "tp")
    latent_vector = P(("fsdp", "ctx"))
    feature_vector = P("tp")
    weights = (
        feature_vector,
        by_columns,
        by_columns,
        latent_vector,
        latent_vector,
        by_rows,
        by_rows,
        by_columns,
        feature_vector,
        by_rows,
        by_rows,
        by_columns,
    )
    return jax.shard_map(
        per_device,
        mesh=mesh,
        in_specs=(tokens,) + weights + (tokens,),
        out_specs=(tokens, tokens) + weights,
        check_vma=False,
    )
```

```python
import functools
import math

import jax
import jax.numpy as jnp
import numpy as np
from jax import lax
from jax.experimental import pallas as pl
from jax.experimental.pallas import tpu as pltpu
from jax.sharding import PartitionSpec as P

NOPE = 64
ROPE = 32
VDIM = 64
QRANK = 768
KVRANK = 256
LANES = 128
SUBLANES = 16

RESID = 1.4 / math.sqrt(62.0)
EPSILON = 1e-05
NEGATIVE = -1e30
SCORE = 1.0 / math.sqrt(NOPE + ROPE)

F32 = jnp.float32
BF16 = jnp.bfloat16

LATENT = QRANK + KVRANK
LAT_COLS = LATENT + LANES
LOW_ROWS = LAT_COLS - QRANK


def round_up(size, unit):
    return -(-size // unit) * unit


def product(left, right):
    return jnp.dot(left, right, preferred_element_type=F32)


def times_transposed(left, right):
    return lax.dot_general(left, right, (((1,), (1,)), ((), ())), preferred_element_type=F32)


def transposed_times(left, right):
    return lax.dot_general(left, right, (((0,), (0,)), ((), ())), preferred_element_type=F32)


def rotary_tables(positions):
    exponent = jnp.arange(0, ROPE, 2, dtype=F32) / ROPE
    inverse = 1.0 / 10000.0**exponent
    angles = positions[:, None] * inverse[None, :]
    angles = jnp.concatenate([angles, angles], axis=1)
    return (jnp.cos(angles), jnp.sin(angles))


def lane_tables(cos_table, sin_table):
    rows = cos_table.shape[0]
    half = ROPE // 2
    ones = jnp.ones((rows, NOPE), F32)
    before = jnp.zeros((rows, NOPE), F32)
    after = jnp.zeros((rows, LANES - NOPE - ROPE), F32)
    gap = jnp.zeros((rows, half), F32)
    return (
        jnp.concatenate([ones, cos_table, after], axis=1),
        jnp.concatenate([before, -sin_table[:, :half], gap, after], axis=1),
        jnp.concatenate([before, gap, sin_table[:, half:], after], axis=1),
    )


def turn_lanes(values, cos_table, lower_table, upper_table, sign):
    return (
        values * cos_table
        + sign * (pltpu.roll(values, LANES - ROPE // 2, 1) * lower_table)
        + sign * (pltpu.roll(values, ROPE // 2, 1) * upper_table)
    )


def swap(value, axis, distance):
    size = lax.axis_size(axis)
    return lax.ppermute(value, axis, [(i, i ^ distance) for i in range(size)])


def together(*arrays):
    count = len(arrays)
    return pl.pallas_call(
        lambda *refs: None,
        in_specs=[pl.BlockSpec(memory_space=pl.ANY)] * count,
        out_specs=[pl.BlockSpec(memory_space=pl.ANY)] * count,
        out_shape=[jax.ShapeDtypeStruct(a.shape, a.dtype) for a in arrays],
        input_output_aliases={i: i for i in range(count)},
        name="together",
    )(*arrays)


def in_turn(operands, order, move):
    operands = dict(operands)
    arrived = {}
    before = []
    for group in order:
        if before:
            both = together(*[operands[name] for name in group], *[arrived[name] for name in before])
            for name, array in zip(group, both[: len(group)]):
                operands[name] = array
            for name, array in zip(before, both[len(group) :]):
                arrived[name] = array
        for name in group:
            arrived[name] = move(name, operands[name])
        before = group
    return operands, arrived


def spread_ctx(own):
    first = swap(own, "ctx", 1)
    second = swap(own, "ctx", 2)
    return [own, first, second, swap(second, "ctx", 1)]


def exchange_ctx(chunks):
    return [chunks[0]] + [swap(chunks[k], "ctx", k) for k in range(1, len(chunks))]


def sum_ctx(parts):
    third = swap(parts[3].astype(BF16), "ctx", 1)
    far = (parts[2].astype(F32) + third.astype(F32)).astype(BF16)
    near = swap(parts[1].astype(BF16), "ctx", 1)
    return parts[0].astype(F32) + near.astype(F32) + swap(far, "ctx", 2).astype(F32)


def spread_tp(own):
    far = swap(own, "tp", 2)
    return [own, swap(own, "tp", 1), far, swap(far, "tp", 1)]


def fold_halves(keep, send):
    pair = (keep + swap(send, "tp", 1)).astype(BF16)
    mine = pair.astype(F32) + swap(pair, "tp", 2).astype(F32)
    return mine, swap(mine, "tp", 1)


def at_once(copies):
    for copy in copies:
        copy.start()
    for copy in copies:
        copy.wait()


def shard_place(where, index, n_ctx):
    return (where[0] ^ (index // n_ctx)) * n_ctx + (where[1] ^ (index % n_ctx))


def row_copies(where, pieces, first_row, rows, target, sems, first_sem, n_ctx):
    if len(pieces) == 1:
        return [pltpu.make_async_copy(pieces[0], target, sems.at[first_sem])]
    out = []
    for index, piece in enumerate(pieces):
        start = pl.multiple_of(shard_place(where, index, n_ctx) * rows, SUBLANES)
        out.append(
            pltpu.make_async_copy(
                piece.at[pl.ds(first_row, rows), :],
                target.at[pl.ds(start, rows), :],
                sems.at[first_sem + index],
            )
        )
    return out


def feature_start(where, place, width):
    return pl.multiple_of((where[2] ^ place) * width, LANES)


def feature_copies(where, pieces, target, row, rows, width, sems, first_sem):
    return [
        pltpu.make_async_copy(
            piece,
            target.at[pl.ds(row, rows), pl.ds(feature_start(where, place, width), width)],
            sems.at[first_sem + place],
        )
        for place, piece in enumerate(pieces)
    ]


def run_kernel(body, inputs, outputs, scratch, flops, moved, name, grid=None, exps=0, waits=()):
    count = len(inputs)
    inputs = list(inputs) + [(array, ANY) for array in waits]

    def used(*refs):
        body(*refs[:count], *refs[len(inputs) :])

    return pl.pallas_call(
        used,
        grid=grid if grid is not None else (),
        in_specs=[spec for _, spec in inputs],
        out_specs=[spec for _, spec in outputs],
        out_shape=[shape for shape, _ in outputs],
        scratch_shapes=scratch,
        compiler_params=pltpu.CompilerParams(vmem_limit_bytes=56 << 20),
        cost_estimate=pl.CostEstimate(flops=flops, bytes_accessed=moved, transcendentals=exps),
        name=name,
    )(*[array for array, _ in inputs])


VMEM = pl.BlockSpec(memory_space=pltpu.VMEM)
SMEM = pl.BlockSpec(memory_space=pltpu.SMEM)
ANY = pl.BlockSpec(memory_space=pl.ANY)


def shape(dims, dtype=BF16):
    return jax.ShapeDtypeStruct(dims, dtype)


def cut_hidden(where, gate, up, down, parts=1, waits=()):
    rows, total = gate.shape
    hidden = total // 4
    columns = round_up(3 * hidden, LANES)

    def body(where_ref, gate_ref, up_ref, down_ref, *rest):
        outs, stage = rest[:-1], rest[-1]
        blank = jnp.zeros((rows, columns - 3 * hidden), BF16)
        for place in range(4):
            units = slice(place * hidden, (place + 1) * hidden)
            stage[place] = jnp.concatenate(
                [gate_ref[:, units], up_ref[:, units], down_ref[:, units], blank], axis=1
            )
        for number, out in enumerate(outs):
            first = number // 4 * (rows // parts)
            out[...] = stage[where_ref[1] ^ (number % 4), first : first + rows // parts]

    return run_kernel(
        body,
        [(where, SMEM), (gate, VMEM), (up, VMEM), (down.T, VMEM)],
        [(shape((rows // parts, columns)), VMEM)] * (4 * parts),
        [pltpu.VMEM((4, rows, columns), BF16)],
        0,
        12 * rows * total,
        "cut_hidden",
        waits=waits,
    )


def join_hidden(where, pieces, hidden, waits=()):
    rows = pieces[0].shape[0]

    def body(where_ref, p0, p1, p2, p3, gate_ref, up_ref, down_ref, stage):
        for step, piece in enumerate((p0, p1, p2, p3)):
            stage[where_ref[1] ^ step] = piece[...]
        for first, out in ((0, gate_ref), (hidden, up_ref), (2 * hidden, down_ref)):
            out[...] = jnp.concatenate(
                [stage[place][:, first : first + hidden].astype(F32) for place in range(4)], axis=1
            )

    return run_kernel(
        body,
        [(where, SMEM)] + [(piece, VMEM) for piece in pieces],
        [
            (shape((rows, 4 * hidden), F32), VMEM),
            (shape((rows, 4 * hidden), F32), VMEM),
            (shape((rows, 4 * hidden), F32), VMEM),
        ],
        [pltpu.VMEM((4,) + pieces[0].shape, BF16)],
        0,
        80 * rows * hidden,
        "join_hidden",
        waits=waits,
    )


def latent_products(
    where, normed, pick, query_pieces, low_pieces, query_rows, low_rows, first_low, n_ctx, paired, waits=()
):
    rows, width = normed.shape
    half = rows // 2
    shared = query_pieces is low_pieces
    shards = len(query_pieces)
    arrays = list(query_pieces) if shared else list(query_pieces) + list(low_pieces)

    def body(where_ref, normed_ref, pick_ref, *rest):
        refs = rest[: len(arrays)]
        keep, send, joined, query_gain, latent_gain, low_in, total, sems = rest[len(arrays) :]
        query_refs = refs[: len(query_pieces)]
        low_refs = query_refs if shared else refs[len(query_pieces) :]
        copies = row_copies(
            where_ref, query_refs, 0, query_rows, joined.at[pl.ds(0, QRANK), :], sems, 0, n_ctx
        )
        copies += row_copies(
            where_ref, low_refs, first_low, low_rows, low_in, sems, len(query_refs), n_ctx
        )
        at_once(copies)
        joined[QRANK:, :] = product(pick_ref[...], low_in[...]).astype(BF16)
        if paired:
            first = LATENT + ROPE
            pieces = joined[first : first + SUBLANES, :LANES].astype(F32)
            query_gain[...] = jnp.concatenate(
                [pieces[i : i + 1, :query_rows] for i in range(shards)], axis=1
            )
            latent_gain[...] = jnp.concatenate(
                [pieces[i : i + 1, query_rows:] for i in range(shards)], axis=1
            )
            joined[first : first + SUBLANES, :] = jnp.zeros((SUBLANES, width), BF16)
        total[...] = times_transposed(normed_ref[...], joined[...])
        core = where_ref[3]
        keep[...] = total[pl.ds(pl.multiple_of(core * half, 8), half), :]
        send[...] = total[pl.ds(pl.multiple_of((1 - core) * half, 8), half), :]

    return run_kernel(
        body,
        [(where, SMEM), (normed, VMEM), (pick, VMEM)] + [(a, ANY) for a in arrays],
        [
            (shape((half, LAT_COLS), F32), VMEM),
            (shape((half, LAT_COLS), F32), VMEM),
            (shape((LAT_COLS, width)), VMEM),
            (shape((1, QRANK), F32), VMEM),
            (shape((1, KVRANK), F32), VMEM),
        ],
        [
            pltpu.VMEM((pick.shape[1], width), BF16),
            pltpu.VMEM((rows, LAT_COLS), F32),
            pltpu.SemaphoreType.DMA((len(query_pieces) + len(low_pieces),)),
        ],
        2 * rows * width * LAT_COLS,
        8 << 20,
        "latent_products",
        waits=waits,
    )


def latent_norms(where, mine, other, gain_query, gain_latent, tables, waits=()):
    half = mine.shape[0]
    rows = 2 * half

    def body(where_ref, mine_ref, other_ref, gq, gl, cos_t, lower_t, upper_t, latent, query_low, payload):
        core = where_ref[3]
        latent[pl.ds(pl.multiple_of(core * half, 8), half), :] = mine_ref[...]
        latent[pl.ds(pl.multiple_of((1 - core) * half, 8), half), :] = other_ref[...]
        query = latent[:, :QRANK]
        inverse = lax.rsqrt(jnp.mean(query * query, axis=1, keepdims=True) + EPSILON)
        query_low[...] = (query * inverse * gq[...]).astype(BF16)
        low = latent[:, QRANK:LATENT]
        inverse = lax.rsqrt(jnp.mean(low * low, axis=1, keepdims=True) + EPSILON)
        payload[:, :KVRANK] = (low * inverse * gl[...]).astype(BF16)
        rope = pltpu.roll(latent[:, LATENT:], NOPE, 1)
        payload[:, KVRANK:] = turn_lanes(rope, cos_t[...], lower_t[...], upper_t[...], 1.0).astype(BF16)

    return run_kernel(
        body,
        [(where, SMEM)]
        + [(a, VMEM) for a in (mine, other, gain_query, gain_latent) + tables],
        [
            (shape((rows, LAT_COLS), F32), VMEM),
            (shape((rows, QRANK)), VMEM),
            (shape((rows, KVRANK + LANES)), VMEM),
        ],
        [],
        20 * rows * LAT_COLS,
        4 << 20,
        "latent_norms",
        waits=waits,
    )


def masked_blocks(scores, place, rows, blocks):
    key_row = lax.broadcasted_iota(jnp.int32, (rows, rows), 0)
    query_column = lax.broadcasted_iota(jnp.int32, (rows, rows), 1)
    out = [jnp.where(key_row <= query_column, scores[:rows], NEGATIVE)]
    for block in range(1, blocks):
        seen = (place ^ block) < place
        out.append(jnp.where(seen, scores[block * rows : (block + 1) * rows], NEGATIVE))
    return out


def head_lanes(index):
    return pl.ds(pl.multiple_of(index * 2 * LANES, 2 * LANES), 2 * LANES)


def up_copies(where_ref, refs, wq, wkv, sems, n_ctx):
    if len(refs) == 3:
        return [
            pltpu.make_async_copy(refs[0], wq, sems.at[0]),
            pltpu.make_async_copy(refs[1], wkv, sems.at[1]),
        ]
    shards = len(refs) // 2
    query_rows = QRANK // shards
    low_rows = KVRANK // shards
    refs = refs[:shards]
    return row_copies(where_ref, refs, 0, query_rows, wq, sems, 0, n_ctx) + row_copies(
        where_ref, refs, query_rows, low_rows, wkv, sems, shards, n_ctx
    )


def out_copies(where_ref, refs, target, sems, first_sem, n_ctx):
    if len(refs) == 3:
        return [pltpu.make_async_copy(refs[2], target, sems.at[first_sem])]
    refs = refs[len(refs) // 2 :]
    return row_copies(where_ref, refs, 0, refs[0].shape[0], target, sems, first_sem, n_ctx)


def sequence_refs(source):
    return [piece for group in source for piece in group]


def sequence_shape(source):
    return (4 * len(source),) + source[0][0].shape


def sequence_copies(where, refs, target, rows, width, sems, first_sem):
    return [
        feature_copies(
            where, refs[at : at + 4], target, at // 4 * rows, rows, width, sems, first_sem + at
        )
        for at in range(0, len(refs), 4)
    ]


def hidden_copies(where, arrays, target, sems, first_sem, n_ctx, columns=None):
    cut = (lambda ref: ref) if columns is None else (lambda ref: ref.at[:, columns])
    if len(arrays) == 1:
        return [pltpu.make_async_copy(cut(arrays[0]), target, sems.at[first_sem])]
    rows = arrays[0].shape[0]
    parts = target.shape[0] // (rows * 2 * n_ctx)
    out = []
    for number, ref in enumerate(arrays):
        part, index = number // (2 * n_ctx), number % (2 * n_ctx)
        start = shard_place(where, index, n_ctx) * parts + part
        start = pl.multiple_of(start * rows, SUBLANES)
        out.append(
            pltpu.make_async_copy(
                cut(ref), target.at[pl.ds(start, rows), :], sems.at[first_sem + number]
            )
        )
    return out


def attention_forward(where, query_low, payloads, ups, tables, heads, n_ctx, waits=()):
    rows = query_low.shape[0]
    blocks = len(payloads)
    keys = blocks * rows
    pairs = heads // 2
    whole = lambda dims: pl.BlockSpec(dims, lambda i: (0, 0))
    column = lambda dims: pl.BlockSpec(dims, lambda i: (0, i))

    def body(where_ref, low_q, cos_t, lower_t, upper_t, *rest):
        sources = rest[:blocks]
        up_refs = rest[blocks : blocks + len(ups)]
        out, q_out, kv_out, lse_out, wq, wkv, tokens, sems = rest[blocks + len(ups) :]
        step = pl.program_id(0)

        @pl.when(step == 0)
        def _():
            copies = up_copies(where_ref, up_refs, wq, wkv, sems, n_ctx)
            first = len(copies)
            for block, source in enumerate(sources):
                copies.append(
                    pltpu.make_async_copy(
                        source, tokens.at[pl.ds(block * rows, rows), :], sems.at[first + block]
                    )
                )
            at_once(copies)

        key_lane = lax.broadcasted_iota(jnp.int32, (keys, LANES), 1)
        raw_pair = product(low_q[...], wq[:, head_lanes(step)])
        kv_pair = product(tokens[:, :KVRANK], wkv[:, head_lanes(step)]).astype(BF16)
        rope_key = tokens[:, KVRANK:]
        kv_out[...] = kv_pair
        outs = []
        for head in range(2):
            lanes = slice(head * LANES, (head + 1) * LANES)
            query = turn_lanes(
                raw_pair[:, lanes], cos_t[...], lower_t[...], upper_t[...], 1.0
            ).astype(BF16)
            pair = kv_pair[:, lanes]
            key = jnp.where(key_lane < NOPE, pair, rope_key)
            q_out[:, lanes] = query
            scores = times_transposed(key, query) * SCORE
            masked = masked_blocks(scores, where_ref[1], rows, blocks)
            top = functools.reduce(
                jnp.maximum, [jnp.max(part, axis=0, keepdims=True) for part in masked]
            )
            powers = [jnp.exp(part - top) for part in masked]
            total = sum(jnp.sum(part, axis=0, keepdims=True) for part in powers)
            prob = jnp.concatenate([part.astype(BF16) for part in powers], axis=0)
            mixed = transposed_times(pair, prob) / total
            outs.append(jnp.transpose(mixed))
            lse_out[0, head : head + 1, :] = top + jnp.log(total)
        lane = lax.broadcasted_iota(jnp.int32, (rows, LANES), 1)
        out[...] = jnp.where(lane < VDIM, pltpu.roll(outs[0], VDIM, 1), outs[1]).astype(BF16)

    return run_kernel(
        body,
        [(where, SMEM), (query_low, whole(query_low.shape))]
        + [(table, whole(table.shape)) for table in tables]
        + [(a, ANY) for a in list(payloads) + list(ups)],
        [
            (shape((rows, pairs * LANES)), column((rows, LANES))),
            (shape((rows, heads * LANES)), column((rows, 2 * LANES))),
            (shape((keys, heads * LANES)), column((keys, 2 * LANES))),
            (shape((pairs, 8, rows), F32), pl.BlockSpec((1, 8, rows), lambda i: (i, 0, 0))),
        ],
        [
            pltpu.VMEM((QRANK, heads * LANES), BF16),
            pltpu.VMEM((KVRANK, heads * LANES), BF16),
            pltpu.VMEM((keys, KVRANK + LANES), BF16),
            pltpu.SemaphoreType.DMA((64 + blocks,)),
        ],
        2 * heads * rows * (QRANK + 2 * keys) * LANES + 2 * heads * keys * KVRANK * LANES,
        12 << 20,
        "attention_forward",
        grid=(pairs,),
        exps=heads * rows * keys,
        waits=waits,
    )


def attention_backward(where, queries, pairs_low, lse, payloads, ups, branch, tables, n_ctx, waits=()):
    rows, q_lanes = queries.shape
    heads = q_lanes // LANES
    pairs = heads // 2
    blocks = len(payloads)
    keys = blocks * rows
    width = branch[0].shape[1]
    full_width = 4 * width
    inner = heads * VDIM
    whole = lambda dims: pl.BlockSpec(dims, lambda i: (0, 0))
    column = lambda dims: pl.BlockSpec(dims, lambda i: (0, i))
    moved = list(payloads) + list(ups) + list(branch)

    def body(where_ref, q_in, kv_in, lse_in, cos_t, lower_t, upper_t, *rest):
        refs = rest[: len(moved)]
        (dq_out, dkv_out, query_sum, kv_keep, kv_1, kv_2, kv_3) = rest[len(moved) : len(moved) + 7]
        wq, wkv, rope_key, wo, grad_in, dout, kv_sum, sems = rest[len(moved) + 7 :]
        step = pl.program_id(0)
        place = where_ref[1]

        @pl.when(step == 0)
        def _():
            at = 0
            sources, at = refs[at : at + blocks], at + blocks
            up_refs, at = refs[at : at + len(ups)], at + len(ups)
            branch_refs = refs[at : at + 4]
            copies = up_copies(where_ref, up_refs, wq, wkv, sems, n_ctx)
            for block, source in enumerate(sources):
                copies.append(
                    pltpu.make_async_copy(
                        source.at[:, pl.ds(KVRANK, LANES)],
                        rope_key.at[pl.ds(block * rows, rows), :],
                        sems.at[len(copies)],
                    )
                )
            copies += feature_copies(
                where_ref, branch_refs, grad_in, 0, rows, width, sems, len(copies)
            )
            copies += out_copies(where_ref, up_refs, wo, sems, len(copies), n_ctx)
            at_once(copies)
            dout[...] = product(grad_in[...], wo[...]).astype(BF16).astype(F32)
            query_sum[...] = jnp.zeros_like(query_sum)
            kv_sum[...] = jnp.zeros_like(kv_sum)

        key_lane = lax.broadcasted_iota(jnp.int32, (keys, LANES), 1)
        lane = lax.broadcasted_iota(jnp.int32, (rows, LANES), 1)
        both = dout[:, pl.ds(pl.multiple_of(step * LANES, LANES), LANES)]
        dkr = jnp.zeros((keys, LANES), F32)
        dq_parts = []
        dkv_parts = []
        for head in range(2):
            lanes = slice(head * LANES, (head + 1) * LANES)
            query = q_in[:, lanes]
            pair = kv_in[:, lanes]
            key = jnp.where(key_lane < NOPE, pair, rope_key[...])
            upper = pltpu.roll(both, VDIM, 1) if head == 0 else both
            out_grad = jnp.where(lane >= NOPE, upper, 0.0).astype(BF16)
            scores = times_transposed(key, query) * SCORE
            top = lse_in[0, head : head + 1, :]
            masked = masked_blocks(scores, place, rows, blocks)
            prob = jnp.concatenate([jnp.exp(part - top) for part in masked], axis=0)
            prob_grad = times_transposed(pair, out_grad)
            weighted = prob * prob_grad
            delta = jnp.sum(weighted, axis=0, keepdims=True)
            score_grad = (weighted - prob * delta).astype(BF16)
            key_grad = product(score_grad, query) * SCORE
            value_grad = product(prob.astype(BF16), out_grad)
            dkv_parts.append(jnp.where(key_lane < NOPE, key_grad, value_grad).astype(BF16))
            dkr = dkr + key_grad
            query_grad = jnp.transpose(transposed_times(key, score_grad)) * SCORE
            dq_parts.append(
                turn_lanes(query_grad, cos_t[...], lower_t[...], upper_t[...], -1.0).astype(BF16)
            )
        dq_pair = jnp.concatenate(dq_parts, axis=1)
        dkv_pair = jnp.concatenate(dkv_parts, axis=1)
        dq_out[...] = dq_pair
        dkv_out[...] = dkv_pair
        query_sum[...] += times_transposed(dq_pair, wq[:, head_lanes(step)])
        kv_sum[:, :KVRANK] += times_transposed(dkv_pair, wkv[:, head_lanes(step)])
        kv_sum[:, KVRANK:] += jnp.where(key_lane >= NOPE, dkr, 0.0)

        @pl.when(step == pairs - 1)
        def _():
            kv_keep[...] = kv_sum[:rows]
            for block, out in ((1, kv_1), (2, kv_2), (3, kv_3)):
                out[...] = kv_sum[block * rows : (block + 1) * rows].astype(BF16)

    return run_kernel(
        body,
        [
            (where, SMEM),
            (queries, column((rows, 2 * LANES))),
            (pairs_low, column((keys, 2 * LANES))),
            (lse, pl.BlockSpec((1, 8, rows), lambda i: (i, 0, 0))),
        ]
        + [(table, whole(table.shape)) for table in tables]
        + [(a, ANY) for a in moved],
        [
            (shape((rows, heads * LANES)), column((rows, 2 * LANES))),
            (shape((keys, heads * LANES)), column((keys, 2 * LANES))),
            (shape((rows, QRANK), F32), whole((rows, QRANK))),
            (shape((rows, KVRANK + LANES), F32), whole((rows, KVRANK + LANES))),
        ]
        + [(shape((rows, KVRANK + LANES)), whole((rows, KVRANK + LANES)))] * 3,
        [
            pltpu.VMEM((QRANK, heads * LANES), BF16),
            pltpu.VMEM((KVRANK, heads * LANES), BF16),
            pltpu.VMEM((keys, LANES), BF16),
            pltpu.VMEM((full_width, inner), BF16),
            pltpu.VMEM((rows, full_width), BF16),
            pltpu.VMEM((rows, inner), F32),
            pltpu.VMEM((keys, KVRANK + LANES), F32),
            pltpu.SemaphoreType.DMA((128 + blocks,)),
        ],
        10 * heads * rows * keys * LANES,
        24 << 20,
        "attention_backward",
        grid=(pairs,),
        exps=heads * rows * keys,
        waits=waits,
    )


def output_products(where, attended, ups, full_width, n_ctx, waits=()):
    rows, inner = attended.shape
    count = len(ups)
    width = full_width // 4

    def body(where_ref, attended_ref, *rest):
        refs = rest[:count]
        keep, send, weight, sems = rest[count:]
        at_once(out_copies(where_ref, refs, weight, sems, 0, n_ctx))
        for place in range(4):
            block = weight[pl.ds(feature_start(where_ref, place, width), width), :]
            part = times_transposed(attended_ref[...], block)
            if place % 2 == 0:
                keep[place // 2] = part
            else:
                send[place // 2] = part.astype(BF16)

    return run_kernel(
        body,
        [(where, SMEM), (attended, VMEM)] + [(a, ANY) for a in ups],
        [(shape((2, rows, width), F32), VMEM), (shape((2, rows, width)), VMEM)],
        [pltpu.VMEM((full_width, inner), BF16), pltpu.SemaphoreType.DMA((64,))],
        2 * rows * inner * full_width,
        6 << 20,
        "output_products",
        waits=waits,
    )


def feed_forward(where, tokens, branches, weights, gains, hidden, n_ctx):
    count, rows, width = sequence_shape(tokens)
    blocks = count // 4
    full_width = 4 * width
    columns = weights[0].shape[-1]
    upper_end = round_up(2 * hidden, LANES)
    lower_start = 2 * hidden // LANES * LANES
    shift = 2 * hidden - lower_start
    lower_cols = columns - lower_start
    total = blocks * rows
    token_list, branch_list = sequence_refs(tokens), sequence_refs(branches)
    flat = len(token_list) + len(branch_list)
    moved = token_list + branch_list + list(gains) + list(weights)

    def body(where_ref, *rest):
        refs = rest[: len(moved)]
        pairs_out, active_out, keep, send, inverse_out = rest[len(moved) : len(moved) + 5]
        normed, branch, weight, gain, sems = rest[len(moved) + 5 :]
        first = 2 * count
        weight_copies = feature_copies(
            where_ref, refs[flat : flat + 4], gain, 0, gain.shape[0], width, sems, first
        ) + hidden_copies(where_ref, refs[flat + 4 :], weight, sems, first + 4, n_ctx)
        token_copies = [
            first_list + second_list
            for first_list, second_list in zip(
                sequence_copies(
                    where_ref, refs[: len(token_list)], normed, rows, width, sems, 0
                ),
                sequence_copies(
                    where_ref, refs[len(token_list) : flat], branch, rows, width, sems, count
                ),
            )
        ]
        for copy in weight_copies + sum(token_copies, []):
            copy.start()
        for copy in weight_copies:
            copy.wait()

        def hidden_block(block, carry):
            for number, copies in enumerate(token_copies):

                @pl.when(block == number)
                def _():
                    for copy in copies:
                        copy.wait()

            here = pl.ds(pl.multiple_of(block * rows, rows), rows)
            source = normed[here, :].astype(F32) / gain[:1, :]
            inverse = lax.rsqrt(jnp.mean(source * source, axis=1, keepdims=True) + EPSILON)

            @pl.when(block == 0)
            def _():
                inverse_out[...] = jnp.broadcast_to(inverse, inverse_out.shape)

            both = product(normed[here, :], weight[:, :upper_end]) * inverse
            lower = product(branch[here, :], weight[:, lower_start:])
            gate = both[:, :hidden]
            upper = both[:, hidden : 2 * hidden]
            grad = lower[:, shift : shift + hidden]
            scaled = grad * inverse
            sigmoid = 1.0 / (1.0 + jnp.exp(-gate))
            active = gate * sigmoid
            pairs_out[here, :] = jnp.concatenate(
                [
                    scaled * upper * sigmoid * (1.0 + gate * (1.0 - sigmoid)),
                    scaled * active,
                    jnp.zeros((rows, upper_end - 2 * hidden), F32),
                ],
                axis=1,
            ).astype(BF16)
            active_out[here, :] = jnp.concatenate(
                [
                    jnp.zeros((rows, shift), F32),
                    active * upper,
                    jnp.zeros((rows, lower_cols - shift - hidden), F32),
                ],
                axis=1,
            ).astype(BF16)
            return carry

        lax.fori_loop(0, blocks, hidden_block, 0)
        for place in range(4):
            block = weight[pl.ds(feature_start(where_ref, place, width), width), :upper_end]
            part = times_transposed(pairs_out[...], block).astype(BF16)
            (send if place % 2 else keep)[place // 2] = part

    return run_kernel(
        body,
        [(where, SMEM)] + [(a, ANY) for a in moved],
        [
            (shape((total, upper_end)), VMEM),
            (shape((total, lower_cols)), VMEM),
            (shape((2, total, width)), VMEM),
            (shape((2, total, width)), VMEM),
            (shape((rows, LANES), F32), VMEM),
        ],
        [
            pltpu.VMEM((total, full_width), BF16),
            pltpu.VMEM((total, full_width), BF16),
            pltpu.VMEM((full_width, columns), BF16),
            pltpu.VMEM(gains[0].shape[:1] + (full_width,), F32),
            pltpu.SemaphoreType.DMA((2 * count + 4 + full_width // SUBLANES,)),
        ],
        10 * total * full_width * hidden,
        28 << 20,
        "feed_forward",
        exps=total * hidden,
    )


def feed_forward_result(where, active, weights, hidden, n_ctx, waits=()):
    total, lower_cols = active.shape
    columns = weights[0].shape[1]
    full_width = sum(a.shape[0] for a in weights)
    width = full_width // 4
    count = len(weights)

    def body(where_ref, active_ref, *rest):
        refs = rest[:count]
        outs = rest[count:-2]
        weight, sems = rest[-2:]
        lower = pl.ds(columns - lower_cols, lower_cols)
        at_once(hidden_copies(where_ref, refs, weight, sems, 0, n_ctx, columns=lower))
        for place in range(4):
            block = weight[pl.ds(feature_start(where_ref, place, width), width), :]
            part = times_transposed(active_ref[...], block).astype(BF16)
            outs[place % 2][place // 2] = part

    return run_kernel(
        body,
        [(where, SMEM), (active, VMEM)] + [(a, ANY) for a in weights],
        [(shape((2, total, width)), VMEM)] * 2,
        [
            pltpu.VMEM((full_width, lower_cols), BF16),
            pltpu.SemaphoreType.DMA((full_width // SUBLANES,)),
        ],
        2 * total * full_width * hidden,
        10 << 20,
        "feed_forward_result",
        waits=waits,
    )


def feed_forward_grads(
    where, tokens, branches, pairs_grad, active, hidden, columns, shards, n_ctx, distance, waits=()
):
    count, rows, width = sequence_shape(tokens)
    token_list, branch_list = sequence_refs(tokens), sequence_refs(branches)
    total = count // 4 * rows
    upper_end = pairs_grad.shape[1]
    lower_cols = active.shape[1]
    lower_start = columns - lower_cols
    shard_rows = 4 * width // shards

    def gradient(normed, branch, pairs_ref, active_ref):
        first = transposed_times(normed, pairs_ref[...])
        second = transposed_times(branch, active_ref[...])
        middle = first[:, lower_start:] + second[:, : upper_end - lower_start]
        return jnp.concatenate(
            [first[:, :lower_start], middle, second[:, upper_end - lower_start :]], axis=1
        ).astype(BF16)

    def body(where_ref, pairs_ref, active_ref, *rest):
        token_refs, rest = rest[: len(token_list)], rest[len(token_list) :]
        branch_refs, rest = rest[: len(branch_list)], rest[len(branch_list) :]
        outs = rest[:-4]
        normed, branch, stage, sems = rest[-4:]
        copies = sequence_copies(where_ref, token_refs, normed, rows, width, sems, 0)
        copies += sequence_copies(where_ref, branch_refs, branch, rows, width, sems, count)
        at_once(sum(copies, []))
        if distance is None:
            for place in range(4):
                here = slice(place * width, (place + 1) * width)
                outs[0][here, :] = gradient(normed[:, here], branch[:, here], pairs_ref, active_ref)
            return
        for number in range(n_ctx // 2):
            place = owner_blocks(where_ref, distance * (n_ctx // 2) + number, n_ctx)
            here = pl.ds(pl.multiple_of(place * width, LANES), width)
            stage[...] = gradient(normed[:, here], branch[:, here], pairs_ref, active_ref)
            for low in range(2):
                start = pl.multiple_of((low ^ (where_ref[1] % 2)) * shard_rows, SUBLANES)
                outs[2 * number + low][...] = stage[pl.ds(start, shard_rows), :]

    if distance is None:
        outputs = [(shape((4 * width, columns)), VMEM)]
    else:
        outputs = [(shape((shard_rows, columns)), VMEM)] * n_ctx
    return run_kernel(
        body,
        [(where, SMEM), (pairs_grad, VMEM), (active, VMEM)]
        + [(a, ANY) for a in token_list + branch_list],
        outputs,
        [
            pltpu.VMEM((total, 4 * width), BF16),
            pltpu.VMEM((total, 4 * width), BF16),
            pltpu.VMEM((width, columns), BF16),
            pltpu.SemaphoreType.DMA((2 * count,)),
        ],
        6 * total * 4 * width * hidden // 2,
        18 << 20,
        "feed_forward_grads",
        waits=waits,
    )


def owner_blocks(where_ref, part, n_ctx):
    per_row = n_ctx // 2
    return (where_ref[0] ^ (part // per_row)) * per_row + ((where_ref[1] // 2) ^ (part % per_row))


def output_grads(where, attended, branch, shards, n_ctx, paired, waits=()):
    rows, inner = attended.shape
    width = branch[0].shape[1]
    shard_rows = 4 * width // shards

    def body(where_ref, attended_ref, b0, b1, b2, b3, *rest):
        outs = rest[:-3]
        grad_in, stage, sems = rest[-3:]
        at_once(feature_copies(where_ref, (b0, b1, b2, b3), grad_in, 0, rows, width, sems, 0))
        for part in range(4):
            place = owner_blocks(where_ref, part, n_ctx) if paired else part
            here = pl.ds(pl.multiple_of(place * width, LANES), width)
            stage[...] = transposed_times(grad_in[:, here], attended_ref[...]).astype(BF16)
            if not paired:
                outs[0][part * width : (part + 1) * width, :] = stage[...]
                continue
            for low in range(2):
                start = pl.multiple_of((low ^ (where_ref[1] % 2)) * shard_rows, SUBLANES)
                outs[2 * part + low][...] = stage[pl.ds(start, shard_rows), :]

    if paired:
        outputs = [(shape((shard_rows, inner)), VMEM)] * shards
    else:
        outputs = [(shape((4 * width, inner)), VMEM)]
    return run_kernel(
        body,
        [(where, SMEM), (attended, VMEM)] + [(a, ANY) for a in branch],
        outputs,
        [
            pltpu.VMEM((rows, 4 * width), BF16),
            pltpu.VMEM((width, inner), BF16),
            pltpu.SemaphoreType.DMA((4,)),
        ],
        2 * rows * inner * 4 * width,
        6 << 20,
        "output_grads",
        waits=waits,
    )


def up_grads(where, query_low, query_grad, payloads, pair_grad, shards, n_ctx, paired, waits=()):
    rows = query_low.shape[0]
    blocks = len(payloads)
    lanes = query_grad.shape[1]
    query_rows = QRANK // shards
    low_rows = KVRANK // shards

    def body(where_ref, low_q, dq, dkv, *rest):
        sources = rest[:blocks]
        rest = rest[blocks:]
        outs = rest[:-4]
        tokens, stage_q, stage_kv, sems = rest[-4:]
        at_once(
            [
                pltpu.make_async_copy(
                    source.at[:, pl.ds(0, KVRANK)],
                    tokens.at[pl.ds(block * rows, rows), :],
                    sems.at[block],
                )
                for block, source in enumerate(sources)
            ]
        )
        grad_q = transposed_times(low_q[...], dq[...]).astype(BF16)
        grad_kv = transposed_times(tokens[...], dkv[...]).astype(BF16)
        if not paired:
            outs[0][...] = grad_q
            outs[1][...] = grad_kv
            return
        stage_q[...] = grad_q
        stage_kv[...] = grad_kv
        for index, out in enumerate(outs):
            place = shard_place(where_ref, index, n_ctx)
            out[:query_rows, :] = stage_q[
                pl.ds(pl.multiple_of(place * query_rows, SUBLANES), query_rows), :
            ]
            out[query_rows:, :] = stage_kv[
                pl.ds(pl.multiple_of(place * low_rows, SUBLANES), low_rows), :
            ]

    if paired:
        outputs = [(shape((query_rows + low_rows, lanes)), VMEM)] * shards
    else:
        outputs = [(shape((QRANK, lanes)), VMEM), (shape((KVRANK, lanes)), VMEM)]
    return run_kernel(
        body,
        [(where, SMEM), (query_low, VMEM), (query_grad, VMEM), (pair_grad, VMEM)]
        + [(a, ANY) for a in payloads],
        outputs,
        [
            pltpu.VMEM((blocks * rows, KVRANK), BF16),
            pltpu.VMEM((QRANK, lanes), BF16),
            pltpu.VMEM((KVRANK, lanes), BF16),
            pltpu.SemaphoreType.DMA((blocks,)),
        ],
        2 * lanes * (rows * QRANK + blocks * rows * KVRANK),
        10 << 20,
        "up_grads",
        waits=waits,
    )


def input_backward(
    where,
    mine,
    other,
    latent,
    gain_query,
    gain_latent,
    tables,
    normed,
    joined,
    activations,
    inverse_one,
    gain_one,
    middle_grad,
    pick,
    query_rows,
    low_rows,
    shards,
    n_ctx,
    paired,
    waits=(),
):
    half = mine.shape[0]
    rows, width = normed.shape
    full_width = 4 * width
    low_in = pick.shape[1]

    def body(
        where_ref, mine_ref, other_ref, latent_ref, gq, gl, cos_t, lower_t, upper_t, normed_ref,
        joined_ref, act_ref, inverse_ref, gain_ref, middle_ref, pick_ref, input_out, query_gain_out,
        latent_gain_out, gain_out, *rest
    ):
        outs = rest[:-3]
        sums, stage_q, stage_low = rest[-3:]
        core = where_ref[3]
        sums[pl.ds(pl.multiple_of(core * half, 8), half), :] = mine_ref[...]
        sums[pl.ds(pl.multiple_of((1 - core) * half, 8), half), :] = other_ref[...]
        parts = []
        for first, last, gain, out in (
            (0, QRANK, gq, query_gain_out),
            (QRANK, LATENT, gl, latent_gain_out),
        ):
            source = latent_ref[:, first:last]
            grad = sums[:, first:last]
            inverse = lax.rsqrt(jnp.mean(source * source, axis=1, keepdims=True) + EPSILON)
            out[...] = jnp.sum(grad * source * inverse, axis=0, keepdims=True)
            scaled = grad * gain[...]
            inner = jnp.mean(scaled * source, axis=1, keepdims=True)
            parts.append(inverse * scaled - source * (inverse * inverse * inverse * inner))
        rope = turn_lanes(sums[:, LATENT:], cos_t[...], lower_t[...], upper_t[...], -1.0)
        parts.append(pltpu.roll(rope, LANES - NOPE, 1))
        latent_grad = jnp.concatenate(parts, axis=1)
        low = latent_grad.astype(BF16)
        down_grad = transposed_times(low, normed_ref[...]).astype(BF16)
        if paired:
            stage_q[...] = down_grad[:QRANK]
            gains = [
                jnp.concatenate(
                    [
                        query_gain_out[:, i * query_rows : (i + 1) * query_rows],
                        latent_gain_out[:, i * KVRANK // shards : (i + 1) * KVRANK // shards],
                        jnp.zeros((1, width - LANES), F32),
                    ],
                    axis=1,
                )
                for i in range(shards)
            ]
            first = LATENT + ROPE - QRANK
            low_part = jnp.concatenate(
                [
                    down_grad[QRANK : LATENT + ROPE].astype(F32),
                    jnp.concatenate(gains, axis=0),
                    jnp.zeros((LOW_ROWS - first - shards, width), F32),
                ],
                axis=0,
            ).astype(BF16)
            stage_low[...] = transposed_times(pick_ref[...], low_part).astype(BF16)
            for index, out in enumerate(outs):
                place = shard_place(where_ref, index, n_ctx)
                out[:query_rows, :] = stage_q[
                    pl.ds(pl.multiple_of(place * query_rows, SUBLANES), query_rows), :
                ]
                out[query_rows:, :] = stage_low[
                    pl.ds(pl.multiple_of(place * low_rows, SUBLANES), low_rows), :
                ]
        else:
            outs[0][...] = down_grad
        row_inner = jnp.sum(latent_grad * latent_ref[...], axis=1, keepdims=True)
        normed_grad = product(low, joined_ref[...])
        source = act_ref[...].astype(F32)
        inverse = inverse_ref[...]
        gain_out[...] = jnp.sum(normed_grad * source * inverse, axis=0, keepdims=True)
        input_out[...] = (
            middle_ref[...]
            + inverse * (normed_grad * gain_ref[...])
            - source * (inverse * inverse * row_inner / full_width)
        )

    if paired:
        outputs = [(shape((query_rows + low_rows, width)), VMEM)] * shards
    else:
        outputs = [(shape((LAT_COLS, width)), VMEM)]
    arrays = (mine, other, latent, gain_query, gain_latent) + tables
    arrays += (normed, joined, activations, inverse_one, gain_one, middle_grad, pick)
    return run_kernel(
        body,
        [(where, SMEM)] + [(a, VMEM) for a in arrays],
        [
            (shape((rows, width), F32), VMEM),
            (shape((1, QRANK), F32), VMEM),
            (shape((1, KVRANK), F32), VMEM),
            (shape((1, width), F32), VMEM),
        ]
        + outputs,
        [
            pltpu.VMEM((rows, LAT_COLS), F32),
            pltpu.VMEM((QRANK, width), BF16),
            pltpu.VMEM((low_in, width), BF16),
        ],
        4 * rows * width * LAT_COLS,
        12 << 20,
        "input_backward",
        waits=waits,
    )


def pick_matrix(columns, rows_each, valid):
    matrix = np.zeros((LOW_ROWS, columns), np.float32)
    for row in range(KVRANK + ROPE):
        matrix[row, row // valid * rows_each + row % valid] = 1.0
    for shard in range(columns // rows_each if rows_each > valid else 0):
        matrix[KVRANK + ROPE + shard, shard * rows_each + valid] = 1.0
    return jnp.asarray(matrix, BF16)


def per_device(
    activations,
    attn_gain,
    query_down,
    latent_down,
    query_gain,
    latent_gain,
    query_up,
    latent_up,
    attn_output,
    ffn_gain,
    ffn_gate,
    ffn_up,
    ffn_down,
    out_grad,
):
    n_fsdp = lax.axis_size("fsdp")
    n_ctx = lax.axis_size("ctx")
    n_tp = lax.axis_size("tp")
    shards = n_fsdp * n_ctx
    paired = n_fsdp == 2 and shards == 2 * n_tp
    rows, width = activations.shape
    full_width = width * n_tp
    fsdp_index = lax.axis_index("fsdp").astype(jnp.int32)
    ctx_index = lax.axis_index("ctx").astype(jnp.int32)
    tp_index = lax.axis_index("tp").astype(jnp.int32)
    shard_index = fsdp_index * n_ctx + ctx_index
    where = jnp.stack([fsdp_index, ctx_index, tp_index, tp_index % 2])
    local_heads = query_up.shape[1] // (NOPE + ROPE)
    hidden = ffn_gate.shape[1] // n_ctx
    columns = round_up(3 * hidden, LANES)
    q_shard = query_down.shape[1]
    low_shard = latent_down.shape[1]
    both_axes = ("fsdp", "ctx")

    def spread_shards(own):
        pieces = spread_ctx(own)
        return pieces + [swap(piece, "fsdp", 1) for piece in pieces]

    def fold_shards(parts):
        return [
            (parts[k].astype(F32) + swap(parts[n_ctx + k], "fsdp", 1).astype(F32)).astype(BF16)
            for k in range(n_ctx)
        ]

    def gather_rows(value):
        return lax.all_gather(value, both_axes, axis=0, tiled=True)

    def scatter_rows(value):
        return lax.psum_scatter(value, both_axes, scatter_dimension=0, tiled=True).astype(F32)

    def spread_sequence(own):
        return [spread_tp(block) for block in spread_ctx(own)]

    inputs = activations.astype(F32)
    gain_one = attn_gain.astype(F32)
    row_sums = lax.psum(jnp.sum(inputs * inputs, axis=1), "tp")
    inverse_one = lax.rsqrt(row_sums / full_width + EPSILON)
    gain_two = ffn_gain.astype(F32)
    gains_two = spread_tp(jnp.broadcast_to(gain_two[None, :], (8, width)))
    normed_low = (inputs * inverse_one[:, None] * gain_one).astype(BF16)

    query_pad = jnp.pad(
        query_up.reshape(query_up.shape[0], local_heads, NOPE + ROPE),
        ((0, 0), (0, 0), (0, LANES - NOPE - ROPE)),
    ).reshape(query_up.shape[0], local_heads * LANES)
    if paired:
        low_rows = round_up(low_shard, SUBLANES)
        pick = pick_matrix(shards * low_rows, low_rows, low_shard)
        down_own = jnp.concatenate(
            [
                query_down.T,
                latent_down.T,
                jnp.pad(
                    jnp.concatenate([query_gain, latent_gain])[None, :],
                    ((0, low_rows - low_shard - 1), (0, width - LANES)),
                ),
            ]
        )
        query_pieces = low_pieces = spread_shards(down_own)
        first_low = q_shard
        ups = spread_shards(jnp.concatenate([query_pad, latent_up])) + spread_shards(attn_output.T)
    else:
        low_rows = low_shard
        pick = pick_matrix(LOW_ROWS, KVRANK + ROPE, KVRANK + ROPE)
        query_pieces = [gather_rows(query_down.T)]
        low_pieces = [
            jnp.pad(gather_rows(latent_down.T), ((0, LOW_ROWS - KVRANK - ROPE), (0, 0)))
        ]
        first_low = 0
        ups = [gather_rows(query_pad), gather_rows(latent_up), gather_rows(attn_output.T)]

    parts = 2 if paired else 1
    chunks = cut_hidden(where, ffn_gate, ffn_up, ffn_down, parts=parts)
    if paired:
        sent = {(part, k): chunks[n_ctx * part + k] for part in range(parts) for k in range(1, n_ctx)}
        order = [[(part, k) for k in group] for part in range(parts) for group in ((2, 1), (3,))]
        _, got = in_turn(sent, order, lambda key, value: swap(value, "ctx", key[1]))
        got.update({(part, 0): chunks[n_ctx * part] for part in range(parts)})
        order = [[(part, 0)] for part in range(parts)]
        order += [[(part, k)] for part in range(parts) for k in range(1, n_ctx)]
        got, crossed = in_turn(got, order, lambda key, value: swap(value, "fsdp", 1))
        weights = []
        for part in range(parts):
            weights += [got[part, k] for k in range(n_ctx)]
            weights += [crossed[part, k] for k in range(n_ctx)]
    else:
        stack = jnp.stack(exchange_ctx(chunks))
        stack = jnp.stack(
            [
                lax.dynamic_index_in_dim(stack, ctx_index ^ k, 0, keepdims=False)
                for k in range(n_ctx)
            ]
        )
        weights = [lax.all_gather(stack, "fsdp", axis=0).reshape(full_width, columns)]

    upstream = out_grad.astype(F32)
    branches = spread_sequence((RESID * upstream).astype(BF16))

    keep, send, joined, gain_query, gain_latent = latent_products(
        where,
        normed_low,
        pick,
        query_pieces,
        low_pieces,
        q_shard,
        low_rows,
        first_low,
        n_ctx,
        paired,
    )
    if not paired:
        gains = jnp.zeros((QRANK + KVRANK,), F32)
        gains = lax.dynamic_update_slice(
            gains, query_gain.astype(F32), (shard_index * query_gain.shape[0],)
        )
        gains = lax.dynamic_update_slice(
            gains, latent_gain.astype(F32), (QRANK + shard_index * latent_gain.shape[0],)
        )
        gains = lax.psum(gains, both_axes)
        gain_query = gains[None, :QRANK]
        gain_latent = gains[None, QRANK:]
    mine, other = fold_halves(keep, send)
    query_pos = ctx_index * rows + jnp.arange(rows, dtype=jnp.int32)
    tables = lane_tables(*rotary_tables(query_pos.astype(F32)))
    latent, query_low, payload = latent_norms(where, mine, other, gain_query, gain_latent, tables)
    payloads = spread_ctx(payload)

    attended, queries_low, pairs_low, lse = attention_forward(
        where, query_low, payloads, ups, tables, local_heads, n_ctx
    )

    def fold_tp(keep, send):
        got = swap(send, "tp", 1)
        far = (keep[1].astype(F32) + got[1].astype(F32)).astype(BF16)
        near = keep[0].astype(F32) + got[0].astype(F32)
        return near + swap(far, "tp", 2).astype(F32)

    keep, send = output_products(where, attended, ups, full_width, n_ctx)
    middle = inputs + RESID * fold_tp(keep, send)

    tokens = spread_sequence((middle * gain_two).astype(BF16))
    pairs_grad, active, keep, send, inverse_two = feed_forward(
        where, tokens, branches, weights, gains_two, hidden, n_ctx
    )
    inverse_two = inverse_two[:, :1]

    def fold_sequence(keep, send):
        got = swap(send, "tp", 1)
        totals = []
        for block in reversed(range(n_ctx)):
            here = slice(block * rows, (block + 1) * rows)
            far = (keep[1, here].astype(F32) + got[1, here].astype(F32)).astype(BF16)
            near = keep[0, here].astype(F32) + got[0, here].astype(F32)
            totals.append(near + swap(far, "tp", 2).astype(F32))
        return sum_ctx(totals[::-1])

    second_grad = fold_sequence(keep, send)
    scaled_two = second_grad * gain_two
    grad_gain_two = jnp.sum(second_grad * middle, axis=0)
    inner_two = lax.psum(jnp.sum(scaled_two * middle, axis=1), "tp") / full_width
    middle_grad = upstream + scaled_two - middle * (inverse_two * inverse_two * inner_two[:, None])
    branch = spread_tp((RESID * middle_grad).astype(BF16))

    result = middle + RESID * fold_sequence(
        *feed_forward_result(where, active, weights, hidden, n_ctx)
    )
    grads = functools.partial(
        feed_forward_grads, where, tokens, branches, pairs_grad, active, hidden, columns, shards, n_ctx
    )
    if paired:
        sent, kept = grads(1), grads(0)
        moved = [swap(sent[k], "fsdp", 1) for k in reversed(range(n_ctx))][::-1]
        sums = [
            (kept[k].astype(F32) + moved[k].astype(F32)).astype(BF16) for k in range(n_ctx)
        ]
    else:
        total = grads(None)[0].reshape(n_fsdp, n_ctx, full_width // shards, columns)
        total = lax.psum_scatter(total, "fsdp", scatter_dimension=0, tiled=False)
        sums = [
            lax.dynamic_index_in_dim(total, ctx_index ^ k, 0, keepdims=False) for k in range(n_ctx)
        ]
    hidden_sums = exchange_ctx(sums)

    query_grad, pair_grad, query_sum, kv_keep, kv_1, kv_2, kv_3 = attention_backward(
        where, queries_low, pairs_low, lse, payloads, ups, branch, tables, n_ctx
    )
    kv_total = sum_ctx([kv_keep, kv_1, kv_2, kv_3])
    both = jnp.concatenate([query_sum, kv_total], axis=1).reshape(2, rows // 2, LAT_COLS)
    mine, other = fold_halves(
        lax.dynamic_index_in_dim(both, tp_index % 2, 0, keepdims=False),
        lax.dynamic_index_in_dim(both, 1 - tp_index % 2, 0, keepdims=False),
    )
    out_parts = output_grads(where, attended, branch, shards, n_ctx, paired)
    up_parts = up_grads(
        where, query_low, query_grad, payloads, pair_grad, shards, n_ctx, paired
    )
    if paired:
        out_sums = fold_shards(out_parts)
        up_sums = fold_shards(up_parts)
    input_grad, grad_query_gain, grad_latent_gain, grad_gain_one, *down_parts = input_backward(
        where,
        mine,
        other,
        latent,
        gain_query,
        gain_latent,
        tables,
        normed_low,
        joined,
        activations,
        inverse_one[:, None],
        gain_one[None, :],
        middle_grad,
        pick,
        q_shard,
        low_rows,
        shards,
        n_ctx,
        paired,
    )
    grad_gate, grad_up, grad_down = join_hidden(where, hidden_sums, hidden)
    if paired:
        grad_out = sum_ctx(out_sums)
        grad_ups = sum_ctx(up_sums)
        grad_query_up = grad_ups[: query_up.shape[0]]
        grad_latent_up = grad_ups[query_up.shape[0] :]
        grad_downs = sum_ctx(fold_shards(down_parts))
        grad_query_down = grad_downs[:q_shard]
        grad_latent_down = grad_downs[q_shard : q_shard + low_shard]
    else:
        grad_out = scatter_rows(out_parts[0])
        grad_query_up, grad_latent_up = scatter_rows(up_parts[0]), scatter_rows(up_parts[1])
        grad_query_down = scatter_rows(down_parts[0][:QRANK])
        grad_latent_down = scatter_rows(down_parts[0][QRANK : LATENT + ROPE])
    grad_query_up = grad_query_up.reshape(query_up.shape[0], local_heads, LANES)
    grad_query_up = grad_query_up[:, :, : NOPE + ROPE].reshape(query_up.shape)

    gain_sums = lax.psum(jnp.concatenate([grad_gain_one[0], grad_gain_two]), both_axes)
    if paired:
        gain_row = grad_downs[q_shard + low_shard]
        gain_query_sum = gain_row[:q_shard]
        gain_latent_sum = gain_row[q_shard : q_shard + latent_gain.shape[0]]
    else:
        gain_query_sum = scatter_rows(grad_query_gain[0])
        gain_latent_sum = scatter_rows(grad_latent_gain[0])
    return (
        result.astype(BF16),
        input_grad,
        gain_sums[:width],
        grad_query_down.T,
        grad_latent_down.T,
        gain_query_sum,
        gain_latent_sum,
        grad_query_up,
        grad_latent_up,
        grad_out.T,
        gain_sums[width : 2 * width],
        grad_gate,
        grad_up,
        grad_down.T,
    )


def solution(mesh):
    tokens = P(("fsdp", "ctx"), "tp")
    by_columns = P("tp", ("fsdp", "ctx"))
    by_rows = P(("fsdp", "ctx"), "tp")
    latent_vector = P(("fsdp", "ctx"))
    feature_vector = P("tp")
    weights = (
        feature_vector,
        by_columns,
        by_columns,
        latent_vector,
        latent_vector,
        by_rows,
        by_rows,
        by_columns,
        feature_vector,
        by_rows,
        by_rows,
        by_columns,
    )
    return jax.shard_map(
        per_device,
        mesh=mesh,
        in_specs=(tokens,) + weights + (tokens,),
        out_specs=(tokens, tokens) + weights,
        check_vma=False,
    )
```

```python
import functools
import math

import jax
import jax.numpy as jnp
import numpy as np
from jax import lax
from jax.experimental import pallas as pl
from jax.experimental.pallas import tpu as pltpu
from jax.sharding import PartitionSpec as P

NOPE = 64
ROPE = 32
VDIM = 64
QRANK = 768
KVRANK = 256
LANES = 128
SUBLANES = 16

RESID = 1.4 / math.sqrt(62.0)
EPSILON = 1e-05
NEGATIVE = -1e30
SCORE = 1.0 / math.sqrt(NOPE + ROPE)

F32 = jnp.float32
BF16 = jnp.bfloat16

LATENT = QRANK + KVRANK
LAT_COLS = LATENT + LANES
LOW_ROWS = LAT_COLS - QRANK


def round_up(size, unit):
    return -(-size // unit) * unit


def product(left, right):
    return jnp.dot(left, right, preferred_element_type=F32)


def times_transposed(left, right):
    return lax.dot_general(left, right, (((1,), (1,)), ((), ())), preferred_element_type=F32)


def transposed_times(left, right):
    return lax.dot_general(left, right, (((0,), (0,)), ((), ())), preferred_element_type=F32)


def rotary_tables(positions):
    exponent = jnp.arange(0, ROPE, 2, dtype=F32) / ROPE
    inverse = 1.0 / 10000.0**exponent
    angles = positions[:, None] * inverse[None, :]
    angles = jnp.concatenate([angles, angles], axis=1)
    return (jnp.cos(angles), jnp.sin(angles))


def lane_tables(cos_table, sin_table):
    rows = cos_table.shape[0]
    half = ROPE // 2
    ones = jnp.ones((rows, NOPE), F32)
    before = jnp.zeros((rows, NOPE), F32)
    after = jnp.zeros((rows, LANES - NOPE - ROPE), F32)
    gap = jnp.zeros((rows, half), F32)
    return (
        jnp.concatenate([ones, cos_table, after], axis=1),
        jnp.concatenate([before, -sin_table[:, :half], gap, after], axis=1),
        jnp.concatenate([before, gap, sin_table[:, half:], after], axis=1),
    )


def turn_lanes(values, cos_table, lower_table, upper_table, sign):
    return (
        values * cos_table
        + sign * (pltpu.roll(values, LANES - ROPE // 2, 1) * lower_table)
        + sign * (pltpu.roll(values, ROPE // 2, 1) * upper_table)
    )


def swap(value, axis, distance):
    size = lax.axis_size(axis)
    return lax.ppermute(value, axis, [(i, i ^ distance) for i in range(size)])


def together(*arrays):
    count = len(arrays)
    return pl.pallas_call(
        lambda *refs: None,
        in_specs=[pl.BlockSpec(memory_space=pl.ANY)] * count,
        out_specs=[pl.BlockSpec(memory_space=pl.ANY)] * count,
        out_shape=[jax.ShapeDtypeStruct(a.shape, a.dtype) for a in arrays],
        input_output_aliases={i: i for i in range(count)},
        name="together",
    )(*arrays)


def in_turn(operands, order, move):
    operands = dict(operands)
    arrived = {}
    before = []
    for group in order:
        if before:
            both = together(*[operands[name] for name in group], *[arrived[name] for name in before])
            for name, array in zip(group, both[: len(group)]):
                operands[name] = array
            for name, array in zip(before, both[len(group) :]):
                arrived[name] = array
        for name in group:
            arrived[name] = move(name, operands[name])
        before = group
    return operands, arrived


def spread_ctx(own):
    first = swap(own, "ctx", 1)
    second = swap(own, "ctx", 2)
    return [own, first, second, swap(second, "ctx", 1)]


def exchange_ctx(chunks):
    return [chunks[0]] + [swap(chunks[k], "ctx", k) for k in range(1, len(chunks))]


def sum_ctx(parts):
    third = swap(parts[3].astype(BF16), "ctx", 1)
    far = (parts[2].astype(F32) + third.astype(F32)).astype(BF16)
    near = swap(parts[1].astype(BF16), "ctx", 1)
    return parts[0].astype(F32) + near.astype(F32) + swap(far, "ctx", 2).astype(F32)


def spread_tp(own):
    far = swap(own, "tp", 2)
    return [own, swap(own, "tp", 1), far, swap(far, "tp", 1)]


def total_tp(value):
    value = value + swap(value, "tp", 1)
    return value + swap(value, "tp", 2)


def fold_halves(keep, send):
    pair = (keep + swap(send, "tp", 1)).astype(BF16)
    mine = pair.astype(F32) + swap(pair, "tp", 2).astype(F32)
    return mine, swap(mine, "tp", 1)


def at_once(copies):
    for copy in copies:
        copy.start()
    for copy in copies:
        copy.wait()


def shard_place(where, index, n_ctx):
    return (where[0] ^ (index // n_ctx)) * n_ctx + (where[1] ^ (index % n_ctx))


def row_copies(where, pieces, first_row, rows, target, sems, first_sem, n_ctx):
    if len(pieces) == 1:
        return [pltpu.make_async_copy(pieces[0], target, sems.at[first_sem])]
    out = []
    for index, piece in enumerate(pieces):
        start = pl.multiple_of(shard_place(where, index, n_ctx) * rows, SUBLANES)
        out.append(
            pltpu.make_async_copy(
                piece.at[pl.ds(first_row, rows), :],
                target.at[pl.ds(start, rows), :],
                sems.at[first_sem + index],
            )
        )
    return out


def feature_start(where, place, width):
    return pl.multiple_of((where[2] ^ place) * width, LANES)


def feature_copies(where, pieces, target, row, rows, width, sems, first_sem):
    return [
        pltpu.make_async_copy(
            piece,
            target.at[pl.ds(row, rows), pl.ds(feature_start(where, place, width), width)],
            sems.at[first_sem + place],
        )
        for place, piece in enumerate(pieces)
    ]


def run_kernel(body, inputs, outputs, scratch, flops, moved, name, grid=None, exps=0, waits=()):
    count = len(inputs)
    inputs = list(inputs) + [(array, ANY) for array in waits]

    def used(*refs):
        body(*refs[:count], *refs[len(inputs) :])

    return pl.pallas_call(
        used,
        grid=grid if grid is not None else (),
        in_specs=[spec for _, spec in inputs],
        out_specs=[spec for _, spec in outputs],
        out_shape=[shape for shape, _ in outputs],
        scratch_shapes=scratch,
        compiler_params=pltpu.CompilerParams(vmem_limit_bytes=56 << 20),
        cost_estimate=pl.CostEstimate(flops=flops, bytes_accessed=moved, transcendentals=exps),
        name=name,
    )(*[array for array, _ in inputs])


VMEM = pl.BlockSpec(memory_space=pltpu.VMEM)
SMEM = pl.BlockSpec(memory_space=pltpu.SMEM)
ANY = pl.BlockSpec(memory_space=pl.ANY)


def shape(dims, dtype=BF16):
    return jax.ShapeDtypeStruct(dims, dtype)


def cut_hidden(where, gate, up, down, parts=1, waits=()):
    rows, total = gate.shape
    hidden = total // 4
    columns = round_up(3 * hidden, LANES)

    def body(where_ref, gate_ref, up_ref, down_ref, *rest):
        outs, stage = rest[:-1], rest[-1]
        blank = jnp.zeros((rows, columns - 3 * hidden), BF16)
        for place in range(4):
            units = slice(place * hidden, (place + 1) * hidden)
            stage[place] = jnp.concatenate(
                [gate_ref[:, units], up_ref[:, units], down_ref[:, units], blank], axis=1
            )
        for number, out in enumerate(outs):
            first = number // 4 * (rows // parts)
            out[...] = stage[where_ref[1] ^ (number % 4), first : first + rows // parts]

    return run_kernel(
        body,
        [(where, SMEM), (gate, VMEM), (up, VMEM), (down.T, VMEM)],
        [(shape((rows // parts, columns)), VMEM)] * (4 * parts),
        [pltpu.VMEM((4, rows, columns), BF16)],
        0,
        12 * rows * total,
        "cut_hidden",
        waits=waits,
    )


def join_hidden(where, pieces, hidden, waits=()):
    rows = pieces[0].shape[0]

    def body(where_ref, p0, p1, p2, p3, gate_ref, up_ref, down_ref, stage):
        for step, piece in enumerate((p0, p1, p2, p3)):
            stage[where_ref[1] ^ step] = piece[...]
        for first, out in ((0, gate_ref), (hidden, up_ref), (2 * hidden, down_ref)):
            out[...] = jnp.concatenate(
                [stage[place][:, first : first + hidden].astype(F32) for place in range(4)], axis=1
            )

    return run_kernel(
        body,
        [(where, SMEM)] + [(piece, VMEM) for piece in pieces],
        [
            (shape((rows, 4 * hidden), F32), VMEM),
            (shape((rows, 4 * hidden), F32), VMEM),
            (shape((rows, 4 * hidden), F32), VMEM),
        ],
        [pltpu.VMEM((4,) + pieces[0].shape, BF16)],
        0,
        80 * rows * hidden,
        "join_hidden",
        waits=waits,
    )


def latent_products(
    where, normed, pick, query_pieces, low_pieces, query_rows, low_rows, first_low, n_ctx, paired, waits=()
):
    rows, width = normed.shape
    half = rows // 2
    shared = query_pieces is low_pieces
    shards = len(query_pieces)
    arrays = list(query_pieces) if shared else list(query_pieces) + list(low_pieces)

    def body(where_ref, normed_ref, pick_ref, *rest):
        refs = rest[: len(arrays)]
        keep, send, joined, query_gain, latent_gain, low_in, total, sems = rest[len(arrays) :]
        query_refs = refs[: len(query_pieces)]
        low_refs = query_refs if shared else refs[len(query_pieces) :]
        copies = row_copies(
            where_ref, query_refs, 0, query_rows, joined.at[pl.ds(0, QRANK), :], sems, 0, n_ctx
        )
        copies += row_copies(
            where_ref, low_refs, first_low, low_rows, low_in, sems, len(query_refs), n_ctx
        )
        at_once(copies)
        joined[QRANK:, :] = product(pick_ref[...], low_in[...]).astype(BF16)
        if paired:
            first = LATENT + ROPE
            pieces = joined[first : first + SUBLANES, :LANES].astype(F32)
            query_gain[...] = jnp.concatenate(
                [pieces[i : i + 1, :query_rows] for i in range(shards)], axis=1
            )
            latent_gain[...] = jnp.concatenate(
                [pieces[i : i + 1, query_rows:] for i in range(shards)], axis=1
            )
            joined[first : first + SUBLANES, :] = jnp.zeros((SUBLANES, width), BF16)
        total[...] = times_transposed(normed_ref[...], joined[...])
        core = where_ref[3]
        keep[...] = total[pl.ds(pl.multiple_of(core * half, 8), half), :]
        send[...] = total[pl.ds(pl.multiple_of((1 - core) * half, 8), half), :]

    return run_kernel(
        body,
        [(where, SMEM), (normed, VMEM), (pick, VMEM)] + [(a, ANY) for a in arrays],
        [
            (shape((half, LAT_COLS), F32), VMEM),
            (shape((half, LAT_COLS), F32), VMEM),
            (shape((LAT_COLS, width)), VMEM),
            (shape((1, QRANK), F32), VMEM),
            (shape((1, KVRANK), F32), VMEM),
        ],
        [
            pltpu.VMEM((pick.shape[1], width), BF16),
            pltpu.VMEM((rows, LAT_COLS), F32),
            pltpu.SemaphoreType.DMA((len(query_pieces) + len(low_pieces),)),
        ],
        2 * rows * width * LAT_COLS,
        8 << 20,
        "latent_products",
        waits=waits,
    )


def latent_norms(where, mine, other, gain_query, gain_latent, tables, waits=()):
    half = mine.shape[0]
    rows = 2 * half

    def body(where_ref, mine_ref, other_ref, gq, gl, cos_t, lower_t, upper_t, latent, query_low, payload):
        core = where_ref[3]
        latent[pl.ds(pl.multiple_of(core * half, 8), half), :] = mine_ref[...]
        latent[pl.ds(pl.multiple_of((1 - core) * half, 8), half), :] = other_ref[...]
        query = latent[:, :QRANK]
        inverse = lax.rsqrt(jnp.mean(query * query, axis=1, keepdims=True) + EPSILON)
        query_low[...] = (query * inverse * gq[...]).astype(BF16)
        low = latent[:, QRANK:LATENT]
        inverse = lax.rsqrt(jnp.mean(low * low, axis=1, keepdims=True) + EPSILON)
        payload[:, :KVRANK] = (low * inverse * gl[...]).astype(BF16)
        rope = pltpu.roll(latent[:, LATENT:], NOPE, 1)
        payload[:, KVRANK:] = turn_lanes(rope, cos_t[...], lower_t[...], upper_t[...], 1.0).astype(BF16)

    return run_kernel(
        body,
        [(where, SMEM)]
        + [(a, VMEM) for a in (mine, other, gain_query, gain_latent) + tables],
        [
            (shape((rows, LAT_COLS), F32), VMEM),
            (shape((rows, QRANK)), VMEM),
            (shape((rows, KVRANK + LANES)), VMEM),
        ],
        [],
        20 * rows * LAT_COLS,
        4 << 20,
        "latent_norms",
        waits=waits,
    )


def masked_blocks(scores, place, rows, blocks):
    key_row = lax.broadcasted_iota(jnp.int32, (rows, rows), 0)
    query_column = lax.broadcasted_iota(jnp.int32, (rows, rows), 1)
    out = [jnp.where(key_row <= query_column, scores[:rows], NEGATIVE)]
    for block in range(1, blocks):
        seen = (place ^ block) < place
        out.append(jnp.where(seen, scores[block * rows : (block + 1) * rows], NEGATIVE))
    return out


def head_lanes(index):
    return pl.ds(pl.multiple_of(index * 2 * LANES, 2 * LANES), 2 * LANES)


def up_copies(where_ref, refs, wq, wkv, sems, n_ctx):
    if len(refs) == 3:
        return [
            pltpu.make_async_copy(refs[0], wq, sems.at[0]),
            pltpu.make_async_copy(refs[1], wkv, sems.at[1]),
        ]
    shards = len(refs) // 2
    query_rows = QRANK // shards
    low_rows = KVRANK // shards
    refs = refs[:shards]
    return row_copies(where_ref, refs, 0, query_rows, wq, sems, 0, n_ctx) + row_copies(
        where_ref, refs, query_rows, low_rows, wkv, sems, shards, n_ctx
    )


def out_copies(where_ref, refs, target, sems, first_sem, n_ctx):
    if len(refs) == 3:
        return [pltpu.make_async_copy(refs[2], target, sems.at[first_sem])]
    refs = refs[len(refs) // 2 :]
    return row_copies(where_ref, refs, 0, refs[0].shape[0], target, sems, first_sem, n_ctx)


def sequence_refs(source):
    return [piece for group in source for piece in group]


def sequence_shape(source):
    return (4 * len(source),) + source[0][0].shape


def sequence_copies(where, refs, target, rows, width, sems, first_sem):
    return [
        feature_copies(
            where, refs[at : at + 4], target, at // 4 * rows, rows, width, sems, first_sem + at
        )
        for at in range(0, len(refs), 4)
    ]


def hidden_copies(where, arrays, target, sems, first_sem, n_ctx, columns=None):
    cut = (lambda ref: ref) if columns is None else (lambda ref: ref.at[:, columns])
    if len(arrays) == 1:
        return [pltpu.make_async_copy(cut(arrays[0]), target, sems.at[first_sem])]
    rows = arrays[0].shape[0]
    parts = target.shape[0] // (rows * 2 * n_ctx)
    out = []
    for number, ref in enumerate(arrays):
        part, index = number // (2 * n_ctx), number % (2 * n_ctx)
        start = shard_place(where, index, n_ctx) * parts + part
        start = pl.multiple_of(start * rows, SUBLANES)
        out.append(
            pltpu.make_async_copy(
                cut(ref), target.at[pl.ds(start, rows), :], sems.at[first_sem + number]
            )
        )
    return out


def attention_forward(where, query_low, payloads, ups, tables, heads, n_ctx, waits=()):
    rows = query_low.shape[0]
    blocks = len(payloads)
    keys = blocks * rows
    pairs = heads // 2
    whole = lambda dims: pl.BlockSpec(dims, lambda i: (0, 0))
    column = lambda dims: pl.BlockSpec(dims, lambda i: (0, i))

    def body(where_ref, low_q, cos_t, lower_t, upper_t, *rest):
        sources = rest[:blocks]
        up_refs = rest[blocks : blocks + len(ups)]
        out, q_out, kv_out, lse_out, wq, wkv, tokens, sems = rest[blocks + len(ups) :]
        step = pl.program_id(0)

        @pl.when(step == 0)
        def _():
            copies = up_copies(where_ref, up_refs, wq, wkv, sems, n_ctx)
            first = len(copies)
            for block, source in enumerate(sources):
                copies.append(
                    pltpu.make_async_copy(
                        source, tokens.at[pl.ds(block * rows, rows), :], sems.at[first + block]
                    )
                )
            at_once(copies)

        key_lane = lax.broadcasted_iota(jnp.int32, (keys, LANES), 1)
        raw_pair = product(low_q[...], wq[:, head_lanes(step)])
        kv_pair = product(tokens[:, :KVRANK], wkv[:, head_lanes(step)]).astype(BF16)
        rope_key = tokens[:, KVRANK:]
        kv_out[...] = kv_pair
        outs = []
        for head in range(2):
            lanes = slice(head * LANES, (head + 1) * LANES)
            query = turn_lanes(
                raw_pair[:, lanes], cos_t[...], lower_t[...], upper_t[...], 1.0
            ).astype(BF16)
            pair = kv_pair[:, lanes]
            key = jnp.where(key_lane < NOPE, pair, rope_key)
            q_out[:, lanes] = query
            scores = times_transposed(key, query) * SCORE
            masked = masked_blocks(scores, where_ref[1], rows, blocks)
            top = functools.reduce(
                jnp.maximum, [jnp.max(part, axis=0, keepdims=True) for part in masked]
            )
            powers = [jnp.exp(part - top) for part in masked]
            total = sum(jnp.sum(part, axis=0, keepdims=True) for part in powers)
            prob = jnp.concatenate([part.astype(BF16) for part in powers], axis=0)
            mixed = transposed_times(pair, prob) / total
            outs.append(jnp.transpose(mixed))
            lse_out[0, head : head + 1, :] = top + jnp.log(total)
        lane = lax.broadcasted_iota(jnp.int32, (rows, LANES), 1)
        out[...] = jnp.where(lane < VDIM, pltpu.roll(outs[0], VDIM, 1), outs[1]).astype(BF16)

    return run_kernel(
        body,
        [(where, SMEM), (query_low, whole(query_low.shape))]
        + [(table, whole(table.shape)) for table in tables]
        + [(a, ANY) for a in list(payloads) + list(ups)],
        [
            (shape((rows, pairs * LANES)), column((rows, LANES))),
            (shape((rows, heads * LANES)), column((rows, 2 * LANES))),
            (shape((keys, heads * LANES)), column((keys, 2 * LANES))),
            (shape((pairs, 8, rows), F32), pl.BlockSpec((1, 8, rows), lambda i: (i, 0, 0))),
        ],
        [
            pltpu.VMEM((QRANK, heads * LANES), BF16),
            pltpu.VMEM((KVRANK, heads * LANES), BF16),
            pltpu.VMEM((keys, KVRANK + LANES), BF16),
            pltpu.SemaphoreType.DMA((64 + blocks,)),
        ],
        2 * heads * rows * (QRANK + 2 * keys) * LANES + 2 * heads * keys * KVRANK * LANES,
        12 << 20,
        "attention_forward",
        grid=(pairs,),
        exps=heads * rows * keys,
        waits=waits,
    )


def attention_backward(where, queries, pairs_low, lse, payloads, ups, branch, tables, n_ctx, waits=()):
    rows, q_lanes = queries.shape
    heads = q_lanes // LANES
    pairs = heads // 2
    blocks = len(payloads)
    keys = blocks * rows
    width = branch[0].shape[1]
    full_width = 4 * width
    inner = heads * VDIM
    whole = lambda dims: pl.BlockSpec(dims, lambda i: (0, 0))
    column = lambda dims: pl.BlockSpec(dims, lambda i: (0, i))
    moved = list(payloads) + list(ups) + list(branch)

    def body(where_ref, q_in, kv_in, lse_in, cos_t, lower_t, upper_t, *rest):
        refs = rest[: len(moved)]
        (dq_out, dkv_out, query_sum, kv_keep, kv_1, kv_2, kv_3) = rest[len(moved) : len(moved) + 7]
        wq, wkv, rope_key, wo, grad_in, dout, kv_sum, sems = rest[len(moved) + 7 :]
        step = pl.program_id(0)
        place = where_ref[1]

        @pl.when(step == 0)
        def _():
            at = 0
            sources, at = refs[at : at + blocks], at + blocks
            up_refs, at = refs[at : at + len(ups)], at + len(ups)
            branch_refs = refs[at : at + 4]
            copies = up_copies(where_ref, up_refs, wq, wkv, sems, n_ctx)
            for block, source in enumerate(sources):
                copies.append(
                    pltpu.make_async_copy(
                        source.at[:, pl.ds(KVRANK, LANES)],
                        rope_key.at[pl.ds(block * rows, rows), :],
                        sems.at[len(copies)],
                    )
                )
            copies += feature_copies(
                where_ref, branch_refs, grad_in, 0, rows, width, sems, len(copies)
            )
            copies += out_copies(where_ref, up_refs, wo, sems, len(copies), n_ctx)
            at_once(copies)
            dout[...] = product(grad_in[...], wo[...]).astype(BF16).astype(F32)
            query_sum[...] = jnp.zeros_like(query_sum)
            kv_sum[...] = jnp.zeros_like(kv_sum)

        key_lane = lax.broadcasted_iota(jnp.int32, (keys, LANES), 1)
        lane = lax.broadcasted_iota(jnp.int32, (rows, LANES), 1)
        both = dout[:, pl.ds(pl.multiple_of(step * LANES, LANES), LANES)]
        dkr = jnp.zeros((keys, LANES), F32)
        dq_parts = []
        dkv_parts = []
        for head in range(2):
            lanes = slice(head * LANES, (head + 1) * LANES)
            query = q_in[:, lanes]
            pair = kv_in[:, lanes]
            key = jnp.where(key_lane < NOPE, pair, rope_key[...])
            upper = pltpu.roll(both, VDIM, 1) if head == 0 else both
            out_grad = jnp.where(lane >= NOPE, upper, 0.0).astype(BF16)
            scores = times_transposed(key, query) * SCORE
            top = lse_in[0, head : head + 1, :]
            masked = masked_blocks(scores, place, rows, blocks)
            prob = jnp.concatenate([jnp.exp(part - top) for part in masked], axis=0)
            prob_grad = times_transposed(pair, out_grad)
            weighted = prob * prob_grad
            delta = jnp.sum(weighted, axis=0, keepdims=True)
            score_grad = (weighted - prob * delta).astype(BF16)
            key_grad = product(score_grad, query) * SCORE
            value_grad = product(prob.astype(BF16), out_grad)
            dkv_parts.append(jnp.where(key_lane < NOPE, key_grad, value_grad).astype(BF16))
            dkr = dkr + key_grad
            query_grad = jnp.transpose(transposed_times(key, score_grad)) * SCORE
            dq_parts.append(
                turn_lanes(query_grad, cos_t[...], lower_t[...], upper_t[...], -1.0).astype(BF16)
            )
        dq_pair = jnp.concatenate(dq_parts, axis=1)
        dkv_pair = jnp.concatenate(dkv_parts, axis=1)
        dq_out[...] = dq_pair
        dkv_out[...] = dkv_pair
        query_sum[...] += times_transposed(dq_pair, wq[:, head_lanes(step)])
        kv_sum[:, :KVRANK] += times_transposed(dkv_pair, wkv[:, head_lanes(step)])
        kv_sum[:, KVRANK:] += jnp.where(key_lane >= NOPE, dkr, 0.0)

        @pl.when(step == pairs - 1)
        def _():
            kv_keep[...] = kv_sum[:rows]
            for block, out in ((1, kv_1), (2, kv_2), (3, kv_3)):
                out[...] = kv_sum[block * rows : (block + 1) * rows].astype(BF16)

    return run_kernel(
        body,
        [
            (where, SMEM),
            (queries, column((rows, 2 * LANES))),
            (pairs_low, column((keys, 2 * LANES))),
            (lse, pl.BlockSpec((1, 8, rows), lambda i: (i, 0, 0))),
        ]
        + [(table, whole(table.shape)) for table in tables]
        + [(a, ANY) for a in moved],
        [
            (shape((rows, heads * LANES)), column((rows, 2 * LANES))),
            (shape((keys, heads * LANES)), column((keys, 2 * LANES))),
            (shape((rows, QRANK), F32), whole((rows, QRANK))),
            (shape((rows, KVRANK + LANES), F32), whole((rows, KVRANK + LANES))),
        ]
        + [(shape((rows, KVRANK + LANES)), whole((rows, KVRANK + LANES)))] * 3,
        [
            pltpu.VMEM((QRANK, heads * LANES), BF16),
            pltpu.VMEM((KVRANK, heads * LANES), BF16),
            pltpu.VMEM((keys, LANES), BF16),
            pltpu.VMEM((full_width, inner), BF16),
            pltpu.VMEM((rows, full_width), BF16),
            pltpu.VMEM((rows, inner), F32),
            pltpu.VMEM((keys, KVRANK + LANES), F32),
            pltpu.SemaphoreType.DMA((128 + blocks,)),
        ],
        10 * heads * rows * keys * LANES,
        24 << 20,
        "attention_backward",
        grid=(pairs,),
        exps=heads * rows * keys,
        waits=waits,
    )


def output_products(where, attended, ups, full_width, n_ctx, waits=()):
    rows, inner = attended.shape
    count = len(ups)
    width = full_width // 4

    def body(where_ref, attended_ref, *rest):
        refs = rest[:count]
        keep, send, weight, sems = rest[count:]
        at_once(out_copies(where_ref, refs, weight, sems, 0, n_ctx))
        for place in range(4):
            block = weight[pl.ds(feature_start(where_ref, place, width), width), :]
            part = times_transposed(attended_ref[...], block)
            if place % 2 == 0:
                keep[place // 2] = part
            else:
                send[place // 2] = part.astype(BF16)

    return run_kernel(
        body,
        [(where, SMEM), (attended, VMEM)] + [(a, ANY) for a in ups],
        [(shape((2, rows, width), F32), VMEM), (shape((2, rows, width)), VMEM)],
        [pltpu.VMEM((full_width, inner), BF16), pltpu.SemaphoreType.DMA((64,))],
        2 * rows * inner * full_width,
        6 << 20,
        "output_products",
        waits=waits,
    )


def feed_forward(where, tokens, branches, weights, gains, hidden, n_ctx):
    count, rows, width = sequence_shape(tokens)
    blocks = count // 4
    full_width = 4 * width
    columns = weights[0].shape[-1]
    upper_end = round_up(2 * hidden, LANES)
    lower_start = 2 * hidden // LANES * LANES
    shift = 2 * hidden - lower_start
    lower_cols = columns - lower_start
    total = blocks * rows
    token_list, branch_list = sequence_refs(tokens), sequence_refs(branches)
    flat = len(token_list) + len(branch_list)
    moved = token_list + branch_list + list(gains) + list(weights)

    def body(where_ref, *rest):
        refs = rest[: len(moved)]
        pairs_out, active_out, keep, send, inverse_out = rest[len(moved) : len(moved) + 5]
        normed, branch, weight, gain, sems = rest[len(moved) + 5 :]
        first = 2 * count
        weight_copies = feature_copies(
            where_ref, refs[flat : flat + 4], gain, 0, gain.shape[0], width, sems, first
        ) + hidden_copies(where_ref, refs[flat + 4 :], weight, sems, first + 4, n_ctx)
        token_copies = [
            first_list + second_list
            for first_list, second_list in zip(
                sequence_copies(
                    where_ref, refs[: len(token_list)], normed, rows, width, sems, 0
                ),
                sequence_copies(
                    where_ref, refs[len(token_list) : flat], branch, rows, width, sems, count
                ),
            )
        ]
        for copy in weight_copies + sum(token_copies, []):
            copy.start()
        for copy in weight_copies:
            copy.wait()

        def hidden_block(block, carry):
            for number, copies in enumerate(token_copies):

                @pl.when(block == number)
                def _():
                    for copy in copies:
                        copy.wait()

            here = pl.ds(pl.multiple_of(block * rows, rows), rows)
            source = normed[here, :].astype(F32) / gain[:1, :]
            inverse = lax.rsqrt(jnp.mean(source * source, axis=1, keepdims=True) + EPSILON)

            @pl.when(block == 0)
            def _():
                inverse_out[...] = jnp.broadcast_to(inverse, inverse_out.shape)

            both = product(normed[here, :], weight[:, :upper_end]) * inverse
            lower = product(branch[here, :], weight[:, lower_start:])
            gate = both[:, :hidden]
            upper = both[:, hidden : 2 * hidden]
            grad = lower[:, shift : shift + hidden]
            scaled = grad * inverse
            sigmoid = 1.0 / (1.0 + jnp.exp(-gate))
            active = gate * sigmoid
            pairs_out[here, :] = jnp.concatenate(
                [
                    scaled * upper * sigmoid * (1.0 + gate * (1.0 - sigmoid)),
                    scaled * active,
                    jnp.zeros((rows, upper_end - 2 * hidden), F32),
                ],
                axis=1,
            ).astype(BF16)
            active_out[here, :] = jnp.concatenate(
                [
                    jnp.zeros((rows, shift), F32),
                    active * upper,
                    jnp.zeros((rows, lower_cols - shift - hidden), F32),
                ],
                axis=1,
            ).astype(BF16)
            return carry

        lax.fori_loop(0, blocks, hidden_block, 0)
        for place in range(4):
            block = weight[pl.ds(feature_start(where_ref, place, width), width), :upper_end]
            part = times_transposed(pairs_out[...], block).astype(BF16)
            (send if place % 2 else keep)[place // 2] = part

    return run_kernel(
        body,
        [(where, SMEM)] + [(a, ANY) for a in moved],
        [
            (shape((total, upper_end)), VMEM),
            (shape((total, lower_cols)), VMEM),
            (shape((2, total, width)), VMEM),
            (shape((2, total, width)), VMEM),
            (shape((rows, LANES), F32), VMEM),
        ],
        [
            pltpu.VMEM((total, full_width), BF16),
            pltpu.VMEM((total, full_width), BF16),
            pltpu.VMEM((full_width, columns), BF16),
            pltpu.VMEM(gains[0].shape[:1] + (full_width,), F32),
            pltpu.SemaphoreType.DMA((2 * count + 4 + full_width // SUBLANES,)),
        ],
        10 * total * full_width * hidden,
        28 << 20,
        "feed_forward",
        exps=total * hidden,
    )


def feed_forward_result(where, active, weights, hidden, n_ctx, waits=()):
    total, lower_cols = active.shape
    columns = weights[0].shape[1]
    full_width = sum(a.shape[0] for a in weights)
    width = full_width // 4
    count = len(weights)

    def body(where_ref, active_ref, *rest):
        refs = rest[:count]
        outs = rest[count:-2]
        weight, sems = rest[-2:]
        lower = pl.ds(columns - lower_cols, lower_cols)
        at_once(hidden_copies(where_ref, refs, weight, sems, 0, n_ctx, columns=lower))
        for place in range(4):
            block = weight[pl.ds(feature_start(where_ref, place, width), width), :]
            part = times_transposed(active_ref[...], block).astype(BF16)
            outs[place % 2][place // 2] = part

    return run_kernel(
        body,
        [(where, SMEM), (active, VMEM)] + [(a, ANY) for a in weights],
        [(shape((2, total, width)), VMEM)] * 2,
        [
            pltpu.VMEM((full_width, lower_cols), BF16),
            pltpu.SemaphoreType.DMA((full_width // SUBLANES,)),
        ],
        2 * total * full_width * hidden,
        10 << 20,
        "feed_forward_result",
        waits=waits,
    )


def feed_forward_grads(
    where, tokens, branches, pairs_grad, active, hidden, columns, shards, n_ctx, distance, waits=()
):
    count, rows, width = sequence_shape(tokens)
    token_list, branch_list = sequence_refs(tokens), sequence_refs(branches)
    total = count // 4 * rows
    upper_end = pairs_grad.shape[1]
    lower_cols = active.shape[1]
    lower_start = columns - lower_cols
    shard_rows = 4 * width // shards

    def gradient(normed, branch, pairs_ref, active_ref):
        first = transposed_times(normed, pairs_ref[...])
        second = transposed_times(branch, active_ref[...])
        middle = first[:, lower_start:] + second[:, : upper_end - lower_start]
        return jnp.concatenate(
            [first[:, :lower_start], middle, second[:, upper_end - lower_start :]], axis=1
        ).astype(BF16)

    def body(where_ref, pairs_ref, active_ref, *rest):
        token_refs, rest = rest[: len(token_list)], rest[len(token_list) :]
        branch_refs, rest = rest[: len(branch_list)], rest[len(branch_list) :]
        outs = rest[:-4]
        normed, branch, stage, sems = rest[-4:]
        copies = sequence_copies(where_ref, token_refs, normed, rows, width, sems, 0)
        copies += sequence_copies(where_ref, branch_refs, branch, rows, width, sems, count)
        at_once(sum(copies, []))
        if distance is None:
            for place in range(4):
                here = slice(place * width, (place + 1) * width)
                outs[0][here, :] = gradient(normed[:, here], branch[:, here], pairs_ref, active_ref)
            return
        for number in range(n_ctx // 2):
            place = owner_blocks(where_ref, distance * (n_ctx // 2) + number, n_ctx)
            here = pl.ds(pl.multiple_of(place * width, LANES), width)
            stage[...] = gradient(normed[:, here], branch[:, here], pairs_ref, active_ref)
            for low in range(2):
                start = pl.multiple_of((low ^ (where_ref[1] % 2)) * shard_rows, SUBLANES)
                outs[2 * number + low][...] = stage[pl.ds(start, shard_rows), :]

    if distance is None:
        outputs = [(shape((4 * width, columns)), VMEM)]
    else:
        outputs = [(shape((shard_rows, columns)), VMEM)] * n_ctx
    return run_kernel(
        body,
        [(where, SMEM), (pairs_grad, VMEM), (active, VMEM)]
        + [(a, ANY) for a in token_list + branch_list],
        outputs,
        [
            pltpu.VMEM((total, 4 * width), BF16),
            pltpu.VMEM((total, 4 * width), BF16),
            pltpu.VMEM((width, columns), BF16),
            pltpu.SemaphoreType.DMA((2 * count,)),
        ],
        6 * total * 4 * width * hidden // 2,
        18 << 20,
        "feed_forward_grads",
        waits=waits,
    )


def owner_blocks(where_ref, part, n_ctx):
    per_row = n_ctx // 2
    return (where_ref[0] ^ (part // per_row)) * per_row + ((where_ref[1] // 2) ^ (part % per_row))


def output_grads(where, attended, branch, shards, n_ctx, paired, waits=()):
    rows, inner = attended.shape
    width = branch[0].shape[1]
    shard_rows = 4 * width // shards

    def body(where_ref, attended_ref, b0, b1, b2, b3, *rest):
        outs = rest[:-3]
        grad_in, stage, sems = rest[-3:]
        at_once(feature_copies(where_ref, (b0, b1, b2, b3), grad_in, 0, rows, width, sems, 0))
        for part in range(4):
            place = owner_blocks(where_ref, part, n_ctx) if paired else part
            here = pl.ds(pl.multiple_of(place * width, LANES), width)
            stage[...] = transposed_times(grad_in[:, here], attended_ref[...]).astype(BF16)
            if not paired:
                outs[0][part * width : (part + 1) * width, :] = stage[...]
                continue
            for low in range(2):
                start = pl.multiple_of((low ^ (where_ref[1] % 2)) * shard_rows, SUBLANES)
                outs[2 * part + low][...] = stage[pl.ds(start, shard_rows), :]

    if paired:
        outputs = [(shape((shard_rows, inner)), VMEM)] * shards
    else:
        outputs = [(shape((4 * width, inner)), VMEM)]
    return run_kernel(
        body,
        [(where, SMEM), (attended, VMEM)] + [(a, ANY) for a in branch],
        outputs,
        [
            pltpu.VMEM((rows, 4 * width), BF16),
            pltpu.VMEM((width, inner), BF16),
            pltpu.SemaphoreType.DMA((4,)),
        ],
        2 * rows * inner * 4 * width,
        6 << 20,
        "output_grads",
        waits=waits,
    )


def up_grads(where, query_low, query_grad, payloads, pair_grad, shards, n_ctx, paired, waits=()):
    rows = query_low.shape[0]
    blocks = len(payloads)
    lanes = query_grad.shape[1]
    query_rows = QRANK // shards
    low_rows = KVRANK // shards

    def body(where_ref, low_q, dq, dkv, *rest):
        sources = rest[:blocks]
        rest = rest[blocks:]
        outs = rest[:-4]
        tokens, stage_q, stage_kv, sems = rest[-4:]
        at_once(
            [
                pltpu.make_async_copy(
                    source.at[:, pl.ds(0, KVRANK)],
                    tokens.at[pl.ds(block * rows, rows), :],
                    sems.at[block],
                )
                for block, source in enumerate(sources)
            ]
        )
        grad_q = transposed_times(low_q[...], dq[...]).astype(BF16)
        grad_kv = transposed_times(tokens[...], dkv[...]).astype(BF16)
        if not paired:
            outs[0][...] = grad_q
            outs[1][...] = grad_kv
            return
        stage_q[...] = grad_q
        stage_kv[...] = grad_kv
        for index, out in enumerate(outs):
            place = shard_place(where_ref, index, n_ctx)
            out[:query_rows, :] = stage_q[
                pl.ds(pl.multiple_of(place * query_rows, SUBLANES), query_rows), :
            ]
            out[query_rows:, :] = stage_kv[
                pl.ds(pl.multiple_of(place * low_rows, SUBLANES), low_rows), :
            ]

    if paired:
        outputs = [(shape((query_rows + low_rows, lanes)), VMEM)] * shards
    else:
        outputs = [(shape((QRANK, lanes)), VMEM), (shape((KVRANK, lanes)), VMEM)]
    return run_kernel(
        body,
        [(where, SMEM), (query_low, VMEM), (query_grad, VMEM), (pair_grad, VMEM)]
        + [(a, ANY) for a in payloads],
        outputs,
        [
            pltpu.VMEM((blocks * rows, KVRANK), BF16),
            pltpu.VMEM((QRANK, lanes), BF16),
            pltpu.VMEM((KVRANK, lanes), BF16),
            pltpu.SemaphoreType.DMA((blocks,)),
        ],
        2 * lanes * (rows * QRANK + blocks * rows * KVRANK),
        10 << 20,
        "up_grads",
        waits=waits,
    )


def input_backward(
    where,
    mine,
    other,
    latent,
    gain_query,
    gain_latent,
    tables,
    normed,
    joined,
    activations,
    inverse_one,
    gain_one,
    middle_grad,
    pick,
    query_rows,
    low_rows,
    shards,
    n_ctx,
    paired,
    waits=(),
):
    half = mine.shape[0]
    rows, width = normed.shape
    full_width = 4 * width
    low_in = pick.shape[1]

    def body(
        where_ref, mine_ref, other_ref, latent_ref, gq, gl, cos_t, lower_t, upper_t, normed_ref,
        joined_ref, act_ref, inverse_ref, gain_ref, middle_ref, pick_ref, input_out, query_gain_out,
        latent_gain_out, gain_out, *rest
    ):
        outs = rest[:-3]
        sums, stage_q, stage_low = rest[-3:]
        core = where_ref[3]
        sums[pl.ds(pl.multiple_of(core * half, 8), half), :] = mine_ref[...]
        sums[pl.ds(pl.multiple_of((1 - core) * half, 8), half), :] = other_ref[...]
        parts = []
        for first, last, gain, out in (
            (0, QRANK, gq, query_gain_out),
            (QRANK, LATENT, gl, latent_gain_out),
        ):
            source = latent_ref[:, first:last]
            grad = sums[:, first:last]
            inverse = lax.rsqrt(jnp.mean(source * source, axis=1, keepdims=True) + EPSILON)
            out[...] = jnp.sum(grad * source * inverse, axis=0, keepdims=True)
            scaled = grad * gain[...]
            inner = jnp.mean(scaled * source, axis=1, keepdims=True)
            parts.append(inverse * scaled - source * (inverse * inverse * inverse * inner))
        rope = turn_lanes(sums[:, LATENT:], cos_t[...], lower_t[...], upper_t[...], -1.0)
        parts.append(pltpu.roll(rope, LANES - NOPE, 1))
        latent_grad = jnp.concatenate(parts, axis=1)
        low = latent_grad.astype(BF16)
        down_grad = transposed_times(low, normed_ref[...]).astype(BF16)
        if paired:
            stage_q[...] = down_grad[:QRANK]
            gains = [
                jnp.concatenate(
                    [
                        query_gain_out[:, i * query_rows : (i + 1) * query_rows],
                        latent_gain_out[:, i * KVRANK // shards : (i + 1) * KVRANK // shards],
                        jnp.zeros((1, width - LANES), F32),
                    ],
                    axis=1,
                )
                for i in range(shards)
            ]
            first = LATENT + ROPE - QRANK
            low_part = jnp.concatenate(
                [
                    down_grad[QRANK : LATENT + ROPE].astype(F32),
                    jnp.concatenate(gains, axis=0),
                    jnp.zeros((LOW_ROWS - first - shards, width), F32),
                ],
                axis=0,
            ).astype(BF16)
            stage_low[...] = transposed_times(pick_ref[...], low_part).astype(BF16)
            for index, out in enumerate(outs):
                place = shard_place(where_ref, index, n_ctx)
                out[:query_rows, :] = stage_q[
                    pl.ds(pl.multiple_of(place * query_rows, SUBLANES), query_rows), :
                ]
                out[query_rows:, :] = stage_low[
                    pl.ds(pl.multiple_of(place * low_rows, SUBLANES), low_rows), :
                ]
        else:
            outs[0][...] = down_grad
        row_inner = jnp.sum(latent_grad * latent_ref[...], axis=1, keepdims=True)
        normed_grad = product(low, joined_ref[...])
        source = act_ref[...].astype(F32)
        inverse = inverse_ref[...]
        gain_out[...] = jnp.sum(normed_grad * source * inverse, axis=0, keepdims=True)
        input_out[...] = (
            middle_ref[...]
            + inverse * (normed_grad * gain_ref[...])
            - source * (inverse * inverse * row_inner / full_width)
        )

    if paired:
        outputs = [(shape((query_rows + low_rows, width)), VMEM)] * shards
    else:
        outputs = [(shape((LAT_COLS, width)), VMEM)]
    arrays = (mine, other, latent, gain_query, gain_latent) + tables
    arrays += (normed, joined, activations, inverse_one, gain_one, middle_grad, pick)
    return run_kernel(
        body,
        [(where, SMEM)] + [(a, VMEM) for a in arrays],
        [
            (shape((rows, width), F32), VMEM),
            (shape((1, QRANK), F32), VMEM),
            (shape((1, KVRANK), F32), VMEM),
            (shape((1, width), F32), VMEM),
        ]
        + outputs,
        [
            pltpu.VMEM((rows, LAT_COLS), F32),
            pltpu.VMEM((QRANK, width), BF16),
            pltpu.VMEM((low_in, width), BF16),
        ],
        4 * rows * width * LAT_COLS,
        12 << 20,
        "input_backward",
        waits=waits,
    )


def pick_matrix(columns, rows_each, valid):
    matrix = np.zeros((LOW_ROWS, columns), np.float32)
    for row in range(KVRANK + ROPE):
        matrix[row, row // valid * rows_each + row % valid] = 1.0
    for shard in range(columns // rows_each if rows_each > valid else 0):
        matrix[KVRANK + ROPE + shard, shard * rows_each + valid] = 1.0
    return jnp.asarray(matrix, BF16)


def per_device(
    activations,
    attn_gain,
    query_down,
    latent_down,
    query_gain,
    latent_gain,
    query_up,
    latent_up,
    attn_output,
    ffn_gain,
    ffn_gate,
    ffn_up,
    ffn_down,
    out_grad,
):
    n_fsdp = lax.axis_size("fsdp")
    n_ctx = lax.axis_size("ctx")
    n_tp = lax.axis_size("tp")
    shards = n_fsdp * n_ctx
    paired = n_fsdp == 2 and shards == 2 * n_tp
    rows, width = activations.shape
    full_width = width * n_tp
    fsdp_index = lax.axis_index("fsdp").astype(jnp.int32)
    ctx_index = lax.axis_index("ctx").astype(jnp.int32)
    tp_index = lax.axis_index("tp").astype(jnp.int32)
    shard_index = fsdp_index * n_ctx + ctx_index
    where = jnp.stack([fsdp_index, ctx_index, tp_index, tp_index % 2])
    local_heads = query_up.shape[1] // (NOPE + ROPE)
    hidden = ffn_gate.shape[1] // n_ctx
    columns = round_up(3 * hidden, LANES)
    q_shard = query_down.shape[1]
    low_shard = latent_down.shape[1]
    both_axes = ("fsdp", "ctx")

    def spread_shards(own):
        pieces = spread_ctx(own)
        return pieces + [swap(piece, "fsdp", 1) for piece in pieces]

    def fold_shards(parts):
        return [
            (parts[k].astype(F32) + swap(parts[n_ctx + k], "fsdp", 1).astype(F32)).astype(BF16)
            for k in range(n_ctx)
        ]

    def gather_rows(value):
        return lax.all_gather(value, both_axes, axis=0, tiled=True)

    def scatter_rows(value):
        return lax.psum_scatter(value, both_axes, scatter_dimension=0, tiled=True).astype(F32)

    def spread_sequence(own):
        return [spread_tp(block) for block in spread_ctx(own)]

    inputs = activations.astype(F32)
    gain_one = attn_gain.astype(F32)
    row_sums = total_tp(jnp.sum(inputs * inputs, axis=1))
    inverse_one = lax.rsqrt(row_sums / full_width + EPSILON)
    gain_two = ffn_gain.astype(F32)
    gains_two = spread_tp(jnp.broadcast_to(gain_two[None, :], (8, width)))
    normed_low = (inputs * inverse_one[:, None] * gain_one).astype(BF16)

    query_pad = jnp.pad(
        query_up.reshape(query_up.shape[0], local_heads, NOPE + ROPE),
        ((0, 0), (0, 0), (0, LANES - NOPE - ROPE)),
    ).reshape(query_up.shape[0], local_heads * LANES)
    if paired:
        low_rows = round_up(low_shard, SUBLANES)
        pick = pick_matrix(shards * low_rows, low_rows, low_shard)
        down_own = jnp.concatenate(
            [
                query_down.T,
                latent_down.T,
                jnp.pad(
                    jnp.concatenate([query_gain, latent_gain])[None, :],
                    ((0, low_rows - low_shard - 1), (0, width - LANES)),
                ),
            ]
        )
        query_pieces = low_pieces = spread_shards(down_own)
        first_low = q_shard
        ups = spread_shards(jnp.concatenate([query_pad, latent_up])) + spread_shards(attn_output.T)
    else:
        low_rows = low_shard
        pick = pick_matrix(LOW_ROWS, KVRANK + ROPE, KVRANK + ROPE)
        query_pieces = [gather_rows(query_down.T)]
        low_pieces = [
            jnp.pad(gather_rows(latent_down.T), ((0, LOW_ROWS - KVRANK - ROPE), (0, 0)))
        ]
        first_low = 0
        ups = [gather_rows(query_pad), gather_rows(latent_up), gather_rows(attn_output.T)]

    parts = 2 if paired else 1
    chunks = cut_hidden(where, ffn_gate, ffn_up, ffn_down, parts=parts)
    if paired:
        sent = {(part, k): chunks[n_ctx * part + k] for part in range(parts) for k in range(1, n_ctx)}
        order = [[(part, k) for k in group] for part in range(parts) for group in ((2, 1), (3,))]
        _, got = in_turn(sent, order, lambda key, value: swap(value, "ctx", key[1]))
        got.update({(part, 0): chunks[n_ctx * part] for part in range(parts)})
        order = [[(part, 0)] for part in range(parts)]
        order += [[(part, k)] for part in range(parts) for k in range(1, n_ctx)]
        got, crossed = in_turn(got, order, lambda key, value: swap(value, "fsdp", 1))
        weights = []
        for part in range(parts):
            weights += [got[part, k] for k in range(n_ctx)]
            weights += [crossed[part, k] for k in range(n_ctx)]
    else:
        stack = jnp.stack(exchange_ctx(chunks))
        stack = jnp.stack(
            [
                lax.dynamic_index_in_dim(stack, ctx_index ^ k, 0, keepdims=False)
                for k in range(n_ctx)
            ]
        )
        weights = [lax.all_gather(stack, "fsdp", axis=0).reshape(full_width, columns)]

    upstream = out_grad.astype(F32)
    branches = spread_sequence((RESID * upstream).astype(BF16))

    keep, send, joined, gain_query, gain_latent = latent_products(
        where,
        normed_low,
        pick,
        query_pieces,
        low_pieces,
        q_shard,
        low_rows,
        first_low,
        n_ctx,
        paired,
        waits=chunks[:1],
    )
    if not paired:
        gains = jnp.zeros((QRANK + KVRANK,), F32)
        gains = lax.dynamic_update_slice(
            gains, query_gain.astype(F32), (shard_index * query_gain.shape[0],)
        )
        gains = lax.dynamic_update_slice(
            gains, latent_gain.astype(F32), (QRANK + shard_index * latent_gain.shape[0],)
        )
        gains = lax.psum(gains, both_axes)
        gain_query = gains[None, :QRANK]
        gain_latent = gains[None, QRANK:]
    mine, other = fold_halves(keep, send)
    query_pos = ctx_index * rows + jnp.arange(rows, dtype=jnp.int32)
    tables = lane_tables(*rotary_tables(query_pos.astype(F32)))
    latent, query_low, payload = latent_norms(where, mine, other, gain_query, gain_latent, tables)
    payloads = spread_ctx(payload)

    attended, queries_low, pairs_low, lse = attention_forward(
        where, query_low, payloads, ups, tables, local_heads, n_ctx
    )

    def fold_tp(keep, send):
        got = swap(send, "tp", 1)
        far = (keep[1].astype(F32) + got[1].astype(F32)).astype(BF16)
        near = keep[0].astype(F32) + got[0].astype(F32)
        return near + swap(far, "tp", 2).astype(F32)

    keep, send = output_products(where, attended, ups, full_width, n_ctx)
    middle = inputs + RESID * fold_tp(keep, send)

    tokens = spread_sequence((middle * gain_two).astype(BF16))
    pairs_grad, active, keep, send, inverse_two = feed_forward(
        where, tokens, branches, weights, gains_two, hidden, n_ctx
    )
    inverse_two = inverse_two[:, :1]

    def fold_sequence(keep, send):
        got = swap(send, "tp", 1)
        totals = []
        for block in reversed(range(n_ctx)):
            here = slice(block * rows, (block + 1) * rows)
            far = (keep[1, here].astype(F32) + got[1, here].astype(F32)).astype(BF16)
            near = keep[0, here].astype(F32) + got[0, here].astype(F32)
            totals.append(near + swap(far, "tp", 2).astype(F32))
        return sum_ctx(totals[::-1])

    second_grad = fold_sequence(keep, send)
    scaled_two = second_grad * gain_two
    grad_gain_two = jnp.sum(second_grad * middle, axis=0)
    inner_two = lax.psum(jnp.sum(scaled_two * middle, axis=1), "tp") / full_width
    middle_grad = upstream + scaled_two - middle * (inverse_two * inverse_two * inner_two[:, None])
    branch = spread_tp((RESID * middle_grad).astype(BF16))

    result = middle + RESID * fold_sequence(
        *feed_forward_result(where, active, weights, hidden, n_ctx)
    )
    grads = functools.partial(
        feed_forward_grads, where, tokens, branches, pairs_grad, active, hidden, columns, shards, n_ctx
    )
    if paired:
        sent, kept = grads(1), grads(0)
        moved = [swap(sent[k], "fsdp", 1) for k in reversed(range(n_ctx))][::-1]
        sums = [
            (kept[k].astype(F32) + moved[k].astype(F32)).astype(BF16) for k in range(n_ctx)
        ]
    else:
        total = grads(None)[0].reshape(n_fsdp, n_ctx, full_width // shards, columns)
        total = lax.psum_scatter(total, "fsdp", scatter_dimension=0, tiled=False)
        sums = [
            lax.dynamic_index_in_dim(total, ctx_index ^ k, 0, keepdims=False) for k in range(n_ctx)
        ]
    hidden_sums = exchange_ctx(sums)

    query_grad, pair_grad, query_sum, kv_keep, kv_1, kv_2, kv_3 = attention_backward(
        where, queries_low, pairs_low, lse, payloads, ups, branch, tables, n_ctx
    )
    kv_total = sum_ctx([kv_keep, kv_1, kv_2, kv_3])
    both = jnp.concatenate([query_sum, kv_total], axis=1).reshape(2, rows // 2, LAT_COLS)
    mine, other = fold_halves(
        lax.dynamic_index_in_dim(both, tp_index % 2, 0, keepdims=False),
        lax.dynamic_index_in_dim(both, 1 - tp_index % 2, 0, keepdims=False),
    )
    out_parts = output_grads(where, attended, branch, shards, n_ctx, paired)
    up_parts = up_grads(
        where, query_low, query_grad, payloads, pair_grad, shards, n_ctx, paired
    )
    if paired:
        out_sums = fold_shards(out_parts)
        up_sums = fold_shards(up_parts)
    input_grad, grad_query_gain, grad_latent_gain, grad_gain_one, *down_parts = input_backward(
        where,
        mine,
        other,
        latent,
        gain_query,
        gain_latent,
        tables,
        normed_low,
        joined,
        activations,
        inverse_one[:, None],
        gain_one[None, :],
        middle_grad,
        pick,
        q_shard,
        low_rows,
        shards,
        n_ctx,
        paired,
    )
    grad_gate, grad_up, grad_down = join_hidden(where, hidden_sums, hidden)
    if paired:
        grad_out = sum_ctx(out_sums)
        grad_ups = sum_ctx(up_sums)
        grad_query_up = grad_ups[: query_up.shape[0]]
        grad_latent_up = grad_ups[query_up.shape[0] :]
        grad_downs = sum_ctx(fold_shards(down_parts))
        grad_query_down = grad_downs[:q_shard]
        grad_latent_down = grad_downs[q_shard : q_shard + low_shard]
    else:
        grad_out = scatter_rows(out_parts[0])
        grad_query_up, grad_latent_up = scatter_rows(up_parts[0]), scatter_rows(up_parts[1])
        grad_query_down = scatter_rows(down_parts[0][:QRANK])
        grad_latent_down = scatter_rows(down_parts[0][QRANK : LATENT + ROPE])
    grad_query_up = grad_query_up.reshape(query_up.shape[0], local_heads, LANES)
    grad_query_up = grad_query_up[:, :, : NOPE + ROPE].reshape(query_up.shape)

    gain_sums = lax.psum(jnp.concatenate([grad_gain_one[0], grad_gain_two]), both_axes)
    if paired:
        gain_row = grad_downs[q_shard + low_shard]
        gain_query_sum = gain_row[:q_shard]
        gain_latent_sum = gain_row[q_shard : q_shard + latent_gain.shape[0]]
    else:
        gain_query_sum = scatter_rows(grad_query_gain[0])
        gain_latent_sum = scatter_rows(grad_latent_gain[0])
    return (
        result.astype(BF16),
        input_grad,
        gain_sums[:width],
        grad_query_down.T,
        grad_latent_down.T,
        gain_query_sum,
        gain_latent_sum,
        grad_query_up,
        grad_latent_up,
        grad_out.T,
        gain_sums[width : 2 * width],
        grad_gate,
        grad_up,
        grad_down.T,
    )


def solution(mesh):
    tokens = P(("fsdp", "ctx"), "tp")
    by_columns = P("tp", ("fsdp", "ctx"))
    by_rows = P(("fsdp", "ctx"), "tp")
    latent_vector = P(("fsdp", "ctx"))
    feature_vector = P("tp")
    weights = (
        feature_vector,
        by_columns,
        by_columns,
        latent_vector,
        latent_vector,
        by_rows,
        by_rows,
        by_columns,
        feature_vector,
        by_rows,
        by_rows,
        by_columns,
    )
    return jax.shard_map(
        per_device,
        mesh=mesh,
        in_specs=(tokens,) + weights + (tokens,),
        out_specs=(tokens, tokens) + weights,
        check_vma=False,
    )
```

```python
import functools
import math

import jax
import jax.numpy as jnp
import numpy as np
from jax import lax
from jax.experimental import pallas as pl
from jax.experimental.pallas import tpu as pltpu
from jax.sharding import PartitionSpec as P

NOPE = 64
ROPE = 32
VDIM = 64
QRANK = 768
KVRANK = 256
LANES = 128
SUBLANES = 16

RESID = 1.4 / math.sqrt(62.0)
EPSILON = 1e-05
NEGATIVE = -1e30
SCORE = 1.0 / math.sqrt(NOPE + ROPE)

F32 = jnp.float32
BF16 = jnp.bfloat16

LATENT = QRANK + KVRANK
LAT_COLS = LATENT + LANES
LOW_ROWS = LAT_COLS - QRANK


def round_up(size, unit):
    return -(-size // unit) * unit


def product(left, right):
    return jnp.dot(left, right, preferred_element_type=F32)


def times_transposed(left, right):
    return lax.dot_general(left, right, (((1,), (1,)), ((), ())), preferred_element_type=F32)


def transposed_times(left, right):
    return lax.dot_general(left, right, (((0,), (0,)), ((), ())), preferred_element_type=F32)


def rotary_tables(positions):
    exponent = jnp.arange(0, ROPE, 2, dtype=F32) / ROPE
    inverse = 1.0 / 10000.0**exponent
    angles = positions[:, None] * inverse[None, :]
    angles = jnp.concatenate([angles, angles], axis=1)
    return (jnp.cos(angles), jnp.sin(angles))


def lane_tables(cos_table, sin_table):
    rows = cos_table.shape[0]
    half = ROPE // 2
    ones = jnp.ones((rows, NOPE), F32)
    before = jnp.zeros((rows, NOPE), F32)
    after = jnp.zeros((rows, LANES - NOPE - ROPE), F32)
    gap = jnp.zeros((rows, half), F32)
    return (
        jnp.concatenate([ones, cos_table, after], axis=1),
        jnp.concatenate([before, -sin_table[:, :half], gap, after], axis=1),
        jnp.concatenate([before, gap, sin_table[:, half:], after], axis=1),
    )


def turn_lanes(values, cos_table, lower_table, upper_table, sign):
    return (
        values * cos_table
        + sign * (pltpu.roll(values, LANES - ROPE // 2, 1) * lower_table)
        + sign * (pltpu.roll(values, ROPE // 2, 1) * upper_table)
    )


def swap(value, axis, distance):
    size = lax.axis_size(axis)
    return lax.ppermute(value, axis, [(i, i ^ distance) for i in range(size)])


def together(*arrays):
    count = len(arrays)
    return pl.pallas_call(
        lambda *refs: None,
        in_specs=[pl.BlockSpec(memory_space=pl.ANY)] * count,
        out_specs=[pl.BlockSpec(memory_space=pl.ANY)] * count,
        out_shape=[jax.ShapeDtypeStruct(a.shape, a.dtype) for a in arrays],
        input_output_aliases={i: i for i in range(count)},
        name="together",
    )(*arrays)


def in_turn(operands, order, move):
    operands = dict(operands)
    arrived = {}
    before = []
    for group in order:
        if before:
            both = together(*[operands[name] for name in group], *[arrived[name] for name in before])
            for name, array in zip(group, both[: len(group)]):
                operands[name] = array
            for name, array in zip(before, both[len(group) :]):
                arrived[name] = array
        for name in group:
            arrived[name] = move(name, operands[name])
        before = group
    return operands, arrived


def spread_ctx(own):
    first = swap(own, "ctx", 1)
    second = swap(own, "ctx", 2)
    return [own, first, second, swap(second, "ctx", 1)]


def exchange_ctx(chunks):
    return [chunks[0]] + [swap(chunks[k], "ctx", k) for k in range(1, len(chunks))]


def sum_ctx(parts):
    third = swap(parts[3].astype(BF16), "ctx", 1)
    far = (parts[2].astype(F32) + third.astype(F32)).astype(BF16)
    near = swap(parts[1].astype(BF16), "ctx", 1)
    return parts[0].astype(F32) + near.astype(F32) + swap(far, "ctx", 2).astype(F32)


def spread_tp(own):
    far = swap(own, "tp", 2)
    return [own, swap(own, "tp", 1), far, swap(far, "tp", 1)]


def total_tp(value):
    value = value + swap(value, "tp", 1)
    return value + swap(value, "tp", 2)


def fold_halves(keep, send):
    pair = (keep + swap(send, "tp", 1)).astype(BF16)
    mine = pair.astype(F32) + swap(pair, "tp", 2).astype(F32)
    return mine, swap(mine, "tp", 1)


def at_once(copies):
    for copy in copies:
        copy.start()
    for copy in copies:
        copy.wait()


def shard_place(where, index, n_ctx):
    return (where[0] ^ (index // n_ctx)) * n_ctx + (where[1] ^ (index % n_ctx))


def row_copies(where, pieces, first_row, rows, target, sems, first_sem, n_ctx):
    if len(pieces) == 1:
        return [pltpu.make_async_copy(pieces[0], target, sems.at[first_sem])]
    out = []
    for index, piece in enumerate(pieces):
        start = pl.multiple_of(shard_place(where, index, n_ctx) * rows, SUBLANES)
        out.append(
            pltpu.make_async_copy(
                piece.at[pl.ds(first_row, rows), :],
                target.at[pl.ds(start, rows), :],
                sems.at[first_sem + index],
            )
        )
    return out


def feature_start(where, place, width):
    return pl.multiple_of((where[2] ^ place) * width, LANES)


def feature_copies(where, pieces, target, row, rows, width, sems, first_sem):
    return [
        pltpu.make_async_copy(
            piece,
            target.at[pl.ds(row, rows), pl.ds(feature_start(where, place, width), width)],
            sems.at[first_sem + place],
        )
        for place, piece in enumerate(pieces)
    ]


def run_kernel(body, inputs, outputs, scratch, flops, moved, name, grid=None, exps=0, waits=()):
    count = len(inputs)
    inputs = list(inputs) + [(array, ANY) for array in waits]

    def used(*refs):
        body(*refs[:count], *refs[len(inputs) :])

    return pl.pallas_call(
        used,
        grid=grid if grid is not None else (),
        in_specs=[spec for _, spec in inputs],
        out_specs=[spec for _, spec in outputs],
        out_shape=[shape for shape, _ in outputs],
        scratch_shapes=scratch,
        compiler_params=pltpu.CompilerParams(vmem_limit_bytes=56 << 20),
        cost_estimate=pl.CostEstimate(flops=flops, bytes_accessed=moved, transcendentals=exps),
        name=name,
    )(*[array for array, _ in inputs])


VMEM = pl.BlockSpec(memory_space=pltpu.VMEM)
SMEM = pl.BlockSpec(memory_space=pltpu.SMEM)
ANY = pl.BlockSpec(memory_space=pl.ANY)


def shape(dims, dtype=BF16):
    return jax.ShapeDtypeStruct(dims, dtype)


def cut_hidden(where, gate, up, down, parts=1, waits=()):
    rows, total = gate.shape
    hidden = total // 4
    columns = round_up(3 * hidden, LANES)

    def body(where_ref, gate_ref, up_ref, down_ref, *rest):
        outs, stage = rest[:-1], rest[-1]
        blank = jnp.zeros((rows, columns - 3 * hidden), BF16)
        for place in range(4):
            units = slice(place * hidden, (place + 1) * hidden)
            stage[place] = jnp.concatenate(
                [gate_ref[:, units], up_ref[:, units], down_ref[:, units], blank], axis=1
            )
        for number, out in enumerate(outs):
            first = number // 4 * (rows // parts)
            out[...] = stage[where_ref[1] ^ (number % 4), first : first + rows // parts]

    return run_kernel(
        body,
        [(where, SMEM), (gate, VMEM), (up, VMEM), (down.T, VMEM)],
        [(shape((rows // parts, columns)), VMEM)] * (4 * parts),
        [pltpu.VMEM((4, rows, columns), BF16)],
        0,
        12 * rows * total,
        "cut_hidden",
        waits=waits,
    )


def join_hidden(where, pieces, hidden, waits=()):
    rows = pieces[0].shape[0]

    def body(where_ref, p0, p1, p2, p3, gate_ref, up_ref, down_ref, stage):
        for step, piece in enumerate((p0, p1, p2, p3)):
            stage[where_ref[1] ^ step] = piece[...]
        for first, out in ((0, gate_ref), (hidden, up_ref), (2 * hidden, down_ref)):
            out[...] = jnp.concatenate(
                [stage[place][:, first : first + hidden].astype(F32) for place in range(4)], axis=1
            )

    return run_kernel(
        body,
        [(where, SMEM)] + [(piece, VMEM) for piece in pieces],
        [
            (shape((rows, 4 * hidden), F32), VMEM),
            (shape((rows, 4 * hidden), F32), VMEM),
            (shape((rows, 4 * hidden), F32), VMEM),
        ],
        [pltpu.VMEM((4,) + pieces[0].shape, BF16)],
        0,
        80 * rows * hidden,
        "join_hidden",
        waits=waits,
    )


def latent_products(
    where, normed, pick, query_pieces, low_pieces, query_rows, low_rows, first_low, n_ctx, paired, waits=()
):
    rows, width = normed.shape
    half = rows // 2
    shared = query_pieces is low_pieces
    shards = len(query_pieces)
    arrays = list(query_pieces) if shared else list(query_pieces) + list(low_pieces)

    def body(where_ref, normed_ref, pick_ref, *rest):
        refs = rest[: len(arrays)]
        keep, send, joined, query_gain, latent_gain, low_in, total, sems = rest[len(arrays) :]
        query_refs = refs[: len(query_pieces)]
        low_refs = query_refs if shared else refs[len(query_pieces) :]
        copies = row_copies(
            where_ref, query_refs, 0, query_rows, joined.at[pl.ds(0, QRANK), :], sems, 0, n_ctx
        )
        copies += row_copies(
            where_ref, low_refs, first_low, low_rows, low_in, sems, len(query_refs), n_ctx
        )
        at_once(copies)
        joined[QRANK:, :] = product(pick_ref[...], low_in[...]).astype(BF16)
        if paired:
            first = LATENT + ROPE
            pieces = joined[first : first + SUBLANES, :LANES].astype(F32)
            query_gain[...] = jnp.concatenate(
                [pieces[i : i + 1, :query_rows] for i in range(shards)], axis=1
            )
            latent_gain[...] = jnp.concatenate(
                [pieces[i : i + 1, query_rows:] for i in range(shards)], axis=1
            )
            joined[first : first + SUBLANES, :] = jnp.zeros((SUBLANES, width), BF16)
        total[...] = times_transposed(normed_ref[...], joined[...])
        core = where_ref[3]
        keep[...] = total[pl.ds(pl.multiple_of(core * half, 8), half), :]
        send[...] = total[pl.ds(pl.multiple_of((1 - core) * half, 8), half), :]

    return run_kernel(
        body,
        [(where, SMEM), (normed, VMEM), (pick, VMEM)] + [(a, ANY) for a in arrays],
        [
            (shape((half, LAT_COLS), F32), VMEM),
            (shape((half, LAT_COLS), F32), VMEM),
            (shape((LAT_COLS, width)), VMEM),
            (shape((1, QRANK), F32), VMEM),
            (shape((1, KVRANK), F32), VMEM),
        ],
        [
            pltpu.VMEM((pick.shape[1], width), BF16),
            pltpu.VMEM((rows, LAT_COLS), F32),
            pltpu.SemaphoreType.DMA((len(query_pieces) + len(low_pieces),)),
        ],
        2 * rows * width * LAT_COLS,
        8 << 20,
        "latent_products",
        waits=waits,
    )


def latent_norms(where, mine, other, gain_query, gain_latent, tables, waits=()):
    half = mine.shape[0]
    rows = 2 * half

    def body(where_ref, mine_ref, other_ref, gq, gl, cos_t, lower_t, upper_t, latent, query_low, payload):
        core = where_ref[3]
        latent[pl.ds(pl.multiple_of(core * half, 8), half), :] = mine_ref[...]
        latent[pl.ds(pl.multiple_of((1 - core) * half, 8), half), :] = other_ref[...]
        query = latent[:, :QRANK]
        inverse = lax.rsqrt(jnp.mean(query * query, axis=1, keepdims=True) + EPSILON)
        query_low[...] = (query * inverse * gq[...]).astype(BF16)
        low = latent[:, QRANK:LATENT]
        inverse = lax.rsqrt(jnp.mean(low * low, axis=1, keepdims=True) + EPSILON)
        payload[:, :KVRANK] = (low * inverse * gl[...]).astype(BF16)
        rope = pltpu.roll(latent[:, LATENT:], NOPE, 1)
        payload[:, KVRANK:] = turn_lanes(rope, cos_t[...], lower_t[...], upper_t[...], 1.0).astype(BF16)

    return run_kernel(
        body,
        [(where, SMEM)]
        + [(a, VMEM) for a in (mine, other, gain_query, gain_latent) + tables],
        [
            (shape((rows, LAT_COLS), F32), VMEM),
            (shape((rows, QRANK)), VMEM),
            (shape((rows, KVRANK + LANES)), VMEM),
        ],
        [],
        20 * rows * LAT_COLS,
        4 << 20,
        "latent_norms",
        waits=waits,
    )


def masked_blocks(scores, place, rows, blocks):
    key_row = lax.broadcasted_iota(jnp.int32, (rows, rows), 0)
    query_column = lax.broadcasted_iota(jnp.int32, (rows, rows), 1)
    out = [jnp.where(key_row <= query_column, scores[:rows], NEGATIVE)]
    for block in range(1, blocks):
        seen = (place ^ block) < place
        out.append(jnp.where(seen, scores[block * rows : (block + 1) * rows], NEGATIVE))
    return out


def head_lanes(index):
    return pl.ds(pl.multiple_of(index * 2 * LANES, 2 * LANES), 2 * LANES)


def up_copies(where_ref, refs, wq, wkv, sems, n_ctx):
    if len(refs) == 3:
        return [
            pltpu.make_async_copy(refs[0], wq, sems.at[0]),
            pltpu.make_async_copy(refs[1], wkv, sems.at[1]),
        ]
    shards = len(refs) // 2
    query_rows = QRANK // shards
    low_rows = KVRANK // shards
    refs = refs[:shards]
    return row_copies(where_ref, refs, 0, query_rows, wq, sems, 0, n_ctx) + row_copies(
        where_ref, refs, query_rows, low_rows, wkv, sems, shards, n_ctx
    )


def out_copies(where_ref, refs, target, sems, first_sem, n_ctx):
    if len(refs) == 3:
        return [pltpu.make_async_copy(refs[2], target, sems.at[first_sem])]
    refs = refs[len(refs) // 2 :]
    return row_copies(where_ref, refs, 0, refs[0].shape[0], target, sems, first_sem, n_ctx)


def sequence_refs(source):
    return [piece for group in source for piece in group]


def sequence_shape(source):
    return (4 * len(source),) + source[0][0].shape


def sequence_copies(where, refs, target, rows, width, sems, first_sem):
    return [
        feature_copies(
            where, refs[at : at + 4], target, at // 4 * rows, rows, width, sems, first_sem + at
        )
        for at in range(0, len(refs), 4)
    ]


def hidden_copies(where, arrays, target, sems, first_sem, n_ctx, columns=None):
    cut = (lambda ref: ref) if columns is None else (lambda ref: ref.at[:, columns])
    if len(arrays) == 1:
        return [pltpu.make_async_copy(cut(arrays[0]), target, sems.at[first_sem])]
    rows = arrays[0].shape[0]
    parts = target.shape[0] // (rows * 2 * n_ctx)
    out = []
    for number, ref in enumerate(arrays):
        part, index = number // (2 * n_ctx), number % (2 * n_ctx)
        start = shard_place(where, index, n_ctx) * parts + part
        start = pl.multiple_of(start * rows, SUBLANES)
        out.append(
            pltpu.make_async_copy(
                cut(ref), target.at[pl.ds(start, rows), :], sems.at[first_sem + number]
            )
        )
    return out


def attention_forward(where, query_low, payloads, ups, tables, heads, n_ctx, waits=()):
    rows = query_low.shape[0]
    blocks = len(payloads)
    keys = blocks * rows
    pairs = heads // 2
    whole = lambda dims: pl.BlockSpec(dims, lambda i: (0, 0))
    column = lambda dims: pl.BlockSpec(dims, lambda i: (0, i))

    def body(where_ref, low_q, cos_t, lower_t, upper_t, *rest):
        sources = rest[:blocks]
        up_refs = rest[blocks : blocks + len(ups)]
        out, q_out, kv_out, lse_out, wq, wkv, tokens, sems = rest[blocks + len(ups) :]
        step = pl.program_id(0)

        @pl.when(step == 0)
        def _():
            copies = up_copies(where_ref, up_refs, wq, wkv, sems, n_ctx)
            first = len(copies)
            for block, source in enumerate(sources):
                copies.append(
                    pltpu.make_async_copy(
                        source, tokens.at[pl.ds(block * rows, rows), :], sems.at[first + block]
                    )
                )
            at_once(copies)

        key_lane = lax.broadcasted_iota(jnp.int32, (keys, LANES), 1)
        raw_pair = product(low_q[...], wq[:, head_lanes(step)])
        kv_pair = product(tokens[:, :KVRANK], wkv[:, head_lanes(step)]).astype(BF16)
        rope_key = tokens[:, KVRANK:]
        kv_out[...] = kv_pair
        outs = []
        for head in range(2):
            lanes = slice(head * LANES, (head + 1) * LANES)
            query = turn_lanes(
                raw_pair[:, lanes], cos_t[...], lower_t[...], upper_t[...], 1.0
            ).astype(BF16)
            pair = kv_pair[:, lanes]
            key = jnp.where(key_lane < NOPE, pair, rope_key)
            q_out[:, lanes] = query
            scores = times_transposed(key, query) * SCORE
            masked = masked_blocks(scores, where_ref[1], rows, blocks)
            top = functools.reduce(
                jnp.maximum, [jnp.max(part, axis=0, keepdims=True) for part in masked]
            )
            powers = [jnp.exp(part - top) for part in masked]
            total = sum(jnp.sum(part, axis=0, keepdims=True) for part in powers)
            prob = jnp.concatenate([part.astype(BF16) for part in powers], axis=0)
            mixed = transposed_times(pair, prob) / total
            outs.append(jnp.transpose(mixed))
            lse_out[0, head : head + 1, :] = top + jnp.log(total)
        lane = lax.broadcasted_iota(jnp.int32, (rows, LANES), 1)
        out[...] = jnp.where(lane < VDIM, pltpu.roll(outs[0], VDIM, 1), outs[1]).astype(BF16)

    return run_kernel(
        body,
        [(where, SMEM), (query_low, whole(query_low.shape))]
        + [(table, whole(table.shape)) for table in tables]
        + [(a, ANY) for a in list(payloads) + list(ups)],
        [
            (shape((rows, pairs * LANES)), column((rows, LANES))),
            (shape((rows, heads * LANES)), column((rows, 2 * LANES))),
            (shape((keys, heads * LANES)), column((keys, 2 * LANES))),
            (shape((pairs, 8, rows), F32), pl.BlockSpec((1, 8, rows), lambda i: (i, 0, 0))),
        ],
        [
            pltpu.VMEM((QRANK, heads * LANES), BF16),
            pltpu.VMEM((KVRANK, heads * LANES), BF16),
            pltpu.VMEM((keys, KVRANK + LANES), BF16),
            pltpu.SemaphoreType.DMA((64 + blocks,)),
        ],
        2 * heads * rows * (QRANK + 2 * keys) * LANES + 2 * heads * keys * KVRANK * LANES,
        12 << 20,
        "attention_forward",
        grid=(pairs,),
        exps=heads * rows * keys,
        waits=waits,
    )


def attention_backward(where, queries, pairs_low, lse, payloads, ups, branch, tables, n_ctx, waits=()):
    rows, q_lanes = queries.shape
    heads = q_lanes // LANES
    pairs = heads // 2
    blocks = len(payloads)
    keys = blocks * rows
    width = branch[0].shape[1]
    full_width = 4 * width
    inner = heads * VDIM
    whole = lambda dims: pl.BlockSpec(dims, lambda i: (0, 0))
    column = lambda dims: pl.BlockSpec(dims, lambda i: (0, i))
    moved = list(payloads) + list(ups) + list(branch)

    def body(where_ref, q_in, kv_in, lse_in, cos_t, lower_t, upper_t, *rest):
        refs = rest[: len(moved)]
        (dq_out, dkv_out, query_sum, kv_keep, kv_1, kv_2, kv_3) = rest[len(moved) : len(moved) + 7]
        wq, wkv, rope_key, wo, grad_in, dout, kv_sum, sems = rest[len(moved) + 7 :]
        step = pl.program_id(0)
        place = where_ref[1]

        @pl.when(step == 0)
        def _():
            at = 0
            sources, at = refs[at : at + blocks], at + blocks
            up_refs, at = refs[at : at + len(ups)], at + len(ups)
            branch_refs = refs[at : at + 4]
            copies = up_copies(where_ref, up_refs, wq, wkv, sems, n_ctx)
            for block, source in enumerate(sources):
                copies.append(
                    pltpu.make_async_copy(
                        source.at[:, pl.ds(KVRANK, LANES)],
                        rope_key.at[pl.ds(block * rows, rows), :],
                        sems.at[len(copies)],
                    )
                )
            copies += feature_copies(
                where_ref, branch_refs, grad_in, 0, rows, width, sems, len(copies)
            )
            copies += out_copies(where_ref, up_refs, wo, sems, len(copies), n_ctx)
            at_once(copies)
            dout[...] = product(grad_in[...], wo[...]).astype(BF16).astype(F32)
            query_sum[...] = jnp.zeros_like(query_sum)
            kv_sum[...] = jnp.zeros_like(kv_sum)

        key_lane = lax.broadcasted_iota(jnp.int32, (keys, LANES), 1)
        lane = lax.broadcasted_iota(jnp.int32, (rows, LANES), 1)
        both = dout[:, pl.ds(pl.multiple_of(step * LANES, LANES), LANES)]
        dkr = jnp.zeros((keys, LANES), F32)
        dq_parts = []
        dkv_parts = []
        for head in range(2):
            lanes = slice(head * LANES, (head + 1) * LANES)
            query = q_in[:, lanes]
            pair = kv_in[:, lanes]
            key = jnp.where(key_lane < NOPE, pair, rope_key[...])
            upper = pltpu.roll(both, VDIM, 1) if head == 0 else both
            out_grad = jnp.where(lane >= NOPE, upper, 0.0).astype(BF16)
            scores = times_transposed(key, query) * SCORE
            top = lse_in[0, head : head + 1, :]
            masked = masked_blocks(scores, place, rows, blocks)
            prob = jnp.concatenate([jnp.exp(part - top) for part in masked], axis=0)
            prob_grad = times_transposed(pair, out_grad)
            weighted = prob * prob_grad
            delta = jnp.sum(weighted, axis=0, keepdims=True)
            score_grad = (weighted - prob * delta).astype(BF16)
            key_grad = product(score_grad, query) * SCORE
            value_grad = product(prob.astype(BF16), out_grad)
            dkv_parts.append(jnp.where(key_lane < NOPE, key_grad, value_grad).astype(BF16))
            dkr = dkr + key_grad
            query_grad = jnp.transpose(transposed_times(key, score_grad)) * SCORE
            dq_parts.append(
                turn_lanes(query_grad, cos_t[...], lower_t[...], upper_t[...], -1.0).astype(BF16)
            )
        dq_pair = jnp.concatenate(dq_parts, axis=1)
        dkv_pair = jnp.concatenate(dkv_parts, axis=1)
        dq_out[...] = dq_pair
        dkv_out[...] = dkv_pair
        query_sum[...] += times_transposed(dq_pair, wq[:, head_lanes(step)])
        kv_sum[:, :KVRANK] += times_transposed(dkv_pair, wkv[:, head_lanes(step)])
        kv_sum[:, KVRANK:] += jnp.where(key_lane >= NOPE, dkr, 0.0)

        @pl.when(step == pairs - 1)
        def _():
            kv_keep[...] = kv_sum[:rows]
            for block, out in ((1, kv_1), (2, kv_2), (3, kv_3)):
                out[...] = kv_sum[block * rows : (block + 1) * rows].astype(BF16)

    return run_kernel(
        body,
        [
            (where, SMEM),
            (queries, column((rows, 2 * LANES))),
            (pairs_low, column((keys, 2 * LANES))),
            (lse, pl.BlockSpec((1, 8, rows), lambda i: (i, 0, 0))),
        ]
        + [(table, whole(table.shape)) for table in tables]
        + [(a, ANY) for a in moved],
        [
            (shape((rows, heads * LANES)), column((rows, 2 * LANES))),
            (shape((keys, heads * LANES)), column((keys, 2 * LANES))),
            (shape((rows, QRANK), F32), whole((rows, QRANK))),
            (shape((rows, KVRANK + LANES), F32), whole((rows, KVRANK + LANES))),
        ]
        + [(shape((rows, KVRANK + LANES)), whole((rows, KVRANK + LANES)))] * 3,
        [
            pltpu.VMEM((QRANK, heads * LANES), BF16),
            pltpu.VMEM((KVRANK, heads * LANES), BF16),
            pltpu.VMEM((keys, LANES), BF16),
            pltpu.VMEM((full_width, inner), BF16),
            pltpu.VMEM((rows, full_width), BF16),
            pltpu.VMEM((rows, inner), F32),
            pltpu.VMEM((keys, KVRANK + LANES), F32),
            pltpu.SemaphoreType.DMA((128 + blocks,)),
        ],
        10 * heads * rows * keys * LANES,
        24 << 20,
        "attention_backward",
        grid=(pairs,),
        exps=heads * rows * keys,
        waits=waits,
    )


def output_products(where, attended, ups, full_width, n_ctx, waits=()):
    rows, inner = attended.shape
    count = len(ups)
    width = full_width // 4

    def body(where_ref, attended_ref, *rest):
        refs = rest[:count]
        keep, send, weight, sems = rest[count:]
        at_once(out_copies(where_ref, refs, weight, sems, 0, n_ctx))
        for place in range(4):
            block = weight[pl.ds(feature_start(where_ref, place, width), width), :]
            part = times_transposed(attended_ref[...], block)
            if place % 2 == 0:
                keep[place // 2] = part
            else:
                send[place // 2] = part.astype(BF16)

    return run_kernel(
        body,
        [(where, SMEM), (attended, VMEM)] + [(a, ANY) for a in ups],
        [(shape((2, rows, width), F32), VMEM), (shape((2, rows, width)), VMEM)],
        [pltpu.VMEM((full_width, inner), BF16), pltpu.SemaphoreType.DMA((64,))],
        2 * rows * inner * full_width,
        6 << 20,
        "output_products",
        waits=waits,
    )


def feed_forward(where, tokens, branches, weights, gains, hidden, n_ctx):
    count, rows, width = sequence_shape(tokens)
    blocks = count // 4
    full_width = 4 * width
    columns = weights[0].shape[-1]
    upper_end = round_up(2 * hidden, LANES)
    lower_start = 2 * hidden // LANES * LANES
    shift = 2 * hidden - lower_start
    lower_cols = columns - lower_start
    total = blocks * rows
    token_list, branch_list = sequence_refs(tokens), sequence_refs(branches)
    flat = len(token_list) + len(branch_list)
    moved = token_list + branch_list + list(gains) + list(weights)

    def body(where_ref, *rest):
        refs = rest[: len(moved)]
        pairs_out, active_out, keep, send, inverse_out = rest[len(moved) : len(moved) + 5]
        normed, branch, weight, gain, sems = rest[len(moved) + 5 :]
        first = 2 * count
        weight_copies = feature_copies(
            where_ref, refs[flat : flat + 4], gain, 0, gain.shape[0], width, sems, first
        ) + hidden_copies(where_ref, refs[flat + 4 :], weight, sems, first + 4, n_ctx)
        token_copies = [
            first_list + second_list
            for first_list, second_list in zip(
                sequence_copies(
                    where_ref, refs[: len(token_list)], normed, rows, width, sems, 0
                ),
                sequence_copies(
                    where_ref, refs[len(token_list) : flat], branch, rows, width, sems, count
                ),
            )
        ]
        for copy in weight_copies + sum(token_copies, []):
            copy.start()
        for copy in weight_copies:
            copy.wait()

        def hidden_block(block, carry):
            for number, copies in enumerate(token_copies):

                @pl.when(block == number)
                def _():
                    for copy in copies:
                        copy.wait()

            here = pl.ds(pl.multiple_of(block * rows, rows), rows)
            source = normed[here, :].astype(F32) / gain[:1, :]
            inverse = lax.rsqrt(jnp.mean(source * source, axis=1, keepdims=True) + EPSILON)

            @pl.when(block == 0)
            def _():
                inverse_out[...] = jnp.broadcast_to(inverse, inverse_out.shape)

            both = product(normed[here, :], weight[:, :upper_end]) * inverse
            lower = product(branch[here, :], weight[:, lower_start:])
            gate = both[:, :hidden]
            upper = both[:, hidden : 2 * hidden]
            grad = lower[:, shift : shift + hidden]
            scaled = grad * inverse
            sigmoid = 1.0 / (1.0 + jnp.exp(-gate))
            active = gate * sigmoid
            pairs_out[here, :] = jnp.concatenate(
                [
                    scaled * upper * sigmoid * (1.0 + gate * (1.0 - sigmoid)),
                    scaled * active,
                    jnp.zeros((rows, upper_end - 2 * hidden), F32),
                ],
                axis=1,
            ).astype(BF16)
            active_out[here, :] = jnp.concatenate(
                [
                    jnp.zeros((rows, shift), F32),
                    active * upper,
                    jnp.zeros((rows, lower_cols - shift - hidden), F32),
                ],
                axis=1,
            ).astype(BF16)
            return carry

        lax.fori_loop(0, blocks, hidden_block, 0)
        for place in range(4):
            block = weight[pl.ds(feature_start(where_ref, place, width), width), :upper_end]
            part = times_transposed(pairs_out[...], block).astype(BF16)
            (send if place % 2 else keep)[place // 2] = part

    return run_kernel(
        body,
        [(where, SMEM)] + [(a, ANY) for a in moved],
        [
            (shape((total, upper_end)), VMEM),
            (shape((total, lower_cols)), VMEM),
            (shape((2, total, width)), VMEM),
            (shape((2, total, width)), VMEM),
            (shape((rows, LANES), F32), VMEM),
        ],
        [
            pltpu.VMEM((total, full_width), BF16),
            pltpu.VMEM((total, full_width), BF16),
            pltpu.VMEM((full_width, columns), BF16),
            pltpu.VMEM(gains[0].shape[:1] + (full_width,), F32),
            pltpu.SemaphoreType.DMA((2 * count + 4 + full_width // SUBLANES,)),
        ],
        10 * total * full_width * hidden,
        28 << 20,
        "feed_forward",
        exps=total * hidden,
    )


def feed_forward_result(where, active, weights, hidden, n_ctx, waits=()):
    total, lower_cols = active.shape
    columns = weights[0].shape[1]
    full_width = sum(a.shape[0] for a in weights)
    width = full_width // 4
    count = len(weights)

    def body(where_ref, active_ref, *rest):
        refs = rest[:count]
        outs = rest[count:-2]
        weight, sems = rest[-2:]
        lower = pl.ds(columns - lower_cols, lower_cols)
        at_once(hidden_copies(where_ref, refs, weight, sems, 0, n_ctx, columns=lower))
        for place in range(4):
            block = weight[pl.ds(feature_start(where_ref, place, width), width), :]
            part = times_transposed(active_ref[...], block).astype(BF16)
            outs[place % 2][place // 2] = part

    return run_kernel(
        body,
        [(where, SMEM), (active, VMEM)] + [(a, ANY) for a in weights],
        [(shape((2, total, width)), VMEM)] * 2,
        [
            pltpu.VMEM((full_width, lower_cols), BF16),
            pltpu.SemaphoreType.DMA((full_width // SUBLANES,)),
        ],
        2 * total * full_width * hidden,
        10 << 20,
        "feed_forward_result",
        waits=waits,
    )


def feed_forward_grads(
    where, tokens, branches, pairs_grad, active, hidden, columns, shards, n_ctx, distance, waits=()
):
    count, rows, width = sequence_shape(tokens)
    token_list, branch_list = sequence_refs(tokens), sequence_refs(branches)
    total = count // 4 * rows
    upper_end = pairs_grad.shape[1]
    lower_cols = active.shape[1]
    lower_start = columns - lower_cols
    shard_rows = 4 * width // shards

    def gradient(normed, branch, pairs_ref, active_ref):
        first = transposed_times(normed, pairs_ref[...])
        second = transposed_times(branch, active_ref[...])
        middle = first[:, lower_start:] + second[:, : upper_end - lower_start]
        return jnp.concatenate(
            [first[:, :lower_start], middle, second[:, upper_end - lower_start :]], axis=1
        ).astype(BF16)

    def body(where_ref, pairs_ref, active_ref, *rest):
        token_refs, rest = rest[: len(token_list)], rest[len(token_list) :]
        branch_refs, rest = rest[: len(branch_list)], rest[len(branch_list) :]
        outs = rest[:-4]
        normed, branch, stage, sems = rest[-4:]
        copies = sequence_copies(where_ref, token_refs, normed, rows, width, sems, 0)
        copies += sequence_copies(where_ref, branch_refs, branch, rows, width, sems, count)
        at_once(sum(copies, []))
        if distance is None:
            for place in range(4):
                here = slice(place * width, (place + 1) * width)
                outs[0][here, :] = gradient(normed[:, here], branch[:, here], pairs_ref, active_ref)
            return
        for number in range(n_ctx // 2):
            place = owner_blocks(where_ref, distance * (n_ctx // 2) + number, n_ctx)
            here = pl.ds(pl.multiple_of(place * width, LANES), width)
            stage[...] = gradient(normed[:, here], branch[:, here], pairs_ref, active_ref)
            for low in range(2):
                start = pl.multiple_of((low ^ (where_ref[1] % 2)) * shard_rows, SUBLANES)
                outs[2 * number + low][...] = stage[pl.ds(start, shard_rows), :]

    if distance is None:
        outputs = [(shape((4 * width, columns)), VMEM)]
    else:
        outputs = [(shape((shard_rows, columns)), VMEM)] * n_ctx
    return run_kernel(
        body,
        [(where, SMEM), (pairs_grad, VMEM), (active, VMEM)]
        + [(a, ANY) for a in token_list + branch_list],
        outputs,
        [
            pltpu.VMEM((total, 4 * width), BF16),
            pltpu.VMEM((total, 4 * width), BF16),
            pltpu.VMEM((width, columns), BF16),
            pltpu.SemaphoreType.DMA((2 * count,)),
        ],
        6 * total * 4 * width * hidden // 2,
        18 << 20,
        "feed_forward_grads",
        waits=waits,
    )


def owner_blocks(where_ref, part, n_ctx):
    per_row = n_ctx // 2
    return (where_ref[0] ^ (part // per_row)) * per_row + ((where_ref[1] // 2) ^ (part % per_row))


def output_grads(where, attended, branch, shards, n_ctx, paired, waits=()):
    rows, inner = attended.shape
    width = branch[0].shape[1]
    shard_rows = 4 * width // shards

    def body(where_ref, attended_ref, b0, b1, b2, b3, *rest):
        outs = rest[:-3]
        grad_in, stage, sems = rest[-3:]
        at_once(feature_copies(where_ref, (b0, b1, b2, b3), grad_in, 0, rows, width, sems, 0))
        for part in range(4):
            place = owner_blocks(where_ref, part, n_ctx) if paired else part
            here = pl.ds(pl.multiple_of(place * width, LANES), width)
            stage[...] = transposed_times(grad_in[:, here], attended_ref[...]).astype(BF16)
            if not paired:
                outs[0][part * width : (part + 1) * width, :] = stage[...]
                continue
            for low in range(2):
                start = pl.multiple_of((low ^ (where_ref[1] % 2)) * shard_rows, SUBLANES)
                outs[2 * part + low][...] = stage[pl.ds(start, shard_rows), :]

    if paired:
        outputs = [(shape((shard_rows, inner)), VMEM)] * shards
    else:
        outputs = [(shape((4 * width, inner)), VMEM)]
    return run_kernel(
        body,
        [(where, SMEM), (attended, VMEM)] + [(a, ANY) for a in branch],
        outputs,
        [
            pltpu.VMEM((rows, 4 * width), BF16),
            pltpu.VMEM((width, inner), BF16),
            pltpu.SemaphoreType.DMA((4,)),
        ],
        2 * rows * inner * 4 * width,
        6 << 20,
        "output_grads",
        waits=waits,
    )


def up_grads(where, query_low, query_grad, payloads, pair_grad, shards, n_ctx, paired, waits=()):
    rows = query_low.shape[0]
    blocks = len(payloads)
    lanes = query_grad.shape[1]
    query_rows = QRANK // shards
    low_rows = KVRANK // shards

    def body(where_ref, low_q, dq, dkv, *rest):
        sources = rest[:blocks]
        rest = rest[blocks:]
        outs = rest[:-4]
        tokens, stage_q, stage_kv, sems = rest[-4:]
        at_once(
            [
                pltpu.make_async_copy(
                    source.at[:, pl.ds(0, KVRANK)],
                    tokens.at[pl.ds(block * rows, rows), :],
                    sems.at[block],
                )
                for block, source in enumerate(sources)
            ]
        )
        grad_q = transposed_times(low_q[...], dq[...]).astype(BF16)
        grad_kv = transposed_times(tokens[...], dkv[...]).astype(BF16)
        if not paired:
            outs[0][...] = grad_q
            outs[1][...] = grad_kv
            return
        stage_q[...] = grad_q
        stage_kv[...] = grad_kv
        for index, out in enumerate(outs):
            place = shard_place(where_ref, index, n_ctx)
            out[:query_rows, :] = stage_q[
                pl.ds(pl.multiple_of(place * query_rows, SUBLANES), query_rows), :
            ]
            out[query_rows:, :] = stage_kv[
                pl.ds(pl.multiple_of(place * low_rows, SUBLANES), low_rows), :
            ]

    if paired:
        outputs = [(shape((query_rows + low_rows, lanes)), VMEM)] * shards
    else:
        outputs = [(shape((QRANK, lanes)), VMEM), (shape((KVRANK, lanes)), VMEM)]
    return run_kernel(
        body,
        [(where, SMEM), (query_low, VMEM), (query_grad, VMEM), (pair_grad, VMEM)]
        + [(a, ANY) for a in payloads],
        outputs,
        [
            pltpu.VMEM((blocks * rows, KVRANK), BF16),
            pltpu.VMEM((QRANK, lanes), BF16),
            pltpu.VMEM((KVRANK, lanes), BF16),
            pltpu.SemaphoreType.DMA((blocks,)),
        ],
        2 * lanes * (rows * QRANK + blocks * rows * KVRANK),
        10 << 20,
        "up_grads",
        waits=waits,
    )


def input_backward(
    where,
    mine,
    other,
    latent,
    gain_query,
    gain_latent,
    tables,
    normed,
    joined,
    activations,
    inverse_one,
    gain_one,
    middle_grad,
    pick,
    query_rows,
    low_rows,
    shards,
    n_ctx,
    paired,
    waits=(),
):
    half = mine.shape[0]
    rows, width = normed.shape
    full_width = 4 * width
    low_in = pick.shape[1]

    def body(
        where_ref, mine_ref, other_ref, latent_ref, gq, gl, cos_t, lower_t, upper_t, normed_ref,
        joined_ref, act_ref, inverse_ref, gain_ref, middle_ref, pick_ref, input_out, query_gain_out,
        latent_gain_out, gain_out, *rest
    ):
        outs = rest[:-3]
        sums, stage_q, stage_low = rest[-3:]
        core = where_ref[3]
        sums[pl.ds(pl.multiple_of(core * half, 8), half), :] = mine_ref[...]
        sums[pl.ds(pl.multiple_of((1 - core) * half, 8), half), :] = other_ref[...]
        parts = []
        for first, last, gain, out in (
            (0, QRANK, gq, query_gain_out),
            (QRANK, LATENT, gl, latent_gain_out),
        ):
            source = latent_ref[:, first:last]
            grad = sums[:, first:last]
            inverse = lax.rsqrt(jnp.mean(source * source, axis=1, keepdims=True) + EPSILON)
            out[...] = jnp.sum(grad * source * inverse, axis=0, keepdims=True)
            scaled = grad * gain[...]
            inner = jnp.mean(scaled * source, axis=1, keepdims=True)
            parts.append(inverse * scaled - source * (inverse * inverse * inverse * inner))
        rope = turn_lanes(sums[:, LATENT:], cos_t[...], lower_t[...], upper_t[...], -1.0)
        parts.append(pltpu.roll(rope, LANES - NOPE, 1))
        latent_grad = jnp.concatenate(parts, axis=1)
        low = latent_grad.astype(BF16)
        down_grad = transposed_times(low, normed_ref[...]).astype(BF16)
        if paired:
            stage_q[...] = down_grad[:QRANK]
            gains = [
                jnp.concatenate(
                    [
                        query_gain_out[:, i * query_rows : (i + 1) * query_rows],
                        latent_gain_out[:, i * KVRANK // shards : (i + 1) * KVRANK // shards],
                        jnp.zeros((1, width - LANES), F32),
                    ],
                    axis=1,
                )
                for i in range(shards)
            ]
            first = LATENT + ROPE - QRANK
            low_part = jnp.concatenate(
                [
                    down_grad[QRANK : LATENT + ROPE].astype(F32),
                    jnp.concatenate(gains, axis=0),
                    jnp.zeros((LOW_ROWS - first - shards, width), F32),
                ],
                axis=0,
            ).astype(BF16)
            stage_low[...] = transposed_times(pick_ref[...], low_part).astype(BF16)
            for index, out in enumerate(outs):
                place = shard_place(where_ref, index, n_ctx)
                out[:query_rows, :] = stage_q[
                    pl.ds(pl.multiple_of(place * query_rows, SUBLANES), query_rows), :
                ]
                out[query_rows:, :] = stage_low[
                    pl.ds(pl.multiple_of(place * low_rows, SUBLANES), low_rows), :
                ]
        else:
            outs[0][...] = down_grad
        row_inner = jnp.sum(latent_grad * latent_ref[...], axis=1, keepdims=True)
        normed_grad = product(low, joined_ref[...])
        source = act_ref[...].astype(F32)
        inverse = inverse_ref[...]
        gain_out[...] = jnp.sum(normed_grad * source * inverse, axis=0, keepdims=True)
        input_out[...] = (
            middle_ref[...]
            + inverse * (normed_grad * gain_ref[...])
            - source * (inverse * inverse * row_inner / full_width)
        )

    if paired:
        outputs = [(shape((query_rows + low_rows, width)), VMEM)] * shards
    else:
        outputs = [(shape((LAT_COLS, width)), VMEM)]
    arrays = (mine, other, latent, gain_query, gain_latent) + tables
    arrays += (normed, joined, activations, inverse_one, gain_one, middle_grad, pick)
    return run_kernel(
        body,
        [(where, SMEM)] + [(a, VMEM) for a in arrays],
        [
            (shape((rows, width), F32), VMEM),
            (shape((1, QRANK), F32), VMEM),
            (shape((1, KVRANK), F32), VMEM),
            (shape((1, width), F32), VMEM),
        ]
        + outputs,
        [
            pltpu.VMEM((rows, LAT_COLS), F32),
            pltpu.VMEM((QRANK, width), BF16),
            pltpu.VMEM((low_in, width), BF16),
        ],
        4 * rows * width * LAT_COLS,
        12 << 20,
        "input_backward",
        waits=waits,
    )


def pick_matrix(columns, rows_each, valid):
    matrix = np.zeros((LOW_ROWS, columns), np.float32)
    for row in range(KVRANK + ROPE):
        matrix[row, row // valid * rows_each + row % valid] = 1.0
    for shard in range(columns // rows_each if rows_each > valid else 0):
        matrix[KVRANK + ROPE + shard, shard * rows_each + valid] = 1.0
    return jnp.asarray(matrix, BF16)


def per_device(
    activations,
    attn_gain,
    query_down,
    latent_down,
    query_gain,
    latent_gain,
    query_up,
    latent_up,
    attn_output,
    ffn_gain,
    ffn_gate,
    ffn_up,
    ffn_down,
    out_grad,
):
    n_fsdp = lax.axis_size("fsdp")
    n_ctx = lax.axis_size("ctx")
    n_tp = lax.axis_size("tp")
    shards = n_fsdp * n_ctx
    paired = n_fsdp == 2 and shards == 2 * n_tp
    rows, width = activations.shape
    full_width = width * n_tp
    fsdp_index = lax.axis_index("fsdp").astype(jnp.int32)
    ctx_index = lax.axis_index("ctx").astype(jnp.int32)
    tp_index = lax.axis_index("tp").astype(jnp.int32)
    shard_index = fsdp_index * n_ctx + ctx_index
    where = jnp.stack([fsdp_index, ctx_index, tp_index, tp_index % 2])
    local_heads = query_up.shape[1] // (NOPE + ROPE)
    hidden = ffn_gate.shape[1] // n_ctx
    columns = round_up(3 * hidden, LANES)
    q_shard = query_down.shape[1]
    low_shard = latent_down.shape[1]
    both_axes = ("fsdp", "ctx")

    def spread_shards(own):
        pieces = spread_ctx(own)
        return pieces + [swap(piece, "fsdp", 1) for piece in pieces]

    def fold_shards(parts):
        return [
            (parts[k].astype(F32) + swap(parts[n_ctx + k], "fsdp", 1).astype(F32)).astype(BF16)
            for k in range(n_ctx)
        ]

    def gather_rows(value):
        return lax.all_gather(value, both_axes, axis=0, tiled=True)

    def scatter_rows(value):
        return lax.psum_scatter(value, both_axes, scatter_dimension=0, tiled=True).astype(F32)

    def spread_sequence(own):
        return [spread_tp(block) for block in spread_ctx(own)]

    inputs = activations.astype(F32)
    gain_one = attn_gain.astype(F32)
    row_sums = total_tp(jnp.sum(inputs * inputs, axis=1))
    inverse_one = lax.rsqrt(row_sums / full_width + EPSILON)
    gain_two = ffn_gain.astype(F32)
    gains_two = spread_tp(jnp.broadcast_to(gain_two[None, :], (8, width)))
    normed_low = (inputs * inverse_one[:, None] * gain_one).astype(BF16)

    query_pad = jnp.pad(
        query_up.reshape(query_up.shape[0], local_heads, NOPE + ROPE),
        ((0, 0), (0, 0), (0, LANES - NOPE - ROPE)),
    ).reshape(query_up.shape[0], local_heads * LANES)
    if paired:
        low_rows = round_up(low_shard, SUBLANES)
        pick = pick_matrix(shards * low_rows, low_rows, low_shard)
        down_own = jnp.concatenate(
            [
                query_down.T,
                latent_down.T,
                jnp.pad(
                    jnp.concatenate([query_gain, latent_gain])[None, :],
                    ((0, low_rows - low_shard - 1), (0, width - LANES)),
                ),
            ]
        )
        query_pieces = low_pieces = spread_shards(down_own)
        first_low = q_shard
        ups = spread_shards(jnp.concatenate([query_pad, latent_up])) + spread_shards(attn_output.T)
    else:
        low_rows = low_shard
        pick = pick_matrix(LOW_ROWS, KVRANK + ROPE, KVRANK + ROPE)
        query_pieces = [gather_rows(query_down.T)]
        low_pieces = [
            jnp.pad(gather_rows(latent_down.T), ((0, LOW_ROWS - KVRANK - ROPE), (0, 0)))
        ]
        first_low = 0
        ups = [gather_rows(query_pad), gather_rows(latent_up), gather_rows(attn_output.T)]

    parts = 2 if paired else 1
    chunks = cut_hidden(where, ffn_gate, ffn_up, ffn_down, parts=parts)
    if paired:
        sent = {(part, k): chunks[n_ctx * part + k] for part in range(parts) for k in range(1, n_ctx)}
        order = [[(part, k) for k in group] for part in range(parts) for group in ((2, 1), (3,))]
        _, got = in_turn(sent, order, lambda key, value: swap(value, "ctx", key[1]))
        got.update({(part, 0): chunks[n_ctx * part] for part in range(parts)})
        order = [[(part, 0)] for part in range(parts)]
        order += [[(part, k)] for part in range(parts) for k in range(1, n_ctx)]
        got, crossed = in_turn(got, order, lambda key, value: swap(value, "fsdp", 1))
        weights = []
        for part in range(parts):
            weights += [got[part, k] for k in range(n_ctx)]
            weights += [crossed[part, k] for k in range(n_ctx)]
    else:
        stack = jnp.stack(exchange_ctx(chunks))
        stack = jnp.stack(
            [
                lax.dynamic_index_in_dim(stack, ctx_index ^ k, 0, keepdims=False)
                for k in range(n_ctx)
            ]
        )
        weights = [lax.all_gather(stack, "fsdp", axis=0).reshape(full_width, columns)]

    upstream = out_grad.astype(F32)
    branches = spread_sequence((RESID * upstream).astype(BF16))

    keep, send, joined, gain_query, gain_latent = latent_products(
        where,
        normed_low,
        pick,
        query_pieces,
        low_pieces,
        q_shard,
        low_rows,
        first_low,
        n_ctx,
        paired,
        waits=list(chunks[:1]) + ups[1:2],
    )
    if not paired:
        gains = jnp.zeros((QRANK + KVRANK,), F32)
        gains = lax.dynamic_update_slice(
            gains, query_gain.astype(F32), (shard_index * query_gain.shape[0],)
        )
        gains = lax.dynamic_update_slice(
            gains, latent_gain.astype(F32), (QRANK + shard_index * latent_gain.shape[0],)
        )
        gains = lax.psum(gains, both_axes)
        gain_query = gains[None, :QRANK]
        gain_latent = gains[None, QRANK:]
    mine, other = fold_halves(keep, send)
    query_pos = ctx_index * rows + jnp.arange(rows, dtype=jnp.int32)
    tables = lane_tables(*rotary_tables(query_pos.astype(F32)))
    latent, query_low, payload = latent_norms(where, mine, other, gain_query, gain_latent, tables)
    payloads = spread_ctx(payload)

    attended, queries_low, pairs_low, lse = attention_forward(
        where, query_low, payloads, ups, tables, local_heads, n_ctx
    )

    def fold_tp(keep, send):
        got = swap(send, "tp", 1)
        far = (keep[1].astype(F32) + got[1].astype(F32)).astype(BF16)
        near = keep[0].astype(F32) + got[0].astype(F32)
        return near + swap(far, "tp", 2).astype(F32)

    keep, send = output_products(where, attended, ups, full_width, n_ctx)
    middle = inputs + RESID * fold_tp(keep, send)

    tokens = spread_sequence((middle * gain_two).astype(BF16))
    pairs_grad, active, keep, send, inverse_two = feed_forward(
        where, tokens, branches, weights, gains_two, hidden, n_ctx
    )
    inverse_two = inverse_two[:, :1]

    def fold_sequence(keep, send):
        got = swap(send, "tp", 1)
        totals = []
        for block in reversed(range(n_ctx)):
            here = slice(block * rows, (block + 1) * rows)
            far = (keep[1, here].astype(F32) + got[1, here].astype(F32)).astype(BF16)
            near = keep[0, here].astype(F32) + got[0, here].astype(F32)
            totals.append(near + swap(far, "tp", 2).astype(F32))
        return sum_ctx(totals[::-1])

    second_grad = fold_sequence(keep, send)
    scaled_two = second_grad * gain_two
    grad_gain_two = jnp.sum(second_grad * middle, axis=0)
    inner_two = lax.psum(jnp.sum(scaled_two * middle, axis=1), "tp") / full_width
    middle_grad = upstream + scaled_two - middle * (inverse_two * inverse_two * inner_two[:, None])
    branch = spread_tp((RESID * middle_grad).astype(BF16))

    result = middle + RESID * fold_sequence(
        *feed_forward_result(where, active, weights, hidden, n_ctx)
    )
    grads = functools.partial(
        feed_forward_grads, where, tokens, branches, pairs_grad, active, hidden, columns, shards, n_ctx
    )
    if paired:
        sent, kept = grads(1), grads(0)
        moved = [swap(sent[k], "fsdp", 1) for k in reversed(range(n_ctx))][::-1]
        sums = [
            (kept[k].astype(F32) + moved[k].astype(F32)).astype(BF16) for k in range(n_ctx)
        ]
    else:
        total = grads(None)[0].reshape(n_fsdp, n_ctx, full_width // shards, columns)
        total = lax.psum_scatter(total, "fsdp", scatter_dimension=0, tiled=False)
        sums = [
            lax.dynamic_index_in_dim(total, ctx_index ^ k, 0, keepdims=False) for k in range(n_ctx)
        ]
    sent = {k: sums[k] for k in range(1, n_ctx)}
    _, got = in_turn(sent, ((3, 1), (2,)), lambda key, value: swap(value, "ctx", key))
    hidden_sums = [sums[0]] + [got[k] for k in range(1, n_ctx)]

    query_grad, pair_grad, query_sum, kv_keep, kv_1, kv_2, kv_3 = attention_backward(
        where, queries_low, pairs_low, lse, payloads, ups, branch, tables, n_ctx
    )
    kv_total = sum_ctx([kv_keep, kv_1, kv_2, kv_3])
    both = jnp.concatenate([query_sum, kv_total], axis=1).reshape(2, rows // 2, LAT_COLS)
    mine, other = fold_halves(
        lax.dynamic_index_in_dim(both, tp_index % 2, 0, keepdims=False),
        lax.dynamic_index_in_dim(both, 1 - tp_index % 2, 0, keepdims=False),
    )
    out_parts = output_grads(where, attended, branch, shards, n_ctx, paired)
    up_parts = up_grads(
        where, query_low, query_grad, payloads, pair_grad, shards, n_ctx, paired
    )
    if paired:
        out_sums = fold_shards(out_parts)
        up_sums = fold_shards(up_parts)
    input_grad, grad_query_gain, grad_latent_gain, grad_gain_one, *down_parts = input_backward(
        where,
        mine,
        other,
        latent,
        gain_query,
        gain_latent,
        tables,
        normed_low,
        joined,
        activations,
        inverse_one[:, None],
        gain_one[None, :],
        middle_grad,
        pick,
        q_shard,
        low_rows,
        shards,
        n_ctx,
        paired,
    )
    grad_gate, grad_up, grad_down = join_hidden(where, hidden_sums, hidden)
    if paired:
        grad_out = sum_ctx(out_sums)
        grad_ups = sum_ctx(up_sums)
        grad_query_up = grad_ups[: query_up.shape[0]]
        grad_latent_up = grad_ups[query_up.shape[0] :]
        grad_downs = sum_ctx(fold_shards(down_parts))
        grad_query_down = grad_downs[:q_shard]
        grad_latent_down = grad_downs[q_shard : q_shard + low_shard]
    else:
        grad_out = scatter_rows(out_parts[0])
        grad_query_up, grad_latent_up = scatter_rows(up_parts[0]), scatter_rows(up_parts[1])
        grad_query_down = scatter_rows(down_parts[0][:QRANK])
        grad_latent_down = scatter_rows(down_parts[0][QRANK : LATENT + ROPE])
    grad_query_up = grad_query_up.reshape(query_up.shape[0], local_heads, LANES)
    grad_query_up = grad_query_up[:, :, : NOPE + ROPE].reshape(query_up.shape)

    gain_sums = lax.psum(jnp.concatenate([grad_gain_one[0], grad_gain_two]), both_axes)
    if paired:
        gain_row = grad_downs[q_shard + low_shard]
        gain_query_sum = gain_row[:q_shard]
        gain_latent_sum = gain_row[q_shard : q_shard + latent_gain.shape[0]]
    else:
        gain_query_sum = scatter_rows(grad_query_gain[0])
        gain_latent_sum = scatter_rows(grad_latent_gain[0])
    return (
        result.astype(BF16),
        input_grad,
        gain_sums[:width],
        grad_query_down.T,
        grad_latent_down.T,
        gain_query_sum,
        gain_latent_sum,
        grad_query_up,
        grad_latent_up,
        grad_out.T,
        gain_sums[width : 2 * width],
        grad_gate,
        grad_up,
        grad_down.T,
    )


def solution(mesh):
    tokens = P(("fsdp", "ctx"), "tp")
    by_columns = P("tp", ("fsdp", "ctx"))
    by_rows = P(("fsdp", "ctx"), "tp")
    latent_vector = P(("fsdp", "ctx"))
    feature_vector = P("tp")
    weights = (
        feature_vector,
        by_columns,
        by_columns,
        latent_vector,
        latent_vector,
        by_rows,
        by_rows,
        by_columns,
        feature_vector,
        by_rows,
        by_rows,
        by_columns,
    )
    return jax.shard_map(
        per_device,
        mesh=mesh,
        in_specs=(tokens,) + weights + (tokens,),
        out_specs=(tokens, tokens) + weights,
        check_vma=False,
    )
```

```python
import functools
import math

import jax
import jax.numpy as jnp
import numpy as np
from jax import lax
from jax.experimental import pallas as pl
from jax.experimental.pallas import tpu as pltpu
from jax.sharding import PartitionSpec as P

NOPE = 64
ROPE = 32
VDIM = 64
QRANK = 768
KVRANK = 256
LANES = 128
SUBLANES = 16

RESID = 1.4 / math.sqrt(62.0)
EPSILON = 1e-05
NEGATIVE = -1e30
SCORE = 1.0 / math.sqrt(NOPE + ROPE)

F32 = jnp.float32
BF16 = jnp.bfloat16

LATENT = QRANK + KVRANK
LAT_COLS = LATENT + LANES
LOW_ROWS = LAT_COLS - QRANK


def round_up(size, unit):
    return -(-size // unit) * unit


def product(left, right):
    return jnp.dot(left, right, preferred_element_type=F32)


def times_transposed(left, right):
    return lax.dot_general(left, right, (((1,), (1,)), ((), ())), preferred_element_type=F32)


def transposed_times(left, right):
    return lax.dot_general(left, right, (((0,), (0,)), ((), ())), preferred_element_type=F32)


def rotary_tables(positions):
    exponent = jnp.arange(0, ROPE, 2, dtype=F32) / ROPE
    inverse = 1.0 / 10000.0**exponent
    angles = positions[:, None] * inverse[None, :]
    angles = jnp.concatenate([angles, angles], axis=1)
    return (jnp.cos(angles), jnp.sin(angles))


def lane_tables(cos_table, sin_table):
    rows = cos_table.shape[0]
    half = ROPE // 2
    ones = jnp.ones((rows, NOPE), F32)
    before = jnp.zeros((rows, NOPE), F32)
    after = jnp.zeros((rows, LANES - NOPE - ROPE), F32)
    gap = jnp.zeros((rows, half), F32)
    return (
        jnp.concatenate([ones, cos_table, after], axis=1),
        jnp.concatenate([before, -sin_table[:, :half], gap, after], axis=1),
        jnp.concatenate([before, gap, sin_table[:, half:], after], axis=1),
    )


def turn_lanes(values, cos_table, lower_table, upper_table, sign):
    return (
        values * cos_table
        + sign * (pltpu.roll(values, LANES - ROPE // 2, 1) * lower_table)
        + sign * (pltpu.roll(values, ROPE // 2, 1) * upper_table)
    )


def swap(value, axis, distance):
    size = lax.axis_size(axis)
    return lax.ppermute(value, axis, [(i, i ^ distance) for i in range(size)])


def together(*arrays):
    count = len(arrays)
    return pl.pallas_call(
        lambda *refs: None,
        in_specs=[pl.BlockSpec(memory_space=pl.ANY)] * count,
        out_specs=[pl.BlockSpec(memory_space=pl.ANY)] * count,
        out_shape=[jax.ShapeDtypeStruct(a.shape, a.dtype) for a in arrays],
        input_output_aliases={i: i for i in range(count)},
        name="together",
    )(*arrays)


def in_turn(operands, order, move):
    operands = dict(operands)
    arrived = {}
    before = []
    for group in order:
        if before:
            both = together(*[operands[name] for name in group], *[arrived[name] for name in before])
            for name, array in zip(group, both[: len(group)]):
                operands[name] = array
            for name, array in zip(before, both[len(group) :]):
                arrived[name] = array
        for name in group:
            arrived[name] = move(name, operands[name])
        before = group
    return operands, arrived


def spread_ctx(own):
    first = swap(own, "ctx", 1)
    second = swap(own, "ctx", 2)
    return [own, first, second, swap(second, "ctx", 1)]


def exchange_ctx(chunks):
    return [chunks[0]] + [swap(chunks[k], "ctx", k) for k in range(1, len(chunks))]


def sum_ctx(parts):
    third = swap(parts[3].astype(BF16), "ctx", 1)
    far = (parts[2].astype(F32) + third.astype(F32)).astype(BF16)
    near = swap(parts[1].astype(BF16), "ctx", 1)
    return parts[0].astype(F32) + near.astype(F32) + swap(far, "ctx", 2).astype(F32)


def spread_tp(own):
    far = swap(own, "tp", 2)
    return [own, swap(own, "tp", 1), far, swap(far, "tp", 1)]


def total_tp(value):
    value = value + swap(value, "tp", 1)
    return value + swap(value, "tp", 2)


def fold_halves(keep, send):
    pair = (keep + swap(send, "tp", 1)).astype(BF16)
    mine = pair.astype(F32) + swap(pair, "tp", 2).astype(F32)
    return mine, swap(mine, "tp", 1)


def at_once(copies):
    for copy in copies:
        copy.start()
    for copy in copies:
        copy.wait()


def shard_place(where, index, n_ctx):
    return (where[0] ^ (index // n_ctx)) * n_ctx + (where[1] ^ (index % n_ctx))


def row_copies(where, pieces, first_row, rows, target, sems, first_sem, n_ctx):
    if len(pieces) == 1:
        return [pltpu.make_async_copy(pieces[0], target, sems.at[first_sem])]
    out = []
    for index, piece in enumerate(pieces):
        start = pl.multiple_of(shard_place(where, index, n_ctx) * rows, SUBLANES)
        out.append(
            pltpu.make_async_copy(
                piece.at[pl.ds(first_row, rows), :],
                target.at[pl.ds(start, rows), :],
                sems.at[first_sem + index],
            )
        )
    return out


def feature_start(where, place, width):
    return pl.multiple_of((where[2] ^ place) * width, LANES)


def feature_copies(where, pieces, target, row, rows, width, sems, first_sem):
    return [
        pltpu.make_async_copy(
            piece,
            target.at[pl.ds(row, rows), pl.ds(feature_start(where, place, width), width)],
            sems.at[first_sem + place],
        )
        for place, piece in enumerate(pieces)
    ]


def run_kernel(body, inputs, outputs, scratch, flops, moved, name, grid=None, exps=0, waits=()):
    count = len(inputs)
    inputs = list(inputs) + [(array, ANY) for array in waits]

    def used(*refs):
        body(*refs[:count], *refs[len(inputs) :])

    return pl.pallas_call(
        used,
        grid=grid if grid is not None else (),
        in_specs=[spec for _, spec in inputs],
        out_specs=[spec for _, spec in outputs],
        out_shape=[shape for shape, _ in outputs],
        scratch_shapes=scratch,
        compiler_params=pltpu.CompilerParams(vmem_limit_bytes=56 << 20),
        cost_estimate=pl.CostEstimate(flops=flops, bytes_accessed=moved, transcendentals=exps),
        name=name,
    )(*[array for array, _ in inputs])


VMEM = pl.BlockSpec(memory_space=pltpu.VMEM)
SMEM = pl.BlockSpec(memory_space=pltpu.SMEM)
ANY = pl.BlockSpec(memory_space=pl.ANY)


def shape(dims, dtype=BF16):
    return jax.ShapeDtypeStruct(dims, dtype)


def cut_hidden(where, gate, up, down, parts=1, waits=()):
    rows, total = gate.shape
    hidden = total // 4
    columns = round_up(3 * hidden, LANES)

    def body(where_ref, gate_ref, up_ref, down_ref, *rest):
        outs, stage = rest[:-1], rest[-1]
        blank = jnp.zeros((rows, columns - 3 * hidden), BF16)
        for place in range(4):
            units = slice(place * hidden, (place + 1) * hidden)
            stage[place] = jnp.concatenate(
                [gate_ref[:, units], up_ref[:, units], down_ref[:, units], blank], axis=1
            )
        for number, out in enumerate(outs):
            first = number // 4 * (rows // parts)
            out[...] = stage[where_ref[1] ^ (number % 4), first : first + rows // parts]

    return run_kernel(
        body,
        [(where, SMEM), (gate, VMEM), (up, VMEM), (down.T, VMEM)],
        [(shape((rows // parts, columns)), VMEM)] * (4 * parts),
        [pltpu.VMEM((4, rows, columns), BF16)],
        0,
        12 * rows * total,
        "cut_hidden",
        waits=waits,
    )


def join_hidden(where, pieces, hidden, waits=()):
    rows = pieces[0].shape[0]

    def body(where_ref, p0, p1, p2, p3, gate_ref, up_ref, down_ref, stage):
        for step, piece in enumerate((p0, p1, p2, p3)):
            stage[where_ref[1] ^ step] = piece[...]
        for first, out in ((0, gate_ref), (hidden, up_ref), (2 * hidden, down_ref)):
            out[...] = jnp.concatenate(
                [stage[place][:, first : first + hidden].astype(F32) for place in range(4)], axis=1
            )

    return run_kernel(
        body,
        [(where, SMEM)] + [(piece, VMEM) for piece in pieces],
        [
            (shape((rows, 4 * hidden), F32), VMEM),
            (shape((rows, 4 * hidden), F32), VMEM),
            (shape((rows, 4 * hidden), F32), VMEM),
        ],
        [pltpu.VMEM((4,) + pieces[0].shape, BF16)],
        0,
        80 * rows * hidden,
        "join_hidden",
        waits=waits,
    )


def latent_products(
    where, normed, pick, query_pieces, low_pieces, query_rows, low_rows, first_low, n_ctx, paired, waits=()
):
    rows, width = normed.shape
    half = rows // 2
    shared = query_pieces is low_pieces
    shards = len(query_pieces)
    arrays = list(query_pieces) if shared else list(query_pieces) + list(low_pieces)

    def body(where_ref, normed_ref, pick_ref, *rest):
        refs = rest[: len(arrays)]
        keep, send, joined, query_gain, latent_gain, low_in, total, sems = rest[len(arrays) :]
        query_refs = refs[: len(query_pieces)]
        low_refs = query_refs if shared else refs[len(query_pieces) :]
        copies = row_copies(
            where_ref, query_refs, 0, query_rows, joined.at[pl.ds(0, QRANK), :], sems, 0, n_ctx
        )
        copies += row_copies(
            where_ref, low_refs, first_low, low_rows, low_in, sems, len(query_refs), n_ctx
        )
        at_once(copies)
        joined[QRANK:, :] = product(pick_ref[...], low_in[...]).astype(BF16)
        if paired:
            first = LATENT + ROPE
            pieces = joined[first : first + SUBLANES, :LANES].astype(F32)
            query_gain[...] = jnp.concatenate(
                [pieces[i : i + 1, :query_rows] for i in range(shards)], axis=1
            )
            latent_gain[...] = jnp.concatenate(
                [pieces[i : i + 1, query_rows:] for i in range(shards)], axis=1
            )
            joined[first : first + SUBLANES, :] = jnp.zeros((SUBLANES, width), BF16)
        total[...] = times_transposed(normed_ref[...], joined[...])
        core = where_ref[3]
        keep[...] = total[pl.ds(pl.multiple_of(core * half, 8), half), :]
        send[...] = total[pl.ds(pl.multiple_of((1 - core) * half, 8), half), :]

    return run_kernel(
        body,
        [(where, SMEM), (normed, VMEM), (pick, VMEM)] + [(a, ANY) for a in arrays],
        [
            (shape((half, LAT_COLS), F32), VMEM),
            (shape((half, LAT_COLS), F32), VMEM),
            (shape((LAT_COLS, width)), VMEM),
            (shape((1, QRANK), F32), VMEM),
            (shape((1, KVRANK), F32), VMEM),
        ],
        [
            pltpu.VMEM((pick.shape[1], width), BF16),
            pltpu.VMEM((rows, LAT_COLS), F32),
            pltpu.SemaphoreType.DMA((len(query_pieces) + len(low_pieces),)),
        ],
        2 * rows * width * LAT_COLS,
        8 << 20,
        "latent_products",
        waits=waits,
    )


def latent_norms(where, mine, other, gain_query, gain_latent, tables, waits=()):
    half = mine.shape[0]
    rows = 2 * half

    def body(where_ref, mine_ref, other_ref, gq, gl, cos_t, lower_t, upper_t, latent, query_low, payload):
        core = where_ref[3]
        latent[pl.ds(pl.multiple_of(core * half, 8), half), :] = mine_ref[...]
        latent[pl.ds(pl.multiple_of((1 - core) * half, 8), half), :] = other_ref[...]
        query = latent[:, :QRANK]
        inverse = lax.rsqrt(jnp.mean(query * query, axis=1, keepdims=True) + EPSILON)
        query_low[...] = (query * inverse * gq[...]).astype(BF16)
        low = latent[:, QRANK:LATENT]
        inverse = lax.rsqrt(jnp.mean(low * low, axis=1, keepdims=True) + EPSILON)
        payload[:, :KVRANK] = (low * inverse * gl[...]).astype(BF16)
        rope = pltpu.roll(latent[:, LATENT:], NOPE, 1)
        payload[:, KVRANK:] = turn_lanes(rope, cos_t[...], lower_t[...], upper_t[...], 1.0).astype(BF16)

    return run_kernel(
        body,
        [(where, SMEM)]
        + [(a, VMEM) for a in (mine, other, gain_query, gain_latent) + tables],
        [
            (shape((rows, LAT_COLS), F32), VMEM),
            (shape((rows, QRANK)), VMEM),
            (shape((rows, KVRANK + LANES)), VMEM),
        ],
        [],
        20 * rows * LAT_COLS,
        4 << 20,
        "latent_norms",
        waits=waits,
    )


def masked_blocks(scores, place, rows, blocks):
    key_row = lax.broadcasted_iota(jnp.int32, (rows, rows), 0)
    query_column = lax.broadcasted_iota(jnp.int32, (rows, rows), 1)
    out = [jnp.where(key_row <= query_column, scores[:rows], NEGATIVE)]
    for block in range(1, blocks):
        seen = (place ^ block) < place
        out.append(jnp.where(seen, scores[block * rows : (block + 1) * rows], NEGATIVE))
    return out


def head_lanes(index):
    return pl.ds(pl.multiple_of(index * 2 * LANES, 2 * LANES), 2 * LANES)


def up_copies(where_ref, refs, wq, wkv, sems, n_ctx):
    if len(refs) == 3:
        return [
            pltpu.make_async_copy(refs[0], wq, sems.at[0]),
            pltpu.make_async_copy(refs[1], wkv, sems.at[1]),
        ]
    shards = len(refs) // 2
    query_rows = QRANK // shards
    low_rows = KVRANK // shards
    refs = refs[:shards]
    return row_copies(where_ref, refs, 0, query_rows, wq, sems, 0, n_ctx) + row_copies(
        where_ref, refs, query_rows, low_rows, wkv, sems, shards, n_ctx
    )


def out_copies(where_ref, refs, target, sems, first_sem, n_ctx):
    if len(refs) == 3:
        return [pltpu.make_async_copy(refs[2], target, sems.at[first_sem])]
    refs = refs[len(refs) // 2 :]
    return row_copies(where_ref, refs, 0, refs[0].shape[0], target, sems, first_sem, n_ctx)


def sequence_refs(source):
    return [piece for group in source for piece in group]


def sequence_shape(source):
    return (4 * len(source),) + source[0][0].shape


def sequence_copies(where, refs, target, rows, width, sems, first_sem):
    return [
        feature_copies(
            where, refs[at : at + 4], target, at // 4 * rows, rows, width, sems, first_sem + at
        )
        for at in range(0, len(refs), 4)
    ]


def hidden_copies(where, arrays, target, sems, first_sem, n_ctx, columns=None):
    cut = (lambda ref: ref) if columns is None else (lambda ref: ref.at[:, columns])
    if len(arrays) == 1:
        return [pltpu.make_async_copy(cut(arrays[0]), target, sems.at[first_sem])]
    rows = arrays[0].shape[0]
    parts = target.shape[0] // (rows * 2 * n_ctx)
    out = []
    for number, ref in enumerate(arrays):
        part, index = number // (2 * n_ctx), number % (2 * n_ctx)
        start = shard_place(where, index, n_ctx) * parts + part
        start = pl.multiple_of(start * rows, SUBLANES)
        out.append(
            pltpu.make_async_copy(
                cut(ref), target.at[pl.ds(start, rows), :], sems.at[first_sem + number]
            )
        )
    return out


def attention_forward(where, query_low, payloads, ups, tables, heads, n_ctx, waits=()):
    rows = query_low.shape[0]
    blocks = len(payloads)
    keys = blocks * rows
    pairs = heads // 2
    whole = lambda dims: pl.BlockSpec(dims, lambda i: (0, 0))
    column = lambda dims: pl.BlockSpec(dims, lambda i: (0, i))

    def body(where_ref, low_q, cos_t, lower_t, upper_t, *rest):
        sources = rest[:blocks]
        up_refs = rest[blocks : blocks + len(ups)]
        out, q_out, kv_out, lse_out, wq, wkv, tokens, sems = rest[blocks + len(ups) :]
        step = pl.program_id(0)

        @pl.when(step == 0)
        def _():
            copies = up_copies(where_ref, up_refs, wq, wkv, sems, n_ctx)
            first = len(copies)
            for block, source in enumerate(sources):
                copies.append(
                    pltpu.make_async_copy(
                        source, tokens.at[pl.ds(block * rows, rows), :], sems.at[first + block]
                    )
                )
            at_once(copies)

        key_lane = lax.broadcasted_iota(jnp.int32, (keys, LANES), 1)
        raw_pair = product(low_q[...], wq[:, head_lanes(step)])
        kv_pair = product(tokens[:, :KVRANK], wkv[:, head_lanes(step)]).astype(BF16)
        rope_key = tokens[:, KVRANK:]
        kv_out[...] = kv_pair
        outs = []
        for head in range(2):
            lanes = slice(head * LANES, (head + 1) * LANES)
            query = turn_lanes(
                raw_pair[:, lanes], cos_t[...], lower_t[...], upper_t[...], 1.0
            ).astype(BF16)
            pair = kv_pair[:, lanes]
            key = jnp.where(key_lane < NOPE, pair, rope_key)
            q_out[:, lanes] = query
            scores = times_transposed(key, query) * SCORE
            masked = masked_blocks(scores, where_ref[1], rows, blocks)
            top = functools.reduce(
                jnp.maximum, [jnp.max(part, axis=0, keepdims=True) for part in masked]
            )
            powers = [jnp.exp(part - top) for part in masked]
            total = sum(jnp.sum(part, axis=0, keepdims=True) for part in powers)
            prob = jnp.concatenate([part.astype(BF16) for part in powers], axis=0)
            mixed = transposed_times(pair, prob) / total
            outs.append(jnp.transpose(mixed))
            lse_out[0, head : head + 1, :] = top + jnp.log(total)
        lane = lax.broadcasted_iota(jnp.int32, (rows, LANES), 1)
        out[...] = jnp.where(lane < VDIM, pltpu.roll(outs[0], VDIM, 1), outs[1]).astype(BF16)

    return run_kernel(
        body,
        [(where, SMEM), (query_low, whole(query_low.shape))]
        + [(table, whole(table.shape)) for table in tables]
        + [(a, ANY) for a in list(payloads) + list(ups)],
        [
            (shape((rows, pairs * LANES)), column((rows, LANES))),
            (shape((rows, heads * LANES)), column((rows, 2 * LANES))),
            (shape((keys, heads * LANES)), column((keys, 2 * LANES))),
            (shape((pairs, 8, rows), F32), pl.BlockSpec((1, 8, rows), lambda i: (i, 0, 0))),
        ],
        [
            pltpu.VMEM((QRANK, heads * LANES), BF16),
            pltpu.VMEM((KVRANK, heads * LANES), BF16),
            pltpu.VMEM((keys, KVRANK + LANES), BF16),
            pltpu.SemaphoreType.DMA((64 + blocks,)),
        ],
        2 * heads * rows * (QRANK + 2 * keys) * LANES + 2 * heads * keys * KVRANK * LANES,
        12 << 20,
        "attention_forward",
        grid=(pairs,),
        exps=heads * rows * keys,
        waits=waits,
    )


def attention_backward(where, queries, pairs_low, lse, payloads, ups, branch, tables, n_ctx, waits=()):
    rows, q_lanes = queries.shape
    heads = q_lanes // LANES
    pairs = heads // 2
    blocks = len(payloads)
    keys = blocks * rows
    width = branch[0].shape[1]
    full_width = 4 * width
    inner = heads * VDIM
    whole = lambda dims: pl.BlockSpec(dims, lambda i: (0, 0))
    column = lambda dims: pl.BlockSpec(dims, lambda i: (0, i))
    moved = list(payloads) + list(ups) + list(branch)

    def body(where_ref, q_in, kv_in, lse_in, cos_t, lower_t, upper_t, *rest):
        refs = rest[: len(moved)]
        (dq_out, dkv_out, query_sum, kv_keep, kv_1, kv_2, kv_3) = rest[len(moved) : len(moved) + 7]
        wq, wkv, rope_key, wo, grad_in, dout, kv_sum, sems = rest[len(moved) + 7 :]
        step = pl.program_id(0)
        place = where_ref[1]

        @pl.when(step == 0)
        def _():
            at = 0
            sources, at = refs[at : at + blocks], at + blocks
            up_refs, at = refs[at : at + len(ups)], at + len(ups)
            branch_refs = refs[at : at + 4]
            copies = up_copies(where_ref, up_refs, wq, wkv, sems, n_ctx)
            for block, source in enumerate(sources):
                copies.append(
                    pltpu.make_async_copy(
                        source.at[:, pl.ds(KVRANK, LANES)],
                        rope_key.at[pl.ds(block * rows, rows), :],
                        sems.at[len(copies)],
                    )
                )
            copies += feature_copies(
                where_ref, branch_refs, grad_in, 0, rows, width, sems, len(copies)
            )
            copies += out_copies(where_ref, up_refs, wo, sems, len(copies), n_ctx)
            at_once(copies)
            dout[...] = product(grad_in[...], wo[...]).astype(BF16).astype(F32)
            query_sum[...] = jnp.zeros_like(query_sum)
            kv_sum[...] = jnp.zeros_like(kv_sum)

        key_lane = lax.broadcasted_iota(jnp.int32, (keys, LANES), 1)
        lane = lax.broadcasted_iota(jnp.int32, (rows, LANES), 1)
        both = dout[:, pl.ds(pl.multiple_of(step * LANES, LANES), LANES)]
        dkr = jnp.zeros((keys, LANES), F32)
        dq_parts = []
        dkv_parts = []
        for head in range(2):
            lanes = slice(head * LANES, (head + 1) * LANES)
            query = q_in[:, lanes]
            pair = kv_in[:, lanes]
            key = jnp.where(key_lane < NOPE, pair, rope_key[...])
            upper = pltpu.roll(both, VDIM, 1) if head == 0 else both
            out_grad = jnp.where(lane >= NOPE, upper, 0.0).astype(BF16)
            scores = times_transposed(key, query) * SCORE
            top = lse_in[0, head : head + 1, :]
            masked = masked_blocks(scores, place, rows, blocks)
            prob = jnp.concatenate([jnp.exp(part - top) for part in masked], axis=0)
            prob_grad = times_transposed(pair, out_grad)
            weighted = prob * prob_grad
            delta = jnp.sum(weighted, axis=0, keepdims=True)
            score_grad = (weighted - prob * delta).astype(BF16)
            key_grad = product(score_grad, query) * SCORE
            value_grad = product(prob.astype(BF16), out_grad)
            dkv_parts.append(jnp.where(key_lane < NOPE, key_grad, value_grad).astype(BF16))
            dkr = dkr + key_grad
            query_grad = jnp.transpose(transposed_times(key, score_grad)) * SCORE
            dq_parts.append(
                turn_lanes(query_grad, cos_t[...], lower_t[...], upper_t[...], -1.0).astype(BF16)
            )
        dq_pair = jnp.concatenate(dq_parts, axis=1)
        dkv_pair = jnp.concatenate(dkv_parts, axis=1)
        dq_out[...] = dq_pair
        dkv_out[...] = dkv_pair
        query_sum[...] += times_transposed(dq_pair, wq[:, head_lanes(step)])
        kv_sum[:, :KVRANK] += times_transposed(dkv_pair, wkv[:, head_lanes(step)])
        kv_sum[:, KVRANK:] += jnp.where(key_lane >= NOPE, dkr, 0.0)

        @pl.when(step == pairs - 1)
        def _():
            kv_keep[...] = kv_sum[:rows]
            for block, out in ((1, kv_1), (2, kv_2), (3, kv_3)):
                out[...] = kv_sum[block * rows : (block + 1) * rows].astype(BF16)

    return run_kernel(
        body,
        [
            (where, SMEM),
            (queries, column((rows, 2 * LANES))),
            (pairs_low, column((keys, 2 * LANES))),
            (lse, pl.BlockSpec((1, 8, rows), lambda i: (i, 0, 0))),
        ]
        + [(table, whole(table.shape)) for table in tables]
        + [(a, ANY) for a in moved],
        [
            (shape((rows, heads * LANES)), column((rows, 2 * LANES))),
            (shape((keys, heads * LANES)), column((keys, 2 * LANES))),
            (shape((rows, QRANK), F32), whole((rows, QRANK))),
            (shape((rows, KVRANK + LANES), F32), whole((rows, KVRANK + LANES))),
        ]
        + [(shape((rows, KVRANK + LANES)), whole((rows, KVRANK + LANES)))] * 3,
        [
            pltpu.VMEM((QRANK, heads * LANES), BF16),
            pltpu.VMEM((KVRANK, heads * LANES), BF16),
            pltpu.VMEM((keys, LANES), BF16),
            pltpu.VMEM((full_width, inner), BF16),
            pltpu.VMEM((rows, full_width), BF16),
            pltpu.VMEM((rows, inner), F32),
            pltpu.VMEM((keys, KVRANK + LANES), F32),
            pltpu.SemaphoreType.DMA((128 + blocks,)),
        ],
        10 * heads * rows * keys * LANES,
        24 << 20,
        "attention_backward",
        grid=(pairs,),
        exps=heads * rows * keys,
        waits=waits,
    )


def output_products(where, attended, ups, full_width, n_ctx, waits=()):
    rows, inner = attended.shape
    count = len(ups)
    width = full_width // 4

    def body(where_ref, attended_ref, *rest):
        refs = rest[:count]
        keep, send, weight, sems = rest[count:]
        at_once(out_copies(where_ref, refs, weight, sems, 0, n_ctx))
        for place in range(4):
            block = weight[pl.ds(feature_start(where_ref, place, width), width), :]
            part = times_transposed(attended_ref[...], block)
            if place % 2 == 0:
                keep[place // 2] = part
            else:
                send[place // 2] = part.astype(BF16)

    return run_kernel(
        body,
        [(where, SMEM), (attended, VMEM)] + [(a, ANY) for a in ups],
        [(shape((2, rows, width), F32), VMEM), (shape((2, rows, width)), VMEM)],
        [pltpu.VMEM((full_width, inner), BF16), pltpu.SemaphoreType.DMA((64,))],
        2 * rows * inner * full_width,
        6 << 20,
        "output_products",
        waits=waits,
    )


def feed_forward(where, tokens, branches, weights, gains, hidden, n_ctx):
    count, rows, width = sequence_shape(tokens)
    blocks = count // 4
    full_width = 4 * width
    columns = weights[0].shape[-1]
    upper_end = round_up(2 * hidden, LANES)
    lower_start = 2 * hidden // LANES * LANES
    shift = 2 * hidden - lower_start
    lower_cols = columns - lower_start
    total = blocks * rows
    token_list, branch_list = sequence_refs(tokens), sequence_refs(branches)
    flat = len(token_list) + len(branch_list)
    moved = token_list + branch_list + list(gains) + list(weights)

    def body(where_ref, *rest):
        refs = rest[: len(moved)]
        pairs_out, active_out, keep, send, inverse_out = rest[len(moved) : len(moved) + 5]
        normed, branch, weight, gain, sems = rest[len(moved) + 5 :]
        first = 2 * count
        weight_copies = feature_copies(
            where_ref, refs[flat : flat + 4], gain, 0, gain.shape[0], width, sems, first
        ) + hidden_copies(where_ref, refs[flat + 4 :], weight, sems, first + 4, n_ctx)
        token_copies = [
            first_list + second_list
            for first_list, second_list in zip(
                sequence_copies(
                    where_ref, refs[: len(token_list)], normed, rows, width, sems, 0
                ),
                sequence_copies(
                    where_ref, refs[len(token_list) : flat], branch, rows, width, sems, count
                ),
            )
        ]
        for copy in weight_copies + sum(token_copies, []):
            copy.start()
        for copy in weight_copies:
            copy.wait()

        def hidden_block(block, carry):
            for number, copies in enumerate(token_copies):

                @pl.when(block == number)
                def _():
                    for copy in copies:
                        copy.wait()

            here = pl.ds(pl.multiple_of(block * rows, rows), rows)
            source = normed[here, :].astype(F32) / gain[:1, :]
            inverse = lax.rsqrt(jnp.mean(source * source, axis=1, keepdims=True) + EPSILON)

            @pl.when(block == 0)
            def _():
                inverse_out[...] = jnp.broadcast_to(inverse, inverse_out.shape)

            both = product(normed[here, :], weight[:, :upper_end]) * inverse
            lower = product(branch[here, :], weight[:, lower_start:])
            gate = both[:, :hidden]
            upper = both[:, hidden : 2 * hidden]
            grad = lower[:, shift : shift + hidden]
            scaled = grad * inverse
            sigmoid = 1.0 / (1.0 + jnp.exp(-gate))
            active = gate * sigmoid
            pairs_out[here, :] = jnp.concatenate(
                [
                    scaled * upper * sigmoid * (1.0 + gate * (1.0 - sigmoid)),
                    scaled * active,
                    jnp.zeros((rows, upper_end - 2 * hidden), F32),
                ],
                axis=1,
            ).astype(BF16)
            active_out[here, :] = jnp.concatenate(
                [
                    jnp.zeros((rows, shift), F32),
                    active * upper,
                    jnp.zeros((rows, lower_cols - shift - hidden), F32),
                ],
                axis=1,
            ).astype(BF16)
            return carry

        lax.fori_loop(0, blocks, hidden_block, 0)
        for place in range(4):
            block = weight[pl.ds(feature_start(where_ref, place, width), width), :upper_end]
            part = times_transposed(pairs_out[...], block).astype(BF16)
            (send if place % 2 else keep)[place // 2] = part

    return run_kernel(
        body,
        [(where, SMEM)] + [(a, ANY) for a in moved],
        [
            (shape((total, upper_end)), VMEM),
            (shape((total, lower_cols)), VMEM),
            (shape((2, total, width)), VMEM),
            (shape((2, total, width)), VMEM),
            (shape((rows, LANES), F32), VMEM),
        ],
        [
            pltpu.VMEM((total, full_width), BF16),
            pltpu.VMEM((total, full_width), BF16),
            pltpu.VMEM((full_width, columns), BF16),
            pltpu.VMEM(gains[0].shape[:1] + (full_width,), F32),
            pltpu.SemaphoreType.DMA((2 * count + 4 + full_width // SUBLANES,)),
        ],
        10 * total * full_width * hidden,
        28 << 20,
        "feed_forward",
        exps=total * hidden,
    )


def feed_forward_result(where, active, weights, hidden, n_ctx, waits=()):
    total, lower_cols = active.shape
    columns = weights[0].shape[1]
    full_width = sum(a.shape[0] for a in weights)
    width = full_width // 4
    count = len(weights)

    def body(where_ref, active_ref, *rest):
        refs = rest[:count]
        outs = rest[count:-2]
        weight, sems = rest[-2:]
        lower = pl.ds(columns - lower_cols, lower_cols)
        at_once(hidden_copies(where_ref, refs, weight, sems, 0, n_ctx, columns=lower))
        for place in range(4):
            block = weight[pl.ds(feature_start(where_ref, place, width), width), :]
            part = times_transposed(active_ref[...], block).astype(BF16)
            outs[place % 2][place // 2] = part

    return run_kernel(
        body,
        [(where, SMEM), (active, VMEM)] + [(a, ANY) for a in weights],
        [(shape((2, total, width)), VMEM)] * 2,
        [
            pltpu.VMEM((full_width, lower_cols), BF16),
            pltpu.SemaphoreType.DMA((full_width // SUBLANES,)),
        ],
        2 * total * full_width * hidden,
        10 << 20,
        "feed_forward_result",
        waits=waits,
    )


def feed_forward_grads(
    where, tokens, branches, pairs_grad, active, hidden, columns, shards, n_ctx, distance, waits=()
):
    count, rows, width = sequence_shape(tokens)
    token_list, branch_list = sequence_refs(tokens), sequence_refs(branches)
    total = count // 4 * rows
    upper_end = pairs_grad.shape[1]
    lower_cols = active.shape[1]
    lower_start = columns - lower_cols
    shard_rows = 4 * width // shards

    def gradient(normed, branch, pairs_ref, active_ref):
        first = transposed_times(normed, pairs_ref[...])
        second = transposed_times(branch, active_ref[...])
        middle = first[:, lower_start:] + second[:, : upper_end - lower_start]
        return jnp.concatenate(
            [first[:, :lower_start], middle, second[:, upper_end - lower_start :]], axis=1
        ).astype(BF16)

    def body(where_ref, pairs_ref, active_ref, *rest):
        token_refs, rest = rest[: len(token_list)], rest[len(token_list) :]
        branch_refs, rest = rest[: len(branch_list)], rest[len(branch_list) :]
        outs = rest[:-4]
        normed, branch, stage, sems = rest[-4:]
        copies = sequence_copies(where_ref, token_refs, normed, rows, width, sems, 0)
        copies += sequence_copies(where_ref, branch_refs, branch, rows, width, sems, count)
        if distance is not None:
            for place in range(4):

                @pl.when(((where_ref[2] ^ place) >> 1) == (where_ref[0] ^ distance))
                def _():
                    at_once([group[place] for group in copies])

        else:
            at_once(sum(copies, []))
        if distance is None:
            for place in range(4):
                here = slice(place * width, (place + 1) * width)
                outs[0][here, :] = gradient(normed[:, here], branch[:, here], pairs_ref, active_ref)
            return
        for number in range(n_ctx // 2):
            place = owner_blocks(where_ref, distance * (n_ctx // 2) + number, n_ctx)
            here = pl.ds(pl.multiple_of(place * width, LANES), width)
            stage[...] = gradient(normed[:, here], branch[:, here], pairs_ref, active_ref)
            for low in range(2):
                start = pl.multiple_of((low ^ (where_ref[1] % 2)) * shard_rows, SUBLANES)
                outs[2 * number + low][...] = stage[pl.ds(start, shard_rows), :]

    if distance is None:
        outputs = [(shape((4 * width, columns)), VMEM)]
    else:
        outputs = [(shape((shard_rows, columns)), VMEM)] * n_ctx
    return run_kernel(
        body,
        [(where, SMEM), (pairs_grad, VMEM), (active, VMEM)]
        + [(a, ANY) for a in token_list + branch_list],
        outputs,
        [
            pltpu.VMEM((total, 4 * width), BF16),
            pltpu.VMEM((total, 4 * width), BF16),
            pltpu.VMEM((width, columns), BF16),
            pltpu.SemaphoreType.DMA((2 * count,)),
        ],
        6 * total * 4 * width * hidden // 2,
        18 << 20,
        "feed_forward_grads",
        waits=waits,
    )


def owner_blocks(where_ref, part, n_ctx):
    per_row = n_ctx // 2
    return (where_ref[0] ^ (part // per_row)) * per_row + ((where_ref[1] // 2) ^ (part % per_row))


def output_grads(where, attended, branch, shards, n_ctx, paired, waits=()):
    rows, inner = attended.shape
    width = branch[0].shape[1]
    shard_rows = 4 * width // shards

    def body(where_ref, attended_ref, b0, b1, b2, b3, *rest):
        outs = rest[:-3]
        grad_in, stage, sems = rest[-3:]
        at_once(feature_copies(where_ref, (b0, b1, b2, b3), grad_in, 0, rows, width, sems, 0))
        for part in range(4):
            place = owner_blocks(where_ref, part, n_ctx) if paired else part
            here = pl.ds(pl.multiple_of(place * width, LANES), width)
            stage[...] = transposed_times(grad_in[:, here], attended_ref[...]).astype(BF16)
            if not paired:
                outs[0][part * width : (part + 1) * width, :] = stage[...]
                continue
            for low in range(2):
                start = pl.multiple_of((low ^ (where_ref[1] % 2)) * shard_rows, SUBLANES)
                outs[2 * part + low][...] = stage[pl.ds(start, shard_rows), :]

    if paired:
        outputs = [(shape((shard_rows, inner)), VMEM)] * shards
    else:
        outputs = [(shape((4 * width, inner)), VMEM)]
    return run_kernel(
        body,
        [(where, SMEM), (attended, VMEM)] + [(a, ANY) for a in branch],
        outputs,
        [
            pltpu.VMEM((rows, 4 * width), BF16),
            pltpu.VMEM((width, inner), BF16),
            pltpu.SemaphoreType.DMA((4,)),
        ],
        2 * rows * inner * 4 * width,
        6 << 20,
        "output_grads",
        waits=waits,
    )


def up_grads(where, query_low, query_grad, payloads, pair_grad, shards, n_ctx, paired, waits=()):
    rows = query_low.shape[0]
    blocks = len(payloads)
    lanes = query_grad.shape[1]
    query_rows = QRANK // shards
    low_rows = KVRANK // shards

    def body(where_ref, low_q, dq, dkv, *rest):
        sources = rest[:blocks]
        rest = rest[blocks:]
        outs = rest[:-4]
        tokens, stage_q, stage_kv, sems = rest[-4:]
        at_once(
            [
                pltpu.make_async_copy(
                    source.at[:, pl.ds(0, KVRANK)],
                    tokens.at[pl.ds(block * rows, rows), :],
                    sems.at[block],
                )
                for block, source in enumerate(sources)
            ]
        )
        grad_q = transposed_times(low_q[...], dq[...]).astype(BF16)
        grad_kv = transposed_times(tokens[...], dkv[...]).astype(BF16)
        if not paired:
            outs[0][...] = grad_q
            outs[1][...] = grad_kv
            return
        stage_q[...] = grad_q
        stage_kv[...] = grad_kv
        for index, out in enumerate(outs):
            place = shard_place(where_ref, index, n_ctx)
            out[:query_rows, :] = stage_q[
                pl.ds(pl.multiple_of(place * query_rows, SUBLANES), query_rows), :
            ]
            out[query_rows:, :] = stage_kv[
                pl.ds(pl.multiple_of(place * low_rows, SUBLANES), low_rows), :
            ]

    if paired:
        outputs = [(shape((query_rows + low_rows, lanes)), VMEM)] * shards
    else:
        outputs = [(shape((QRANK, lanes)), VMEM), (shape((KVRANK, lanes)), VMEM)]
    return run_kernel(
        body,
        [(where, SMEM), (query_low, VMEM), (query_grad, VMEM), (pair_grad, VMEM)]
        + [(a, ANY) for a in payloads],
        outputs,
        [
            pltpu.VMEM((blocks * rows, KVRANK), BF16),
            pltpu.VMEM((QRANK, lanes), BF16),
            pltpu.VMEM((KVRANK, lanes), BF16),
            pltpu.SemaphoreType.DMA((blocks,)),
        ],
        2 * lanes * (rows * QRANK + blocks * rows * KVRANK),
        10 << 20,
        "up_grads",
        waits=waits,
    )


def input_backward(
    where,
    mine,
    other,
    latent,
    gain_query,
    gain_latent,
    tables,
    normed,
    joined,
    activations,
    inverse_one,
    gain_one,
    middle_grad,
    pick,
    query_rows,
    low_rows,
    shards,
    n_ctx,
    paired,
    waits=(),
):
    half = mine.shape[0]
    rows, width = normed.shape
    full_width = 4 * width
    low_in = pick.shape[1]

    def body(
        where_ref, mine_ref, other_ref, latent_ref, gq, gl, cos_t, lower_t, upper_t, normed_ref,
        joined_ref, act_ref, inverse_ref, gain_ref, middle_ref, pick_ref, input_out, query_gain_out,
        latent_gain_out, gain_out, *rest
    ):
        outs = rest[:-3]
        sums, stage_q, stage_low = rest[-3:]
        core = where_ref[3]
        sums[pl.ds(pl.multiple_of(core * half, 8), half), :] = mine_ref[...]
        sums[pl.ds(pl.multiple_of((1 - core) * half, 8), half), :] = other_ref[...]
        parts = []
        for first, last, gain, out in (
            (0, QRANK, gq, query_gain_out),
            (QRANK, LATENT, gl, latent_gain_out),
        ):
            source = latent_ref[:, first:last]
            grad = sums[:, first:last]
            inverse = lax.rsqrt(jnp.mean(source * source, axis=1, keepdims=True) + EPSILON)
            out[...] = jnp.sum(grad * source * inverse, axis=0, keepdims=True)
            scaled = grad * gain[...]
            inner = jnp.mean(scaled * source, axis=1, keepdims=True)
            parts.append(inverse * scaled - source * (inverse * inverse * inverse * inner))
        rope = turn_lanes(sums[:, LATENT:], cos_t[...], lower_t[...], upper_t[...], -1.0)
        parts.append(pltpu.roll(rope, LANES - NOPE, 1))
        latent_grad = jnp.concatenate(parts, axis=1)
        low = latent_grad.astype(BF16)
        down_grad = transposed_times(low, normed_ref[...]).astype(BF16)
        if paired:
            stage_q[...] = down_grad[:QRANK]
            gains = [
                jnp.concatenate(
                    [
                        query_gain_out[:, i * query_rows : (i + 1) * query_rows],
                        latent_gain_out[:, i * KVRANK // shards : (i + 1) * KVRANK // shards],
                        jnp.zeros((1, width - LANES), F32),
                    ],
                    axis=1,
                )
                for i in range(shards)
            ]
            first = LATENT + ROPE - QRANK
            low_part = jnp.concatenate(
                [
                    down_grad[QRANK : LATENT + ROPE].astype(F32),
                    jnp.concatenate(gains, axis=0),
                    jnp.zeros((LOW_ROWS - first - shards, width), F32),
                ],
                axis=0,
            ).astype(BF16)
            stage_low[...] = transposed_times(pick_ref[...], low_part).astype(BF16)
            for index, out in enumerate(outs):
                place = shard_place(where_ref, index, n_ctx)
                out[:query_rows, :] = stage_q[
                    pl.ds(pl.multiple_of(place * query_rows, SUBLANES), query_rows), :
                ]
                out[query_rows:, :] = stage_low[
                    pl.ds(pl.multiple_of(place * low_rows, SUBLANES), low_rows), :
                ]
        else:
            outs[0][...] = down_grad
        row_inner = jnp.sum(latent_grad * latent_ref[...], axis=1, keepdims=True)
        normed_grad = product(low, joined_ref[...])
        source = act_ref[...].astype(F32)
        inverse = inverse_ref[...]
        gain_out[...] = jnp.sum(normed_grad * source * inverse, axis=0, keepdims=True)
        input_out[...] = (
            middle_ref[...]
            + inverse * (normed_grad * gain_ref[...])
            - source * (inverse * inverse * row_inner / full_width)
        )

    if paired:
        outputs = [(shape((query_rows + low_rows, width)), VMEM)] * shards
    else:
        outputs = [(shape((LAT_COLS, width)), VMEM)]
    arrays = (mine, other, latent, gain_query, gain_latent) + tables
    arrays += (normed, joined, activations, inverse_one, gain_one, middle_grad, pick)
    return run_kernel(
        body,
        [(where, SMEM)] + [(a, VMEM) for a in arrays],
        [
            (shape((rows, width), F32), VMEM),
            (shape((1, QRANK), F32), VMEM),
            (shape((1, KVRANK), F32), VMEM),
            (shape((1, width), F32), VMEM),
        ]
        + outputs,
        [
            pltpu.VMEM((rows, LAT_COLS), F32),
            pltpu.VMEM((QRANK, width), BF16),
            pltpu.VMEM((low_in, width), BF16),
        ],
        4 * rows * width * LAT_COLS,
        12 << 20,
        "input_backward",
        waits=waits,
    )


def pick_matrix(columns, rows_each, valid):
    matrix = np.zeros((LOW_ROWS, columns), np.float32)
    for row in range(KVRANK + ROPE):
        matrix[row, row // valid * rows_each + row % valid] = 1.0
    for shard in range(columns // rows_each if rows_each > valid else 0):
        matrix[KVRANK + ROPE + shard, shard * rows_each + valid] = 1.0
    return jnp.asarray(matrix, BF16)


def per_device(
    activations,
    attn_gain,
    query_down,
    latent_down,
    query_gain,
    latent_gain,
    query_up,
    latent_up,
    attn_output,
    ffn_gain,
    ffn_gate,
    ffn_up,
    ffn_down,
    out_grad,
):
    n_fsdp = lax.axis_size("fsdp")
    n_ctx = lax.axis_size("ctx")
    n_tp = lax.axis_size("tp")
    shards = n_fsdp * n_ctx
    paired = n_fsdp == 2 and shards == 2 * n_tp
    rows, width = activations.shape
    full_width = width * n_tp
    fsdp_index = lax.axis_index("fsdp").astype(jnp.int32)
    ctx_index = lax.axis_index("ctx").astype(jnp.int32)
    tp_index = lax.axis_index("tp").astype(jnp.int32)
    shard_index = fsdp_index * n_ctx + ctx_index
    where = jnp.stack([fsdp_index, ctx_index, tp_index, tp_index % 2])
    local_heads = query_up.shape[1] // (NOPE + ROPE)
    hidden = ffn_gate.shape[1] // n_ctx
    columns = round_up(3 * hidden, LANES)
    q_shard = query_down.shape[1]
    low_shard = latent_down.shape[1]
    both_axes = ("fsdp", "ctx")

    def spread_shards(own):
        pieces = spread_ctx(own)
        return pieces + [swap(piece, "fsdp", 1) for piece in pieces]

    def fold_shards(parts):
        return [
            (parts[k].astype(F32) + swap(parts[n_ctx + k], "fsdp", 1).astype(F32)).astype(BF16)
            for k in range(n_ctx)
        ]

    def gather_rows(value):
        return lax.all_gather(value, both_axes, axis=0, tiled=True)

    def scatter_rows(value):
        return lax.psum_scatter(value, both_axes, scatter_dimension=0, tiled=True).astype(F32)

    def spread_sequence(own):
        return [spread_tp(block) for block in spread_ctx(own)]

    inputs = activations.astype(F32)
    gain_one = attn_gain.astype(F32)
    row_sums = total_tp(jnp.sum(inputs * inputs, axis=1))
    inverse_one = lax.rsqrt(row_sums / full_width + EPSILON)
    gain_two = ffn_gain.astype(F32)
    gains_two = spread_tp(jnp.broadcast_to(gain_two[None, :], (8, width)))
    normed_low = (inputs * inverse_one[:, None] * gain_one).astype(BF16)

    query_pad = jnp.pad(
        query_up.reshape(query_up.shape[0], local_heads, NOPE + ROPE),
        ((0, 0), (0, 0), (0, LANES - NOPE - ROPE)),
    ).reshape(query_up.shape[0], local_heads * LANES)
    if paired:
        low_rows = round_up(low_shard, SUBLANES)
        pick = pick_matrix(shards * low_rows, low_rows, low_shard)
        down_own = jnp.concatenate(
            [
                query_down.T,
                latent_down.T,
                jnp.pad(
                    jnp.concatenate([query_gain, latent_gain])[None, :],
                    ((0, low_rows - low_shard - 1), (0, width - LANES)),
                ),
            ]
        )
        query_pieces = low_pieces = spread_shards(down_own)
        first_low = q_shard
        ups = spread_shards(jnp.concatenate([query_pad, latent_up])) + spread_shards(attn_output.T)
    else:
        low_rows = low_shard
        pick = pick_matrix(LOW_ROWS, KVRANK + ROPE, KVRANK + ROPE)
        query_pieces = [gather_rows(query_down.T)]
        low_pieces = [
            jnp.pad(gather_rows(latent_down.T), ((0, LOW_ROWS - KVRANK - ROPE), (0, 0)))
        ]
        first_low = 0
        ups = [gather_rows(query_pad), gather_rows(latent_up), gather_rows(attn_output.T)]

    parts = 2 if paired else 1
    chunks = cut_hidden(where, ffn_gate, ffn_up, ffn_down, parts=parts)
    if paired:
        sent = {(part, k): chunks[n_ctx * part + k] for part in range(parts) for k in range(1, n_ctx)}
        order = [[(part, k) for k in group] for part in range(parts) for group in ((2, 1), (3,))]
        _, got = in_turn(sent, order, lambda key, value: swap(value, "ctx", key[1]))
        got.update({(part, 0): chunks[n_ctx * part] for part in range(parts)})
        order = [[(part, 0)] for part in range(parts)]
        order += [[(part, k)] for part in range(parts) for k in range(1, n_ctx)]
        got, crossed = in_turn(got, order, lambda key, value: swap(value, "fsdp", 1))
        weights = []
        for part in range(parts):
            weights += [got[part, k] for k in range(n_ctx)]
            weights += [crossed[part, k] for k in range(n_ctx)]
    else:
        stack = jnp.stack(exchange_ctx(chunks))
        stack = jnp.stack(
            [
                lax.dynamic_index_in_dim(stack, ctx_index ^ k, 0, keepdims=False)
                for k in range(n_ctx)
            ]
        )
        weights = [lax.all_gather(stack, "fsdp", axis=0).reshape(full_width, columns)]

    upstream = out_grad.astype(F32)
    branches = spread_sequence((RESID * upstream).astype(BF16))

    keep, send, joined, gain_query, gain_latent = latent_products(
        where,
        normed_low,
        pick,
        query_pieces,
        low_pieces,
        q_shard,
        low_rows,
        first_low,
        n_ctx,
        paired,
        waits=list(chunks[:1]) + ups[1:2],
    )
    if not paired:
        gains = jnp.zeros((QRANK + KVRANK,), F32)
        gains = lax.dynamic_update_slice(
            gains, query_gain.astype(F32), (shard_index * query_gain.shape[0],)
        )
        gains = lax.dynamic_update_slice(
            gains, latent_gain.astype(F32), (QRANK + shard_index * latent_gain.shape[0],)
        )
        gains = lax.psum(gains, both_axes)
        gain_query = gains[None, :QRANK]
        gain_latent = gains[None, QRANK:]
    mine, other = fold_halves(keep, send)
    query_pos = ctx_index * rows + jnp.arange(rows, dtype=jnp.int32)
    tables = lane_tables(*rotary_tables(query_pos.astype(F32)))
    latent, query_low, payload = latent_norms(where, mine, other, gain_query, gain_latent, tables)
    payloads = spread_ctx(payload)

    attended, queries_low, pairs_low, lse = attention_forward(
        where, query_low, payloads, ups, tables, local_heads, n_ctx
    )

    def fold_tp(keep, send):
        got = swap(send, "tp", 1)
        far = (keep[1].astype(F32) + got[1].astype(F32)).astype(BF16)
        near = keep[0].astype(F32) + got[0].astype(F32)
        return near + swap(far, "tp", 2).astype(F32)

    keep, send = output_products(where, attended, ups, full_width, n_ctx)
    middle = inputs + RESID * fold_tp(keep, send)

    tokens = spread_sequence((middle * gain_two).astype(BF16))
    pairs_grad, active, keep, send, inverse_two = feed_forward(
        where, tokens, branches, weights, gains_two, hidden, n_ctx
    )
    inverse_two = inverse_two[:, :1]

    def fold_sequence(keep, send):
        got = swap(send, "tp", 1)
        totals = []
        for block in reversed(range(n_ctx)):
            here = slice(block * rows, (block + 1) * rows)
            far = (keep[1, here].astype(F32) + got[1, here].astype(F32)).astype(BF16)
            near = keep[0, here].astype(F32) + got[0, here].astype(F32)
            totals.append(near + swap(far, "tp", 2).astype(F32))
        return sum_ctx(totals[::-1])

    second_grad = fold_sequence(keep, send)
    scaled_two = second_grad * gain_two
    grad_gain_two = jnp.sum(second_grad * middle, axis=0)
    inner_two = lax.psum(jnp.sum(scaled_two * middle, axis=1), "tp") / full_width
    middle_grad = upstream + scaled_two - middle * (inverse_two * inverse_two * inner_two[:, None])
    branch = spread_tp((RESID * middle_grad).astype(BF16))

    result = middle + RESID * fold_sequence(
        *feed_forward_result(where, active, weights, hidden, n_ctx)
    )
    grads = functools.partial(
        feed_forward_grads, where, tokens, branches, pairs_grad, active, hidden, columns, shards, n_ctx
    )
    if paired:
        sent, kept = grads(1), grads(0)
        moved = [swap(sent[k], "fsdp", 1) for k in reversed(range(n_ctx))][::-1]
        sums = [
            (kept[k].astype(F32) + moved[k].astype(F32)).astype(BF16) for k in range(n_ctx)
        ]
    else:
        total = grads(None)[0].reshape(n_fsdp, n_ctx, full_width // shards, columns)
        total = lax.psum_scatter(total, "fsdp", scatter_dimension=0, tiled=False)
        sums = [
            lax.dynamic_index_in_dim(total, ctx_index ^ k, 0, keepdims=False) for k in range(n_ctx)
        ]
    sent = {k: sums[k] for k in range(1, n_ctx)}
    _, got = in_turn(sent, ((3, 1), (2,)), lambda key, value: swap(value, "ctx", key))
    hidden_sums = [sums[0]] + [got[k] for k in range(1, n_ctx)]

    out_parts = output_grads(where, attended, branch, shards, n_ctx, paired)
    query_grad, pair_grad, query_sum, kv_keep, kv_1, kv_2, kv_3 = attention_backward(
        where,
        queries_low,
        pairs_low,
        lse,
        payloads,
        ups,
        branch,
        tables,
        n_ctx,
        waits=out_parts[:1],
    )
    kv_total = sum_ctx([kv_keep, kv_1, kv_2, kv_3])
    both = jnp.concatenate([query_sum, kv_total], axis=1).reshape(2, rows // 2, LAT_COLS)
    mine, other = fold_halves(
        lax.dynamic_index_in_dim(both, tp_index % 2, 0, keepdims=False),
        lax.dynamic_index_in_dim(both, 1 - tp_index % 2, 0, keepdims=False),
    )
    up_parts = up_grads(
        where, query_low, query_grad, payloads, pair_grad, shards, n_ctx, paired
    )
    if paired:
        out_sums = fold_shards(out_parts)
        up_sums = fold_shards(up_parts)
    input_grad, grad_query_gain, grad_latent_gain, grad_gain_one, *down_parts = input_backward(
        where,
        mine,
        other,
        latent,
        gain_query,
        gain_latent,
        tables,
        normed_low,
        joined,
        activations,
        inverse_one[:, None],
        gain_one[None, :],
        middle_grad,
        pick,
        q_shard,
        low_rows,
        shards,
        n_ctx,
        paired,
    )
    grad_gate, grad_up, grad_down = join_hidden(where, hidden_sums, hidden)
    if paired:
        grad_out = sum_ctx(out_sums)
        grad_ups = sum_ctx(up_sums)
        grad_query_up = grad_ups[: query_up.shape[0]]
        grad_latent_up = grad_ups[query_up.shape[0] :]
        grad_downs = sum_ctx(fold_shards(down_parts))
        grad_query_down = grad_downs[:q_shard]
        grad_latent_down = grad_downs[q_shard : q_shard + low_shard]
    else:
        grad_out = scatter_rows(out_parts[0])
        grad_query_up, grad_latent_up = scatter_rows(up_parts[0]), scatter_rows(up_parts[1])
        grad_query_down = scatter_rows(down_parts[0][:QRANK])
        grad_latent_down = scatter_rows(down_parts[0][QRANK : LATENT + ROPE])
    grad_query_up = grad_query_up.reshape(query_up.shape[0], local_heads, LANES)
    grad_query_up = grad_query_up[:, :, : NOPE + ROPE].reshape(query_up.shape)

    gain_sums = lax.psum(jnp.concatenate([grad_gain_one[0], grad_gain_two]), both_axes)
    if paired:
        gain_row = grad_downs[q_shard + low_shard]
        gain_query_sum = gain_row[:q_shard]
        gain_latent_sum = gain_row[q_shard : q_shard + latent_gain.shape[0]]
    else:
        gain_query_sum = scatter_rows(grad_query_gain[0])
        gain_latent_sum = scatter_rows(grad_latent_gain[0])
    return (
        result.astype(BF16),
        input_grad,
        gain_sums[:width],
        grad_query_down.T,
        grad_latent_down.T,
        gain_query_sum,
        gain_latent_sum,
        grad_query_up,
        grad_latent_up,
        grad_out.T,
        gain_sums[width : 2 * width],
        grad_gate,
        grad_up,
        grad_down.T,
    )


def solution(mesh):
    tokens = P(("fsdp", "ctx"), "tp")
    by_columns = P("tp", ("fsdp", "ctx"))
    by_rows = P(("fsdp", "ctx"), "tp")
    latent_vector = P(("fsdp", "ctx"))
    feature_vector = P("tp")
    weights = (
        feature_vector,
        by_columns,
        by_columns,
        latent_vector,
        latent_vector,
        by_rows,
        by_rows,
        by_columns,
        feature_vector,
        by_rows,
        by_rows,
        by_columns,
    )
    return jax.shard_map(
        per_device,
        mesh=mesh,
        in_specs=(tokens,) + weights + (tokens,),
        out_specs=(tokens, tokens) + weights,
        check_vma=False,
    )
```
